128 devices in a mesh: dp: 32 (over y, z, core), mp: 4 (over x).
Axes of the slice: x: 4, y: 4, z: 4, core: 2. Of those that a mesh axis runs over, the one named last changes fastest.
Arguments:
- layer_input: bfloat16 [262144, 384], P(('dp', 'mp')), may hold values from -6 to 6
- segments: int32 [32, 8192], P('dp'), may hold values from -1 to 121, as said below
- cotangent: bfloat16 [262144, 384], P(('dp', 'mp')), may hold values from -6 to 6
- first_gain: float32 [384], replicated, may hold values from 0.5 to 1.5
- first_shift: float32 [384], replicated, may hold values from -3 to 3
- inward_weight: bfloat16 [384, 1152], replicated, may hold values from -0.3125 to 0.3125
- inward_bias: float32 [2, 384], replicated, may hold values from -3 to 3
- outward_weight: bfloat16 [384, 384], replicated, may hold values from -1.75 to 1.75
- outward_bias: float32 [384], replicated, may hold values from -3 to 3
- second_gain: float32 [384], replicated, may hold values from 0.5 to 1.5
- second_shift: float32 [384], replicated, may hold values from -3 to 3
- expand_weight: bfloat16 [384, 1536], replicated, may hold values from -0.3125 to 0.3125
- expand_bias: float32 [1536], replicated, may hold values from -3 to 3
- shrink_weight: bfloat16 [1536, 384], replicated, may hold values from -0.15625 to 0.15625
- shrink_bias: float32 [384], replicated, may hold values from -3 to 3
Outputs:
- result: bfloat16 [262144, 384], P(('dp', 'mp'))
- input_gradient: float32 [262144, 384], P(('dp', 'mp'))
- first_gain_gradient: float32 [384], replicated
- first_shift_gradient: float32 [384], replicated
- inward_weight_gradient: float32 [384, 1152], replicated
- inward_bias_gradient: float32 [2, 384], replicated
- outward_weight_gradient: float32 [384, 384], replicated
- outward_bias_gradient: float32 [384], replicated
- second_gain_gradient: float32 [384], replicated
- second_shift_gradient: float32 [384], replicated
- expand_weight_gradient: float32 [384, 1536], replicated
- expand_bias_gradient: float32 [1536], replicated
- shrink_weight_gradient: float32 [1536, 384], replicated
- shrink_bias_gradient: float32 [384], replicated
The draws below stay inside these ranges and needn't reach their ends.
Inputs may be any that keep to these rules, and one draw needn't show every extreme that they name: `segments`: per pack, image numbers count up from 0 in consecutive runs; each image fills 198 // 3 slots or more and 198 at most, the first image of every pack exactly 198; padding (-1) follows the last image, fills 1 to 198 slots and includes the pack's last slot.
All inputs are finite; a program needn't handle non-finite values.
Results may differ from the reference program's by a relative error of at most 0.02.
Values may be sent and summed in bfloat16 or wider, within the bound.
No kernel may reach another device: no remote copies, remote signals or barrier semaphores. Data moves between devices by JAX's collectives and lax.ppermute only.
A program may use at most 192 MiB of HBM per device.

```python
import jax
import jax.numpy as jnp
from jax import lax

D = 384
HD = 64
FF = 1536
SLOTS = 8192
SEQ = 198
TOKENS = 262144
N_DP = 32


def draw_segments(key, part):
    chooser = jax.random.fold_in(key, 12)
    key = jax.random.fold_in(key, 11)
    shortest = SEQ // 3
    images = SLOTS // shortest + 1
    lengths = jax.random.randint(key, (N_DP, images), shortest, SEQ + 1)
    densest = jax.random.randint(chooser, (), 0, N_DP)
    pack_ids = jnp.arange(N_DP, dtype=jnp.int32)[:, None]
    lengths = jnp.where(pack_ids == densest, shortest, lengths)
    lengths = lengths.at[:, 0].set(SEQ)
    ends = jnp.cumsum(lengths, axis=1)
    places = jnp.arange(SLOTS, dtype=jnp.int32)
    number = jnp.sum((ends[:, None, :] <= places[None, :, None]).astype(jnp.int32), axis=2)
    chosen_end = jnp.take_along_axis(ends, jnp.minimum(number, images - 1), axis=1)
    complete = chosen_end <= SLOTS - 1
    return jnp.where(complete, number, -1).astype(jnp.int32)


def steps_of(rng, shape, shards, smallest, high):
    level = 1.0
    for dim, blocks in shards:
        draws = jax.random.uniform(jax.random.fold_in(jax.random.fold_in(rng, 6), dim), (blocks,), jnp.float32, smallest / len(shards), high / len(shards))
        level = level * jnp.repeat(jnp.exp(draws), shape[dim] // blocks).reshape((-1,) + (1,) * (len(shape) - 1 - dim))
    return level


def normal_values(key, extent, scale, limit, split=(), held_as=jnp.bfloat16):
    factor_of = steps_of(key, extent, split, -0.22, 0.18) if split else 1.0
    values = jax.random.normal(key, extent, jnp.float32) * scale * factor_of
    return jnp.minimum(jnp.maximum(values, -limit), limit).astype(held_as)


def setup_inputs(seed: int = 0) -> dict:
    keys = jax.random.split(jax.random.key(seed), 16)
    layer_input = normal_values(keys[0], (TOKENS, D), 1.0, 6.0, ((0, 128),))
    segments = draw_segments(jax.random.fold_in(keys[15], 71), 0)
    cotangent = normal_values(keys[2], (TOKENS, D), 1.0, 6.0, ((0, 128),))
    first_gain = jnp.clip(1.0 + 0.1 * jax.random.normal(keys[3], (D,), jnp.float32), 0.5, 1.5)
    first_shift = normal_values(keys[4], (D,), 0.5, 3.0, (), jnp.float32)
    inward_weight = normal_values(keys[5], (D, 3 * D), D ** -0.5, 0.3125)
    inward_bias = normal_values(keys[6], (2, D), 0.5, 3.0, (), jnp.float32)
    outward_weight = normal_values(keys[7], (D, D), (D // 32) ** -0.5, 1.75)
    outward_bias = normal_values(keys[8], (D,), 0.5, 3.0, (), jnp.float32)
    second_gain = jnp.clip(1.0 + 0.1 * jax.random.normal(keys[9], (D,), jnp.float32), 0.5, 1.5)
    second_shift = normal_values(keys[10], (D,), 0.5, 3.0, (), jnp.float32)
    expand_weight = normal_values(keys[11], (D, FF), D ** -0.5, 0.3125)
    expand_bias = normal_values(keys[12], (FF,), 0.5, 3.0, (), jnp.float32)
    shrink_weight = normal_values(keys[13], (FF, D), FF ** -0.5, 0.15625)
    shrink_bias = normal_values(keys[14], (D,), 0.5, 3.0, (), jnp.float32)
    return dict(layer_input=layer_input, segments=segments, cotangent=cotangent, first_gain=first_gain, first_shift=first_shift, inward_weight=inward_weight, inward_bias=inward_bias, outward_weight=outward_weight, outward_bias=outward_bias, second_gain=second_gain, second_shift=second_shift, expand_weight=expand_weight, expand_bias=expand_bias, shrink_weight=shrink_weight, shrink_bias=shrink_bias)


EPSILON = 1e-06
HIGHEST = lax.Precision.HIGHEST

@jax.custom_vjp
def low(v):
    return lax.optimization_barrier(v.astype(jnp.bfloat16)).astype(jnp.float32)

@jax.custom_vjp
def low_back(v):
    return v

def low_keep(v):
    return (low(v), None)

def low_pass(kept, grad):
    return (grad,)

def back_keep(v):
    return (v, None)

def back_low(kept, grad):
    return (low(grad),)
low.defvjp(low_keep, low_pass)
low_back.defvjp(back_keep, back_low)

def normalize(rows, gain, shift):
    center = lax.optimization_barrier(jnp.mean(rows, axis=-1, keepdims=True))
    centred = rows - center
    spread = lax.optimization_barrier(jnp.mean(centred * centred, axis=-1, keepdims=True))
    return centred * lax.rsqrt(spread + EPSILON) * gain + shift

def pack_forward(rows, seg_row, first_gain, first_shift, inward_weight, inward_bias, outward_weight, outward_bias, second_gain, second_shift, expand_weight, expand_bias, shrink_weight, shrink_bias):
    count = rows.shape[0]
    width = rows.shape[1]
    heads = width // HD
    reach = SEQ - 1
    tile = min(512, count)
    tiles = count // tile
    valid = (seg_row >= 0).astype(jnp.float32)[:, None]
    normed1 = low(normalize(rows, first_gain, first_shift))
    triple = jnp.dot(normed1, inward_weight, precision=HIGHEST)
    blank = jnp.zeros((width,), jnp.float32)
    triple = triple + jnp.concatenate([inward_bias[0], blank, inward_bias[1]])
    triple = low_back(low(triple))
    queries = triple[:, :width].reshape(tiles, tile, heads, HD)
    padded_kv = jnp.pad(triple[:, width:], ((reach, reach), (0, 0)))
    padded_seg = jnp.pad(seg_row, (reach, reach), constant_values=-2)

    def one_tile(items):
        query_tile, seg_tile, index = items
        begin = index * tile
        window = lax.dynamic_slice_in_dim(padded_kv, begin, tile + 2 * reach, 0)
        seg_window = lax.dynamic_slice_in_dim(padded_seg, begin, tile + 2 * reach, 0)
        key_tile = window[:, :width].reshape(-1, heads, HD)
        value_tile = window[:, width:].reshape(-1, heads, HD)
        raw = jnp.einsum('qhd,khd->hqk', query_tile, key_tile, precision=HIGHEST) * HD ** (-0.5)
        allowed = seg_tile[:, None] == seg_window[None, :]
        scores = low_back(jnp.where(allowed[None], raw, -1000000000.0))
        probs = low(jax.nn.softmax(scores, axis=-1))
        return jnp.einsum('hqk,khd->qhd', probs, value_tile, precision=HIGHEST)
    attended = lax.map(jax.checkpoint(one_tile), (queries, seg_row.reshape(tiles, tile), jnp.arange(tiles, dtype=jnp.int32)))
    attended = low_back(low(attended.reshape(count, width)))
    middle = rows + low_back(jnp.dot(attended, outward_weight, precision=HIGHEST)) + outward_bias
    normed2 = low(normalize(middle, second_gain, second_shift))
    before = low_back(jnp.dot(normed2, expand_weight, precision=HIGHEST) + expand_bias)
    hidden = low(jax.nn.gelu(before, approximate=False))
    branch = low_back(jnp.dot(hidden, shrink_weight, precision=HIGHEST))
    return (middle + branch + shrink_bias) * valid

def reference(layer_input, segments, cotangent, first_gain, first_shift, inward_weight, inward_bias, outward_weight, outward_bias, second_gain, second_shift, expand_weight, expand_bias, shrink_weight, shrink_bias):
    params = tuple((item.astype(jnp.float32) for item in (first_gain, first_shift, inward_weight, inward_bias, outward_weight, outward_bias, second_gain, second_shift, expand_weight, expand_bias, shrink_weight, shrink_bias)))
    rows_all = layer_input.astype(jnp.float32).reshape(N_DP, SLOTS, D)
    back_all = cotangent.astype(jnp.float32).reshape(N_DP, SLOTS, D)

    def one_pack(totals, items):
        rows, seg_row, back = items

        def closed(row_values, *weights):
            return pack_forward(row_values, seg_row, *weights)
        output, pullback = jax.vjp(closed, rows, *params)
        grads = pullback(back)
        totals = tuple((left + right for left, right in zip(totals, grads[1:])))
        return (totals, (output.astype(jnp.bfloat16), grads[0]))
    start = tuple((jnp.zeros_like(item) for item in params))
    sums, (outputs, input_grads) = lax.scan(one_pack, start, (rows_all, segments, back_all))
    return (outputs.reshape(N_DP * SLOTS, D), input_grads.reshape(N_DP * SLOTS, D), sums[0], sums[1], sums[2], sums[3], sums[4], sums[5], sums[6], sums[7], sums[8], sums[9], sums[10], sums[11])
```

```python
from functools import partial

import jax
import jax.numpy as jnp
from jax import lax
from jax.experimental import pallas as pl
from jax.experimental.pallas import tpu as pltpu
from jax.sharding import PartitionSpec as P

HD = 64
SEQ = 198
EPSILON = 1e-06
MASKED = -1000000000.0
WIN = 256
TILE = 256
HALO = 208
GROUPS = 24
LANES = 128
BIG = 1 << 20
F32 = jnp.float32
BF16 = jnp.bfloat16
NT = (((1,), (1,)), ((), ()))
TN = (((0,), (0,)), ((), ()))


def dot(a, b):
    return jnp.dot(a, b, preferred_element_type=F32)


def dot_nt(a, b):
    return lax.dot_general(a, b, NT, preferred_element_type=F32)


def dot_tn(a, b):
    return lax.dot_general(a, b, TN, preferred_element_type=F32)


def normalize(rows):
    center = jnp.mean(rows, axis=-1, keepdims=True)
    centred = rows - center
    spread = jnp.mean(centred * centred, axis=-1, keepdims=True)
    inverse = lax.rsqrt(spread + EPSILON)
    return centred * inverse, inverse


def normalize_back(upstream, scaled, inverse, gain):
    direct = upstream * gain
    first = jnp.mean(direct, axis=-1, keepdims=True)
    second = jnp.mean(direct * scaled, axis=-1, keepdims=True)
    return inverse * (direct - first - scaled * second)


def gelu_parts(v):
    size = jnp.abs(v)
    den = 1.0 + (0.3275911 * 0.7071067811865476) * size
    t = pl.reciprocal(den, approx=True)
    t = t * (2.0 - den * t)
    bell = jnp.exp(-0.5 * (v * v))
    poly = t * (
        0.5 * 0.254829592
        + t * (-0.5 * 0.284496736 + t * (0.5 * 1.421413741 + t * (-0.5 * 1.453152027 + t * (0.5 * 1.061405429))))
    )
    tail = poly * bell
    cdf = jnp.where(v >= 0.0, 1.0 - tail, tail)
    return v * cdf, cdf + v * (0.3989422804014327 * bell)


def find_next(seg_ref, start, ident, steps, low, high):
    def step(_, pair):
        lo, hi = pair
        mid = (lo + hi) // 2
        value = seg_ref[0, jnp.minimum(mid, seg_ref.shape[1] - 1)]
        above = jnp.logical_or(jnp.logical_or(value < 0, value > ident), mid >= seg_ref.shape[1])
        return jnp.where(above, lo, mid + 1), jnp.where(above, mid, hi)

    return lax.fori_loop(0, steps, step, (low, high))[0]


def plan_groups(seg_ref, position, last, rows, table):
    slots = seg_ref.shape[1]
    base = position * rows
    before_id = seg_ref[0, jnp.maximum(base - 1, 0)]
    first = find_next(seg_ref, base, before_id, 8, base, base + SEQ)
    first = jnp.where(position == 0, 0, first)
    end_id = seg_ref[0, base + rows - 1]
    last_end = find_next(seg_ref, base, end_id, 8, base + rows, jnp.minimum(base + rows + SEQ, slots))
    pad_start = find_next(seg_ref, base, BIG, 8, slots - SEQ, slots)
    end = jnp.where(last, pad_start, last_end) - base
    first = first - base

    def body(state):
        at, group, window, start, c1, c2 = state
        ident = seg_ref[0, base + at]
        after = find_next(seg_ref, base, ident, 8, base + at + SEQ // 3, base + at + SEQ + 1) - base
        after = jnp.minimum(after, end)
        fits = after - window <= WIN

        @pl.when(jnp.logical_not(fits))
        def _():
            write_group(table, group, window, start, c1, c2, at)

        group = jnp.where(fits, group, group + 1)
        new_c1 = jnp.where(fits, jnp.where(at == start, c1, jnp.where(c1 < 0, at, c1)), -1)
        new_c2 = jnp.where(fits, jnp.where(jnp.logical_and(at != start, c1 >= 0), jnp.where(c2 < 0, at, c2), c2), -1)
        start = jnp.where(fits, start, at)
        window = jnp.where(fits, window, (at // 16) * 16)
        return after, group, window, start, new_c1, new_c2

    init = (first, jnp.int32(0), (first // 16) * 16, first, jnp.int32(-1), jnp.int32(-1))
    at, group, window, start, c1, c2 = lax.while_loop(lambda s: s[0] < end, body, init)
    write_group(table, group, window, start, c1, c2, at)
    table[GROUPS, 0] = group + 1
    table[GROUPS, 1] = first
    table[GROUPS, 2] = end
    return group + 1, first, end


def write_group(table, group, window, start, c1, c2, end):
    table[group, 0] = window
    table[group, 1] = start - window
    table[group, 2] = jnp.where(c1 < 0, end, c1) - window
    table[group, 3] = jnp.where(c2 < 0, end, c2) - window
    table[group, 4] = end - window


def group_bias(table, group):
    bounds = [table[group, i] for i in range(1, 5)]
    row = lax.broadcasted_iota(jnp.int32, (WIN, WIN), 0)
    col = lax.broadcasted_iota(jnp.int32, (WIN, WIN), 1)

    def ident(index):
        return sum((index >= b).astype(jnp.int32) for b in bounds)

    return jnp.where(ident(row) == ident(col), 0.0, MASKED)


def head_masks():
    lane = lax.broadcasted_iota(jnp.int32, (WIN, 2 * HD), 1)
    return lane < HD, lane >= HD


def keep_first(ref, window, begin, cols, value):
    head = pl.ds(window, 16)
    old = ref[head, cols]
    row = lax.broadcasted_iota(jnp.int32, (16, 2 * HD), 0)
    ref[head, cols] = jnp.where(row >= begin, value[:16].astype(F32), old.astype(F32)).astype(BF16)
    ref[pl.ds(window + 16, WIN - 16), cols] = value[16:].astype(BF16)


def attend_group(group, table, triple, attended, stats):
    width = attended.shape[1]
    window = pl.multiple_of(table[group, 0], 16)
    rows = pl.ds(window, WIN)
    begin = table[group, 1]
    bias = group_bias(table, group)
    masks = head_masks()
    for pair in range(width // (2 * HD)):
        cols = pl.ds(pair * 2 * HD, 2 * HD)
        query = triple[rows, pl.ds(pair * 2 * HD, 2 * HD)]
        key = triple[rows, pl.ds(width + pair * 2 * HD, 2 * HD)]
        value = triple[rows, pl.ds(2 * width + pair * 2 * HD, 2 * HD)]
        value_t = value.T
        outs = []
        for h in range(2):
            masked = jnp.where(masks[h], query, jnp.zeros_like(query))
            scores = dot_nt(key, masked) + bias
            highest = jnp.max(scores, axis=0, keepdims=True)
            raised = jnp.exp(scores - highest)
            total = jnp.sum(raised, axis=0, keepdims=True)
            out = dot(value_t[h * HD : (h + 1) * HD], raised.astype(BF16))
            outs.append(out * (1.0 / total))
            stats[group, pl.ds(2 * pair + h, 1), :] = highest + jnp.log(total)
        keep_first(attended, window, begin, cols, jnp.concatenate(outs, axis=0).T)


def attend_back_group(group, table, triple, attended, upstream, stats, triple_grad):
    width = attended.shape[1]
    window = pl.multiple_of(table[group, 0], 16)
    rows = pl.ds(window, WIN)
    begin = table[group, 1]
    bias = group_bias(table, group)
    masks = head_masks()
    for pair in range(width // (2 * HD)):
        cols = pl.ds(pair * 2 * HD, 2 * HD)
        query = triple[rows, pl.ds(pair * 2 * HD, 2 * HD)]
        key = triple[rows, pl.ds(width + pair * 2 * HD, 2 * HD)]
        value = triple[rows, pl.ds(2 * width + pair * 2 * HD, 2 * HD)]
        out_t = attended[rows, cols].T.astype(F32)
        up = upstream[rows, cols]
        up_t = up.T
        product = out_t * up_t.astype(F32)
        key_t = key.T
        query_grads = []
        key_grad = jnp.zeros((WIN, 2 * HD), F32)
        value_grad = jnp.zeros((WIN, 2 * HD), F32)
        for h in range(2):
            masked = jnp.where(masks[h], query, jnp.zeros_like(query))
            lse = stats[group, pl.ds(2 * pair + h, 1), :]
            probs = jnp.exp(dot_nt(key, masked) + bias - lse)
            up_masked = jnp.where(masks[h], up, jnp.zeros_like(up))
            probs_grad = dot_nt(value, up_masked)
            agreement = jnp.sum(product[h * HD : (h + 1) * HD], axis=0, keepdims=True)
            scores_grad = (probs * (probs_grad - agreement)).astype(BF16)
            value_grad = value_grad + dot(probs.astype(BF16), up_masked)
            key_grad = key_grad + dot(scores_grad, masked)
            query_grads.append(dot(key_t[h * HD : (h + 1) * HD], scores_grad) * HD ** (-0.5))
        keep_first(triple_grad, window, begin, cols, jnp.concatenate(query_grads, axis=0).T)
        keep_first(triple_grad, window, begin, pl.ds(width + pair * 2 * HD, 2 * HD), key_grad)
        keep_first(triple_grad, window, begin, pl.ds(2 * width + pair * 2 * HD, 2 * HD), value_grad)


def interval(tile, first, end):
    row = lax.broadcasted_iota(jnp.int32, (TILE, 1), 0) + tile * TILE
    return jnp.logical_and(row >= first, row < end)


def kernel_one(
    place, seg, x_ref, x_halo, cot_ref, cot_halo, gain1, shift1, w_in, b_in, w_out, b_out, gain2, shift2,
    w_ex, b_ex, w_sh, b_sh,
    result, result_halo, triple, attended, upstream, middle_grad, stats, table, mine, other,
    d_ex, d_sh, d_out, small,
):
    rows, width = x_ref.shape
    tiles = triple.shape[0] // TILE
    groups, first, end = plan_groups(seg, place[0], place[1] == 1, rows, table)
    attended[...] = jnp.zeros_like(attended)
    d_ex[...] = jnp.zeros_like(d_ex)
    d_sh[...] = jnp.zeros_like(d_sh)
    d_out[...] = jnp.zeros_like(d_out)
    small[...] = jnp.zeros_like(small)

    def load(ref, halo, tile):
        spot = pl.ds(pl.multiple_of(jnp.minimum(tile, tiles - 2) * TILE, TILE), TILE)
        return jnp.where(tile == tiles - 1, halo[...].astype(F32), ref[spot, :].astype(F32))

    def project(tile, _):
        scaled, _inverse = normalize(load(x_ref, x_halo, tile))
        normed = (scaled * gain1[...] + shift1[...]).astype(BF16)
        spot = pl.ds(pl.multiple_of(tile * TILE, TILE), TILE)
        q = dot(normed, w_in[:, :width]) + b_in[0:1, :]
        triple[spot, :width] = (q.astype(BF16).astype(F32) * HD ** (-0.5)).astype(BF16)
        triple[spot, width : 2 * width] = dot(normed, w_in[:, width : 2 * width]).astype(BF16)
        triple[spot, 2 * width :] = (dot(normed, w_in[:, 2 * width :]) + b_in[1:2, :]).astype(BF16)
        return 0

    lax.fori_loop(0, tiles, project, 0)

    def attend(group, _):
        attend_group(group, table, triple, attended, stats)
        return 0

    lax.fori_loop(0, groups, attend, 0)

    hidden_width = w_ex.shape[1]
    chunk = 512

    def feed(tile, _):
        spot = pl.ds(pl.multiple_of(tile * TILE, TILE), TILE)
        keep = interval(tile, first, end)
        att = attended[spot, :]
        middle = load(x_ref, x_halo, tile) + dot(att, w_out[...]) + b_out[...]
        scaled, inverse = normalize(middle)
        normed = (scaled * gain2[...] + shift2[...]).astype(BF16)
        back = jnp.where(keep, load(cot_ref, cot_halo, tile), 0.0)
        back_low = back.astype(BF16)
        branch = jnp.zeros((TILE, width), F32)
        normed_grad = jnp.zeros((TILE, width), F32)
        for begin in range(0, hidden_width, chunk):
            cols = slice(begin, begin + chunk)
            before = dot(normed, w_ex[:, cols]) + b_ex[:, cols]
            value, slope = gelu_parts(before)
            hidden = value.astype(BF16)
            branch = branch + dot(hidden, w_sh[cols, :])
            before_grad = (dot_nt(back_low, w_sh[cols, :]) * slope)
            before_low = before_grad.astype(BF16)
            normed_grad = normed_grad + dot_nt(before_low, w_ex[:, cols])
            d_sh[:, cols] += dot_tn(back_low, hidden)
            d_ex[:, cols] += dot_tn(normed, before_low)
            small[8:9, cols] += jnp.sum(before_low.astype(F32), axis=0, keepdims=True)
        out = jnp.where(keep, middle + branch + b_sh[...], 0.0).astype(BF16)

        @pl.when(tile < tiles - 1)
        def _():
            result[pl.ds(pl.multiple_of(jnp.minimum(tile, tiles - 2) * TILE, TILE), TILE), :] = out

        @pl.when(tile == tiles - 1)
        def _():
            result_halo[...] = out

        small[0:1, :width] += jnp.sum(back, axis=0, keepdims=True)
        small[1:2, :width] += jnp.sum(normed_grad * scaled, axis=0, keepdims=True)
        small[2:3, :width] += jnp.sum(normed_grad, axis=0, keepdims=True)
        grad = back + normalize_back(normed_grad, scaled, inverse, gain2[...])
        small[3:4, :width] += jnp.sum(grad, axis=0, keepdims=True)
        middle_grad[spot, :] = grad
        grad_low = grad.astype(BF16)
        d_out[...] += dot_tn(att, grad_low)
        upstream[spot, :] = dot_nt(grad_low, w_out[...]).astype(BF16)
        return 0

    lax.fori_loop(0, tiles, feed, 0)
    pack((d_ex, d_sh, d_out), small, place[2], mine, other)


def pack(grads, small, core, mine, other):
    half = grads[0].shape[0] // 2
    at = 0
    for grad in grads:
        for begin in range(0, grad.shape[1], LANES):
            cols = slice(begin, begin + LANES)
            mine[pl.ds(at, half), :] = grad[pl.ds(pl.multiple_of(core * half, half), half), cols].astype(BF16)
            other[pl.ds(at, half), :] = grad[pl.ds(pl.multiple_of((1 - core) * half, half), half), cols].astype(BF16)
            at += half
    rest = mine.shape[0] - at
    mine[pl.ds(at, rest), :] = jnp.zeros((rest, LANES), BF16)
    other[pl.ds(at, rest), :] = jnp.zeros((rest, LANES), BF16)
    count = small.shape[1] // LANES
    for index in range(count):
        cols = slice(index * LANES, (index + 1) * LANES)
        spot = pl.ds(at + (index // 2) * 16, 16)

        @pl.when(core == index % 2)
        def _():
            mine[spot, :] = small[:, cols].astype(BF16)

        @pl.when(core != index % 2)
        def _():
            other[spot, :] = small[:, cols].astype(BF16)


def kernel_two(
    place, table, x_ref, x_halo, gain1, shift1, w_in, triple, attended, upstream, middle_grad, stats,
    input_grad, input_halo, mine, other, triple_grad, d_in, small,
):
    rows, width = x_ref.shape
    tiles = triple.shape[0] // TILE
    triple_grad[...] = jnp.zeros_like(triple_grad)
    d_in[...] = jnp.zeros_like(d_in)
    small[...] = jnp.zeros_like(small)

    def attend(group, _):
        attend_back_group(group, table, triple, attended, upstream, stats, triple_grad)
        return 0

    lax.fori_loop(0, table[GROUPS, 0], attend, 0)

    def load(ref, halo, tile):
        spot = pl.ds(pl.multiple_of(jnp.minimum(tile, tiles - 2) * TILE, TILE), TILE)
        return jnp.where(tile == tiles - 1, halo[...].astype(F32), ref[spot, :].astype(F32))

    def project(tile, _):
        spot = pl.ds(pl.multiple_of(tile * TILE, TILE), TILE)
        scaled, inverse = normalize(load(x_ref, x_halo, tile))
        normed = (scaled * gain1[...] + shift1[...]).astype(BF16)
        grad = triple_grad[spot, :]
        d_in[...] += dot_tn(normed, grad)
        small[4:5, : 3 * width] += jnp.sum(grad.astype(F32), axis=0, keepdims=True)
        normed_grad = dot_nt(grad, w_in[...])
        small[5:6, :width] += jnp.sum(normed_grad * scaled, axis=0, keepdims=True)
        small[6:7, :width] += jnp.sum(normed_grad, axis=0, keepdims=True)
        out = middle_grad[spot, :] + normalize_back(normed_grad, scaled, inverse, gain1[...])

        @pl.when(tile < tiles - 1)
        def _():
            input_grad[pl.ds(pl.multiple_of(jnp.minimum(tile, tiles - 2) * TILE, TILE), TILE), :] = out

        @pl.when(tile == tiles - 1)
        def _():
            input_halo[...] = out

        return 0

    lax.fori_loop(0, tiles, project, 0)
    pack((d_in,), small, place[2], mine, other)


VMEM = pl.BlockSpec(memory_space=pltpu.VMEM)
SMEM = pl.BlockSpec(memory_space=pltpu.SMEM)


def packed_rows(columns, small, pieces):
    half = columns // LANES * 192 + (small // LANES + 1) // 2 * 16
    return pieces * (-(-half // (8 * pieces)) * 8)


def forward_one(place, segments, x, x_halo, cot, cot_halo, weights, pieces):
    rows, width = x.shape
    total = rows + TILE
    hidden = weights[8].shape[1]
    packed = packed_rows(2 * hidden + width, hidden, pieces)
    shapes = (
        jax.ShapeDtypeStruct((rows, width), BF16),
        jax.ShapeDtypeStruct((TILE, width), BF16),
        jax.ShapeDtypeStruct((total, 3 * width), BF16),
        jax.ShapeDtypeStruct((total, width), BF16),
        jax.ShapeDtypeStruct((total, width), BF16),
        jax.ShapeDtypeStruct((total, width), F32),
        jax.ShapeDtypeStruct((GROUPS, 8, WIN), F32),
        jax.ShapeDtypeStruct((GROUPS + 1, 8), jnp.int32),
        jax.ShapeDtypeStruct((packed, LANES), BF16),
        jax.ShapeDtypeStruct((packed, LANES), BF16),
    )
    return pl.pallas_call(
        kernel_one,
        out_shape=shapes,
        in_specs=[SMEM, SMEM] + [VMEM] * 16,
        out_specs=tuple([VMEM] * 7 + [SMEM] + [VMEM] * 2),
        scratch_shapes=[
            pltpu.VMEM((width, hidden), F32),
            pltpu.VMEM((width, hidden), F32),
            pltpu.VMEM((width, width), F32),
            pltpu.VMEM((16, hidden), F32),
        ],
        compiler_params=pltpu.CompilerParams(vmem_limit_bytes=60 * 1024 * 1024),
        name="forward_one",
    )(place, segments, x, x_halo, cot, cot_halo, *weights)


def backward_two(place, table, x, x_halo, gain1, shift1, w_in, kept, pieces):
    rows, width = x.shape
    total = rows + TILE
    packed = packed_rows(3 * width, 3 * width, pieces)
    shapes = (
        jax.ShapeDtypeStruct((rows, width), F32),
        jax.ShapeDtypeStruct((TILE, width), F32),
        jax.ShapeDtypeStruct((packed, LANES), BF16),
        jax.ShapeDtypeStruct((packed, LANES), BF16),
    )
    return pl.pallas_call(
        kernel_two,
        out_shape=shapes,
        in_specs=[SMEM] * 2 + [VMEM] * 10,
        out_specs=tuple([VMEM] * 4),
        scratch_shapes=[
            pltpu.VMEM((total, 3 * width), BF16),
            pltpu.VMEM((width, 3 * width), F32),
            pltpu.VMEM((16, 3 * width), F32),
        ],
        compiler_params=pltpu.CompilerParams(vmem_limit_bytes=60 * 1024 * 1024),
        name="backward_two",
    )(place, table, x, x_halo, gain1, shift1, w_in, *kept)


def same_core_groups():
    packs, parts = lax.axis_size("dp"), lax.axis_size("mp")
    return [[d * parts + m for d in range(c, packs, 2) for m in range(parts)] for c in range(2)]


def swap_cores(block):
    packs = lax.axis_size("dp")
    return lax.ppermute(block, "dp", [(i, i ^ 1) for i in range(packs)])


def scatter_sum(mine, other, pieces):
    both = (mine.astype(F32) + swap_cores(other).astype(F32)).astype(BF16)
    parts = lax.all_to_all(both.reshape(pieces, -1, LANES), ("dp", "mp"), 0, 0, axis_index_groups=same_core_groups())
    return jnp.sum(parts.astype(F32), axis=0).astype(BF16)


def gather_sum(piece, core, pieces):
    sent = jnp.broadcast_to(piece[None], (pieces,) + piece.shape)
    mine = lax.all_to_all(sent, ("dp", "mp"), 0, 0, axis_index_groups=same_core_groups()).reshape(-1, LANES)
    other = swap_cores(mine)
    return jnp.where(core == 0, mine, other), jnp.where(core == 0, other, mine)


def unpack(halves, at, columns):
    low, high = halves
    count = columns // LANES
    blocks = [h[at : at + count * 192].reshape(count, 192, LANES).transpose(1, 0, 2) for h in (low, high)]
    return jnp.concatenate(blocks, axis=0).reshape(384, columns).astype(F32)


def unpack_small(halves, at, columns):
    count = columns // LANES
    rows = [halves[i % 2][at + (i // 2) * 16 : at + (i // 2) * 16 + 16] for i in range(count)]
    return jnp.concatenate(rows, axis=1).astype(F32)


def passed(block, distance):
    count = lax.axis_size("mp")
    route = [(i, i + distance) for i in range(count) if 0 <= i + distance < count]
    return lax.ppermute(block, "mp", route)


def take_over(own, other, first):
    row = lax.broadcasted_iota(jnp.int32, (HALO, 1), 0)
    return lax.dynamic_update_slice(own, jnp.where(row < first, other, own[:HALO]), (0, 0))


def body(
    layer_input, segments, cotangent, first_gain, first_shift, inward_weight, inward_bias, outward_weight,
    outward_bias, second_gain, second_shift, expand_weight, expand_bias, shrink_weight, shrink_bias,
):
    rows, width = layer_input.shape
    position = lax.axis_index("mp")
    core = lax.axis_index("dp") % 2
    pieces = lax.axis_size("dp") * lax.axis_size("mp") // 2
    place = jnp.stack([position, (position == lax.axis_size("mp") - 1).astype(jnp.int32), core]).astype(jnp.int32)
    pad = ((0, TILE - HALO), (0, 0))
    x_halo = jnp.pad(passed(layer_input[:HALO], -1), pad)
    cot_halo = jnp.pad(passed(cotangent[:HALO], -1), pad)
    weights = (
        first_gain[None], first_shift[None], inward_weight, inward_bias, outward_weight, outward_bias[None],
        second_gain[None], second_shift[None], expand_weight, expand_bias[None], shrink_weight, shrink_bias[None],
    )
    outs = forward_one(place, segments, layer_input, x_halo, cotangent, cot_halo, weights, pieces)
    result, result_halo, triple, attended, upstream, middle_grad, stats, table, mine, other = outs
    feed_piece = scatter_sum(mine, other, pieces)
    input_grad, input_halo, mine, other = backward_two(
        place, table, layer_input, x_halo, first_gain[None], first_shift[None], inward_weight,
        (triple, attended, upstream, middle_grad, stats), pieces,
    )
    first = table[GROUPS, 1]
    result = take_over(result, passed(result_halo[:HALO], 1), first)
    input_grad = take_over(input_grad, passed(input_halo[:HALO], 1), first)
    inward_piece = scatter_sum(mine, other, pieces)
    feed_sums = gather_sum(feed_piece, core, pieces)
    inward_sums = gather_sum(inward_piece, core, pieces)
    hidden = expand_weight.shape[1]
    d_ex = unpack(feed_sums, 0, hidden)
    d_sh = unpack(feed_sums, 192 * hidden // LANES, hidden).T
    d_out = unpack(feed_sums, 192 * 2 * hidden // LANES, width)
    d_in = unpack(inward_sums, 0, 3 * width)
    small = unpack_small(feed_sums, 192 * (2 * hidden + width) // LANES, hidden)
    small2 = unpack_small(inward_sums, 192 * 3 * width // LANES, 3 * width)
    return (
        result, input_grad, small2[5, :width], small2[6, :width], d_in,
        jnp.stack([small2[4, :width], small2[4, 2 * width : 3 * width]]),
        d_out, small[3, :width], small[1, :width], small[2, :width], d_ex, small[8], d_sh, small[0, :width],
    )


def solution(mesh):
    rows = P(("dp", "mp"), None)
    in_specs = (rows, P("dp", None), rows) + (P(),) * 12
    out_specs = (rows, rows) + (P(),) * 12
    return jax.shard_map(body, mesh=mesh, in_specs=in_specs, out_specs=out_specs, check_vma=False)
```

```python
from functools import partial

import jax
import jax.numpy as jnp
from jax import lax
from jax.experimental import pallas as pl
from jax.experimental.pallas import tpu as pltpu
from jax.sharding import PartitionSpec as P

HD = 64
SEQ = 198
EPSILON = 1e-06
MASKED = -1000000000.0
WIN = 256
TILE = 256
HALO = 208
WIDE = 768
OWN = 512
GROUPS = 24
LANES = 128
CHUNK = 256
FEED = 768
BIG = 1 << 20
F32 = jnp.float32
BF16 = jnp.bfloat16
NT = (((1,), (1,)), ((), ()))
TN = (((0,), (0,)), ((), ()))


def row_of(ref):
    return ref[...].reshape(1, -1)


def dot(a, b):
    return jnp.dot(a, b, preferred_element_type=F32)


def dot_nt(a, b):
    return lax.dot_general(a, b, NT, preferred_element_type=F32)


def dot_tn(a, b):
    return lax.dot_general(a, b, TN, preferred_element_type=F32)


def normalize(rows):
    center = jnp.mean(rows, axis=-1, keepdims=True)
    centred = rows - center
    spread = jnp.mean(centred * centred, axis=-1, keepdims=True)
    inverse = lax.rsqrt(spread + EPSILON)
    return centred * inverse, inverse


def normalize_back(upstream, scaled, inverse, gain):
    direct = upstream * gain
    first = jnp.mean(direct, axis=-1, keepdims=True)
    second = jnp.mean(direct * scaled, axis=-1, keepdims=True)
    return inverse * (direct - first - scaled * second)


def gelu_parts(v, half_upstream):
    scaled = v * 0.7071067811865476
    double = 1.0 + lax.erf(scaled)
    bell = jnp.exp2((scaled * scaled) * -1.4426950408889634)
    return (0.5 * v) * double, half_upstream * (double + (v * 0.7978845608028654) * bell)


def image_ends(seg, base, work):
    ident = lax.broadcasted_iota(jnp.int32, (LANES, LANES), 0)
    below = jnp.zeros((LANES, LANES), F32)
    for begin in range(0, seg.shape[1], LANES):
        row = seg[0:1, begin : begin + LANES]
        row = jnp.where(row < 0, BIG, row)
        below = below + jnp.where(row <= ident, 1.0, 0.0)
    ends = jnp.broadcast_to(jnp.sum(below, axis=1, keepdims=True), (LANES, LANES))
    started = jnp.sum(jnp.where(ends < base.astype(F32), 1.0, 0.0), axis=0, keepdims=True)
    work[0:1, :] = ends.T[0:1].astype(jnp.int32)
    work[1:2, :] = started.astype(jnp.int32)


def plan_groups(ends, position, rows, table):
    base = position * rows
    limit = jnp.minimum(base + rows, ends[0, LANES - 1]) - base
    image = jnp.where(position == 0, 0, ends[1, 0] + 1)
    first = jnp.where(position == 0, 0, ends[0, jnp.maximum(image - 1, 0)]) - base

    def body(state):
        at, image, group, window, start, c1, c2 = state
        after = ends[0, jnp.minimum(image, LANES - 1)] - base
        fits = after - window <= WIN

        @pl.when(jnp.logical_not(fits))
        def _():
            write_group(table, group, window, start, c1, c2, at)

        group = jnp.where(fits, group, group + 1)
        new_c1 = jnp.where(fits, jnp.where(at == start, c1, jnp.where(c1 < 0, at, c1)), -1)
        new_c2 = jnp.where(fits, jnp.where(jnp.logical_and(at != start, c1 >= 0), jnp.where(c2 < 0, at, c2), c2), -1)
        start = jnp.where(fits, start, at)
        window = jnp.where(fits, window, (at // 16) * 16)
        return after, image + 1, group, window, start, new_c1, new_c2

    init = (first, image, jnp.int32(0), (first // 16) * 16, first, jnp.int32(-1), jnp.int32(-1))
    at, image, group, window, start, c1, c2 = lax.while_loop(lambda s: s[0] < limit, body, init)
    write_group(table, group, window, start, c1, c2, at)
    table[GROUPS, 0] = group + 1
    table[GROUPS, 1] = first
    table[GROUPS, 2] = at


def write_group(table, group, window, start, c1, c2, end):
    table[group, 0] = window
    table[group, 1] = start - window
    table[group, 2] = jnp.where(c1 < 0, end, c1) - window
    table[group, 3] = jnp.where(c2 < 0, end, c2) - window
    table[group, 4] = end - window


def group_bias(table, group):
    bounds = [table[group, i] for i in range(1, 5)]
    row = lax.broadcasted_iota(jnp.int32, (WIN, LANES), 0)
    col = lax.broadcasted_iota(jnp.int32, (1, WIN), 1)

    def ident(index):
        return sum((index >= b).astype(jnp.int32) for b in bounds)

    row, col = ident(row), ident(col)
    return jnp.concatenate(
        [jnp.where(row == col[:, at : at + LANES], 0.0, MASKED) for at in range(0, WIN, LANES)], axis=1
    )


def head_masks():
    lane = lax.broadcasted_iota(jnp.int32, (WIN, 2 * HD), 1)
    return lane < HD, lane >= HD


def keep_first(ref, window, begin, cols, value):
    head = pl.ds(window, 16)
    old = ref[head, cols]
    row = lax.broadcasted_iota(jnp.int32, (16, 2 * HD), 0)
    ref[head, cols] = jnp.where(row >= begin, value[:16].astype(F32), old.astype(F32)).astype(BF16)
    ref[pl.ds(window + 16, WIN - 16), cols] = value[16:].astype(BF16)


def block_diagonal(pair_t):
    zero = jnp.zeros((HD, pair_t.shape[1]), pair_t.dtype)
    return jnp.concatenate(
        [jnp.concatenate([pair_t[:HD], zero], axis=1), jnp.concatenate([zero, pair_t[HD:]], axis=1)], axis=0
    )


def pipelined(groups, first, second, third, arrive=lambda group, have: have):
    def clamped(group):
        return jnp.minimum(group, groups - 1)

    def half(group, slot):
        first(clamped(group), slot)
        second(clamped(group - 1), 1 - slot)
        third(clamped(group - 2), slot)

    have = arrive(clamped(1), jnp.int32(0))
    first(0, 0)
    first(clamped(1), 1)
    second(0, 0)

    def both(step, have):
        have = arrive(clamped(2 * step + 3), have)
        half(2 * step + 2, 0)
        half(2 * step + 3, 1)
        return have

    have = lax.fori_loop(0, (groups + 1) // 2, both, have)
    arrive(None, have)


def group_rows(table, group, shifted=0):
    return pl.ds(pl.multiple_of(table[group, 0] - shifted, 16), WIN)


def attend_groups(groups, table, triple, attended, stats, scores, peaks, raised, scales, alone=None, shifted=0):
    width = attended.shape[1]
    pairs = range(width // (2 * HD))

    def first(group, slot):
        rows = group_rows(table, group, shifted)
        bias = group_bias(table, group)
        bias = jnp.concatenate([bias, bias], axis=1)
        for pair in pairs:
            query_t = triple[rows, pl.ds(pair * 2 * HD, 2 * HD)].T
            key = triple[rows, pl.ds(width + pair * 2 * HD, 2 * HD)]
            value = dot(key, block_diagonal(query_t)) + bias
            scores[slot][pair] = value
            peaks[slot][pair : pair + 1, :] = jnp.max(value, axis=0, keepdims=True)

    def second(group, slot):
        for pair in pairs:
            peak = peaks[slot][pair : pair + 1, :]
            value = jnp.exp(scores[slot][pair] - peak)
            total = jnp.sum(value, axis=0, keepdims=True)
            raised[slot][pair, :WIN] = value[:, :WIN].astype(BF16)
            raised[slot][pair, WIN:] = value[:, WIN:].astype(BF16)
            scales[slot][pair : pair + 1, :] = 1.0 / total
            lse = peak + jnp.log(total)
            stats[group, pl.ds(2 * pair, 1), :] = lse[:, :WIN]
            stats[group, pl.ds(2 * pair + 1, 1), :] = lse[:, WIN:]

    def third(group, slot):
        rows = group_rows(table, group, shifted)
        for pair in pairs:
            value_t = block_diagonal(triple[rows, pl.ds(2 * width + pair * 2 * HD, 2 * HD)].T)
            out = dot(value_t, raised[slot][pair])
            scale = scales[slot][pair : pair + 1, :]
            out = jnp.concatenate([out[:HD] * scale[:, :WIN], out[HD:] * scale[:, WIN:]], axis=0)
            keep_first(attended, group_rows(table, group).start, table[group, 1], pl.ds(pair * 2 * HD, 2 * HD), out.T)

    if alone is None:
        pipelined(groups, first, second, third)
    else:
        for part in (first, second, third):
            part(alone, 0)


def attend_back_groups(
    groups, table, triple, attended, upstream, stats, triple_grad, scores, agreements, probs_grads, probs, scores_grads,
):
    width = attended.shape[1]
    pairs = range(width // (2 * HD))
    masks = head_masks()

    def columns(pair, block):
        return pl.ds(block * width + pair * 2 * HD, 2 * HD)

    def first(group, slot):
        rows = group_rows(table, group)
        bias = group_bias(table, group)
        bias = jnp.concatenate([bias, bias], axis=1)
        for pair in pairs:
            lse = jnp.concatenate(
                [stats[group, pl.ds(2 * pair, 1), :], stats[group, pl.ds(2 * pair + 1, 1), :]], axis=1
            )
            query_t = triple[rows, columns(pair, 0)].T
            scores[slot][pair] = dot(triple[rows, columns(pair, 1)], block_diagonal(query_t)) + bias - lse
            up_t = upstream[rows, columns(pair, 0)].T
            probs_grads[slot][pair] = dot(triple[rows, columns(pair, 2)], block_diagonal(up_t))
            product = attended[rows, columns(pair, 0)].T.astype(F32) * up_t.astype(F32)
            agreements[slot][pair : pair + 1, :] = jnp.concatenate(
                [jnp.sum(product[:HD], axis=0, keepdims=True), jnp.sum(product[HD:], axis=0, keepdims=True)], axis=1
            )

    def second(group, slot):
        for pair in pairs:
            prob = jnp.exp(scores[slot][pair])
            probs[slot][pair] = prob.astype(BF16)
            agreement = agreements[slot][pair : pair + 1, :]
            scores_grads[slot][pair] = (prob * (probs_grads[slot][pair] - agreement)).astype(BF16)

    def stacked(pair_rows):
        zero = jnp.zeros_like(pair_rows)
        return jnp.concatenate([jnp.where(mask, pair_rows, zero) for mask in masks], axis=0)

    def third(group, slot):
        rows = group_rows(table, group)
        window, begin = rows.start, table[group, 1]
        for pair in pairs:
            scores_grad = scores_grads[slot][pair]
            value_grad = dot(probs[slot][pair], stacked(upstream[rows, columns(pair, 0)]))
            key_grad = dot(scores_grad, stacked(triple[rows, columns(pair, 0)]))
            key_t = block_diagonal(triple[rows, columns(pair, 1)].T)
            query_grad = dot(key_t, jnp.concatenate([scores_grad[:, :WIN], scores_grad[:, WIN:]], axis=0))
            keep_first(triple_grad, window, begin, columns(pair, 0), (query_grad * HD ** (-0.5)).T)
            keep_first(triple_grad, window, begin, columns(pair, 1), key_grad)
            keep_first(triple_grad, window, begin, columns(pair, 2), value_grad)

    pipelined(groups, first, second, third)


def interval(tile, first, end, size=TILE):
    row = lax.broadcasted_iota(jnp.int32, (size, 1), 0) + tile * size
    return jnp.logical_and(row >= first, row < end)


class Mover:
    def __init__(self, sems):
        self.sems = sems
        self.count = 0

    def start(self, source, target):
        copy = pltpu.make_async_copy(source, target, self.sems.at[self.count])
        self.count += 1
        copy.start()
        return copy


def project_rows(rows, gain1, shift1, w_in, b_in, target, spot):
    width = rows.shape[1]
    scaled, _inverse = normalize(rows)
    normed = (scaled * row_of(gain1) + row_of(shift1)).astype(BF16)
    q = dot(normed, w_in[:, :width]) + b_in[0:1, :]
    target[spot, :width] = (q.astype(BF16).astype(F32) * HD ** (-0.5)).astype(BF16)
    target[spot, width : 2 * width] = dot(normed, w_in[:, width : 2 * width]).astype(BF16)
    target[spot, 2 * width :] = (dot(normed, w_in[:, 2 * width :]) + b_in[1:2, :]).astype(BF16)


def kernel_own(
    place, seg, gain1, shift1, b_in, x_in, w_in_in,
    triple_out, attended_out, stats, table,
    x, w_in, triple, attended, work, ends, scores, peaks, raised, scales, sems, tile_sems,
):
    rows, width = x_in.shape
    move = Mover(sems)
    early = [move.start(w_in_in, w_in), move.start(x_in, x)]
    image_ends(seg, place[0] * rows, work)
    end_copy = move.start(work, ends)
    attended[...] = jnp.zeros_like(attended)
    spare = pl.ds(rows, triple.shape[0] - rows)
    triple[spare, :] = jnp.zeros((triple.shape[0] - rows, 3 * width), BF16)
    end_copy.wait()
    plan_groups(ends, place[0], rows, table)
    for copy in early:
        copy.wait()

    def step_copy(step):
        spot = pl.ds(pl.multiple_of(step * OWN, OWN), OWN)
        return pltpu.make_async_copy(triple.at[spot], triple_out.at[spot], tile_sems.at[step])

    def step_rows(step, _):
        spot = pl.ds(pl.multiple_of(step * OWN, OWN), OWN)
        project_rows(x[spot, :].astype(F32), gain1, shift1, w_in, b_in, triple, spot)
        step_copy(step).start()
        return 0

    lax.fori_loop(0, rows // OWN, step_rows, 0)
    attend_groups(jnp.maximum(table[GROUPS, 0] - 1, 1), table, triple, attended, stats, scores, peaks, raised, scales)
    leaving = move.start(attended, attended_out)
    for step in range(rows // OWN):
        step_copy(step).wait()
    leaving.wait()


def kernel_rest(
    place, table, gain1, shift1, b_in, b_out, gain2, shift2, b_ex,
    x_in, cot_in, halo_in, triple_in, attended_in, stats_in, w_in_in, w_out_in, w_ex_in, w_sh_in,
    middle_out, middle_grad_out, hidden_out, triple_grad_out, mine, other,
    x, back, w_in, w_out, w_ex, w_sh, triple, attended, middle, middle_grad, upstream, hidden, triple_grad, stats,
    d_ex, d_sh, d_out, product, sums, small, scores, peaks, raised, scales, probs_grads, probs, scores_grads,
    sems, tile_sems,
):
    rows, width = x_in.shape
    total = x.shape[0]
    tiles = total // FEED
    normed2, normed_grad = upstream, middle_grad
    move = Mover(sems)
    own, over = pl.ds(0, rows), pl.ds(rows, HALO)
    early = [
        move.start(halo_in.at[:, pl.ds(0, width)], x.at[over]),
        move.start(w_in_in, w_in),
        move.start(stats_in, stats),
        move.start(triple_in, triple.at[own]),
        move.start(attended_in, attended),
    ]
    late = [
        move.start(w_out_in, w_out),
        move.start(x_in, x.at[own]),
        move.start(cot_in, back.at[own]),
        move.start(halo_in.at[:, pl.ds(width, width)], back.at[over]),
        move.start(w_ex_in, w_ex),
        move.start(w_sh_in, w_sh),
    ]
    rest = pl.ds(rows + HALO, total - rows - HALO)
    x[rest, :] = jnp.zeros((total - rows - HALO, width), BF16)
    back[rest, :] = jnp.zeros((total - rows - HALO, width), BF16)
    for ref in (d_ex, d_sh, d_out, product, sums, small, triple_grad):
        ref[...] = jnp.zeros_like(ref)
    groups, first, end = table[GROUPS, 0], table[GROUPS, 1], table[GROUPS, 2]
    for copy in early:
        copy.wait()
    tail = pl.ds(rows, TILE)
    project_rows(x[tail, :].astype(F32), gain1, shift1, w_in, b_in, triple, tail)
    attend_groups(groups, table, triple, attended, stats, scores, peaks, raised, scales, alone=groups - 1)
    for copy in late:
        copy.wait()
    leaving = []

    hidden_width = w_ex.shape[1]
    begins = list(range(0, hidden_width, CHUNK))

    def wide_rows(step):
        return pl.ds(pl.multiple_of(step * WIDE, WIDE), WIDE)

    def before_feed(step, _):
        spot = wide_rows(step)
        value = x[spot, :].astype(F32) + dot(attended[spot, :], w_out[...]) + row_of(b_out)
        scaled, _inverse = normalize(value)
        middle[spot, :] = value
        normed2[spot, :] = (scaled * row_of(gain2) + row_of(shift2)).astype(BF16)
        keep = interval(step, first, end, WIDE)
        back[spot, :] = jnp.where(keep, back[spot, :].astype(F32), 0.0).astype(BF16)
        return 0

    def feed(tile, _):
        spot = pl.ds(pl.multiple_of(tile * FEED, FEED), FEED)
        normed = normed2[spot, :]
        back_low = back[spot, :]
        back_half = (0.5 * back_low.astype(F32)).astype(BF16)

        def first_part(begin):
            cols = slice(begin, begin + CHUNK)
            before = dot(normed, w_ex[:, cols]) + b_ex[cols].reshape(1, -1)
            return before, dot_nt(back_half, w_sh[cols, :])

        held = [first_part(begins[0])]
        total_grad = jnp.zeros((FEED, width), F32)
        for index, begin in enumerate(begins):
            cols = slice(begin, begin + CHUNK)
            if index + 1 < len(begins):
                held.append(first_part(begins[index + 1]))
            value, grad = gelu_parts(*held[index])
            value, grad = value.astype(BF16), grad.astype(BF16)
            hidden[spot, cols] = value
            total_grad = total_grad + dot_nt(grad, w_ex[:, cols])
            d_sh[:, cols] += dot_tn(back_low, value)
            d_ex[:, cols] += dot_tn(normed, grad)
            small[4:5, cols] += jnp.sum(grad.astype(F32), axis=0, keepdims=True)
        normed_grad[spot, :] = total_grad
        pltpu.make_async_copy(hidden.at[spot], hidden_out.at[spot], tile_sems.at[0]).start()
        return 0

    def after_feed(step, _):
        spot = wide_rows(step)
        back32 = back[spot, :].astype(F32)
        scaled, inverse = normalize(middle[spot, :])
        upstream2 = normed_grad[spot, :]
        small[0:1, :width] += jnp.sum(back32, axis=0, keepdims=True)
        small[1:2, :width] += jnp.sum(upstream2 * scaled, axis=0, keepdims=True)
        small[2:3, :width] += jnp.sum(upstream2, axis=0, keepdims=True)
        grad = back32 + normalize_back(upstream2, scaled, inverse, row_of(gain2))
        small[3:4, :width] += jnp.sum(grad, axis=0, keepdims=True)
        middle_grad[spot, :] = grad
        grad_low = grad.astype(BF16)
        d_out[...] += dot_tn(attended[spot, :], grad_low)
        upstream[spot, :] = dot_nt(grad_low, w_out[...]).astype(BF16)
        pltpu.make_async_copy(middle_grad.at[spot], middle_grad_out.at[spot], tile_sems.at[1]).start()
        return 0

    lax.fori_loop(0, total // WIDE, before_feed, 0)
    leaving.append(move.start(middle, middle_out))
    lax.fori_loop(0, tiles, feed, 0)
    lax.fori_loop(0, total // WIDE, after_feed, 0)
    attend_back_groups(
        groups, table, triple, attended, upstream, stats, triple_grad, scores, peaks, probs_grads, probs, scores_grads,
    )
    leaving.append(move.start(triple_grad, triple_grad_out))
    ones = jnp.ones((16, WIDE), BF16)

    def multiply(step, _):
        spot = wide_rows(step)
        scaled, _inverse = normalize(x[spot, :].astype(F32))
        grad = triple_grad[spot, :]
        product[...] += dot_tn(scaled.astype(BF16), grad)
        sums[...] += dot(ones, grad)
        return 0

    lax.fori_loop(0, total // WIDE, multiply, 0)
    gain = jnp.broadcast_to(row_of(gain1), (LANES, width)).T
    shift = jnp.broadcast_to(row_of(shift1), (LANES, width)).T
    by_gain = jnp.zeros((width, LANES), F32)
    by_shift = jnp.zeros((width, LANES), F32)
    for begin in range(0, 3 * width, LANES):
        cols = slice(begin, begin + LANES)
        block, sum_row = product[:, cols], sums[0:1, cols]
        weight = w_in[:, cols].astype(F32)
        by_gain = by_gain + weight * block
        by_shift = by_shift + weight * sum_row
        product[:, cols] = gain * block + shift * sum_row
    small[5:6, : 3 * width] = sums[0:1, :]
    by_gain = jnp.broadcast_to(jnp.sum(by_gain, axis=1, keepdims=True), (width, LANES)).T
    by_shift = jnp.broadcast_to(jnp.sum(by_shift, axis=1, keepdims=True), (width, LANES)).T
    small[6:7, :width] = by_gain[0:1]
    small[7:8, :width] = by_shift[0:1]
    pack((d_ex, d_sh, d_out, product), small, place[2], mine, other)
    for copy in leaving:
        copy.wait()
    pltpu.make_async_copy(hidden, hidden_out, tile_sems.at[0]).wait()
    pltpu.make_async_copy(middle_grad, middle_grad_out, tile_sems.at[1]).wait()


def pack(grads, small, core, mine, other):
    half = grads[0].shape[0] // 2
    at = 0
    for grad in grads:
        for begin in range(0, grad.shape[1], LANES):
            cols = slice(begin, begin + LANES)
            mine[pl.ds(at, half), :] = grad[pl.ds(pl.multiple_of(core * half, half), half), cols].astype(BF16)
            other[pl.ds(at, half), :] = grad[pl.ds(pl.multiple_of((1 - core) * half, half), half), cols].astype(BF16)
            at += half
    rest = mine.shape[0] - at
    mine[pl.ds(at, rest), :] = jnp.zeros((rest, LANES), BF16)
    other[pl.ds(at, rest), :] = jnp.zeros((rest, LANES), BF16)
    count = small.shape[1] // LANES
    for index in range(count):
        cols = slice(index * LANES, (index + 1) * LANES)
        spot = pl.ds(at + (index // 2) * 16, 16)

        @pl.when(core == index % 2)
        def _():
            mine[spot, :] = small[:, cols].astype(BF16)

        @pl.when(core != index % 2)
        def _():
            other[spot, :] = small[:, cols].astype(BF16)


def step_copies(arrays, step, sems):
    spot = pl.ds(step * WIDE, WIDE)
    return [
        pltpu.make_async_copy(source.at[spot], target.at[spot], sems.at[step, at])
        for at, (source, target) in enumerate(arrays)
    ]


def leave(value_ref, own_out, halo_out, step, sems):
    rows = own_out.shape[0]
    begin, end = step * WIDE, (step + 1) * WIDE
    own = pl.ds(begin, min(rows, end) - begin)
    copies = [pltpu.make_async_copy(value_ref.at[own], own_out.at[own], sems.at[step, 6])]
    if end > rows:
        copies.append(pltpu.make_async_copy(value_ref.at[pl.ds(rows, end - rows)], halo_out, sems.at[step, 7]))
    for copy in copies:
        copy.start()
    return copies


def kernel_input(
    after, gain1, x_in, halo_in, w_in_in, triple_grad_in, middle_grad_in, out, out_halo,
    x, w_in, triple_grad, middle_grad, sems, step_sems,
):
    rows, width = x_in.shape
    total = x.shape[0]
    move = Mover(sems)
    early = [
        move.start(w_in_in, w_in),
        move.start(x_in, x.at[pl.ds(0, rows)]),
        move.start(halo_in.at[:, pl.ds(0, width)], x.at[pl.ds(rows, HALO)]),
    ]
    arrays = ((triple_grad_in, triple_grad), (middle_grad_in, middle_grad))
    steps = range(total // WIDE)
    parts = [step_copies(arrays, step, step_sems) for step in steps]
    for part in parts:
        for copy in part:
            copy.start()
    x[pl.ds(rows + HALO, total - rows - HALO), :] = jnp.zeros((total - rows - HALO, width), BF16)
    for copy in early:
        copy.wait()
    leaving = []
    for step in steps:
        for copy in parts[step]:
            copy.wait()
        spot = pl.ds(step * WIDE, WIDE)
        scaled, inverse = normalize(x[spot, :].astype(F32))
        normed_grad = dot_nt(triple_grad[spot, :], w_in[...])
        middle_grad[spot, :] = middle_grad[spot, :] + normalize_back(normed_grad, scaled, inverse, row_of(gain1))
        leaving += leave(middle_grad, out, out_halo, step, step_sems)
    for copy in leaving:
        copy.wait()


def kernel_result(
    after, table, b_sh, middle_in, hidden_in, w_sh_in, out, out_halo, middle, hidden, w_sh, value, sems, step_sems,
):
    total = middle.shape[0]
    move = Mover(sems)
    weight_copy = move.start(w_sh_in, w_sh)
    arrays = ((middle_in, middle), (hidden_in, hidden))
    steps = range(total // WIDE)
    parts = [step_copies(arrays, step, step_sems) for step in steps]
    for part in parts:
        for copy in part:
            copy.start()
    weight_copy.wait()
    leaving = []
    for step in steps:
        for copy in parts[step]:
            copy.wait()
        spot = pl.ds(step * WIDE, WIDE)
        keep = interval(step, table[GROUPS, 1], table[GROUPS, 2], WIDE)
        row = middle[spot, :] + row_of(b_sh) + dot(hidden[spot, :], w_sh[...])
        value[spot, :] = jnp.where(keep, row, 0.0).astype(BF16)
        leaving += leave(value, out, out_halo, step, step_sems)
    for copy in leaving:
        copy.wait()


def kernel_add(mine, other, out):
    out[...] = (mine[...].astype(F32) + other[...].astype(F32)).astype(BF16)


def kernel_sum(extra, *refs):
    parts_in, out, parts, piece, sems = refs[extra:]
    count = parts.shape[0]
    quarter = max(count // 4, 1)
    copies = []
    for index, begin in enumerate(range(0, count, quarter)):
        spot = pl.ds(begin, quarter)
        copies.append(pltpu.make_async_copy(parts_in.at[spot], parts.at[spot], sems.at[index]))
        copies[-1].start()
    total = jnp.zeros(piece.shape, F32)
    for index, copy in enumerate(copies):
        copy.wait()
        for part in range(index * quarter, (index + 1) * quarter):
            total = total + parts[part].astype(F32)
    piece[...] = total.astype(BF16)
    for part in range(count):
        pltpu.make_async_copy(piece, out.at[part], sems.at[4]).start()
    pltpu.make_async_copy(parts, out, sems.at[4]).wait()


def halves_of(place, mine, other):
    def both(at, count):
        first, second = mine[pl.ds(at, count), :].astype(F32), other[pl.ds(at, count), :].astype(F32)
        swap = place[2] == 1
        return jnp.where(swap, second, first), jnp.where(swap, first, second)

    return both


def unpack(both, at, out):
    for begin in range(0, out.shape[1], LANES):
        low, high = both(at, 192)
        out[:192, begin : begin + LANES] = low
        out[192:, begin : begin + LANES] = high
        at += 192
    return at


def small_blocks(both, at, columns):
    blocks = []
    for index in range(columns // LANES):
        blocks.append(both(at + index // 2 * 16, 16)[index % 2])
    return jnp.concatenate(blocks, axis=1)


def kernel_unpack(
    place, mine, other, d_ex, d_sh, d_out, d_in, b_in, b_sh, gain2, shift2, b_out, b_ex, gain1, shift1
):
    both = halves_of(place, mine, other)
    width = d_out.shape[0]
    at = unpack(both, 0, d_ex)
    for begin in range(0, d_sh.shape[0], LANES):
        low, high = both(at, 192)
        d_sh[begin : begin + LANES, :] = jnp.concatenate([low, high], axis=0).T
        at += 192
    small = small_blocks(both, unpack(both, unpack(both, at, d_out), d_in), d_ex.shape[1])
    for row, ref in ((0, b_sh), (1, gain2), (2, shift2), (3, b_out), (6, gain1), (7, shift1)):
        ref[...] = small[row, :width]
    b_ex[...] = small[4]
    b_in[0:1, :] = small[5:6, :width]
    b_in[1:2, :] = small[5:6, 2 * width : 3 * width]


VMEM = pl.BlockSpec(memory_space=pltpu.VMEM)
SMEM = pl.BlockSpec(memory_space=pltpu.SMEM)
ANY = pl.BlockSpec(memory_space=pl.ANY)


def params(mib):
    return pltpu.CompilerParams(vmem_limit_bytes=mib * 1024 * 1024)


def cost(flops, moved):
    return pl.CostEstimate(flops=int(flops), bytes_accessed=int(moved), transcendentals=0)


def shape(dims, dtype):
    return jax.ShapeDtypeStruct(dims, dtype)


def packed_rows(columns, small, pieces):
    half = columns // LANES * 192 + (small // LANES + 1) // 2 * 16
    return pieces * (-(-half // (8 * pieces)) * 8)


def attention_scratch(pairs):
    return [
        [pltpu.VMEM((pairs, WIN, 2 * WIN), F32)] * 2,
        [pltpu.VMEM((8, 2 * WIN), F32)] * 2,
        [pltpu.VMEM((pairs, 2 * WIN, WIN), BF16)] * 2,
        [pltpu.VMEM((8, 2 * WIN), F32)] * 2,
    ]


def own_part(place, segments, gain1, shift1, b_in, x, w_in):
    rows, width = x.shape
    total = rows + TILE
    vmem = pltpu.VMEM
    return pl.pallas_call(
        kernel_own,
        out_shape=(
            shape((rows, 3 * width), BF16),
            shape((total, width), BF16),
            shape((GROUPS, 8, WIN), F32),
            shape((GROUPS + 1, 8), jnp.int32),
        ),
        in_specs=[SMEM] + [VMEM] * 4 + [ANY] * 2,
        out_specs=(ANY, ANY, VMEM, SMEM),
        scratch_shapes=[
            vmem((rows, width), BF16),
            vmem(w_in.shape, BF16),
            vmem((total, 3 * width), BF16),
            vmem((total, width), BF16),
            vmem((8, LANES), jnp.int32),
            pltpu.SMEM((8, LANES), jnp.int32),
            *attention_scratch(width // (2 * HD)),
            pltpu.SemaphoreType.DMA((8,)),
            pltpu.SemaphoreType.DMA((rows // OWN,)),
        ],
        compiler_params=params(58),
        cost_estimate=cost(2 * 6 * rows * width * 3 * width, 1e7),
        name="own_part",
    )(place, segments, gain1, shift1, b_in, x, w_in)


def rest_part(place, table, vectors, x, cot, halo, triple, attended, stats, w_in, w_out, w_ex, w_sh, pieces):
    rows, width = x.shape
    total = rows + TILE
    hidden = w_ex.shape[1]
    packed = packed_rows(2 * hidden + 4 * width, hidden, pieces)
    vmem = pltpu.VMEM
    pairs = width // (2 * HD)
    square, row = vmem((pairs, WIN, 2 * WIN), F32), vmem((8, 2 * WIN), F32)
    low = vmem((pairs, WIN, 2 * WIN), BF16)
    return pl.pallas_call(
        kernel_rest,
        out_shape=(
            shape((total, width), F32),
            shape((total, width), F32),
            shape((total, hidden), BF16),
            shape((total, 3 * width), BF16),
            shape((packed, LANES), BF16),
            shape((packed, LANES), BF16),
        ),
        in_specs=[SMEM, SMEM] + [VMEM] * 7 + [ANY] * 10,
        out_specs=tuple([ANY] * 4 + [VMEM] * 2),
        scratch_shapes=[
            vmem((total, width), BF16),
            vmem((total, width), BF16),
            vmem(w_in.shape, BF16),
            vmem(w_out.shape, BF16),
            vmem(w_ex.shape, BF16),
            vmem(w_sh.shape, BF16),
            vmem((total, 3 * width), BF16),
            vmem((total, width), BF16),
            vmem((total, width), F32),
            vmem((total, width), F32),
            vmem((total, width), BF16),
            vmem((total, hidden), BF16),
            vmem((total, 3 * width), BF16),
            vmem((GROUPS, 8, WIN), F32),
            vmem((width, hidden), F32),
            vmem((width, hidden), F32),
            vmem((width, width), F32),
            vmem((width, 3 * width), F32),
            vmem((16, 3 * width), F32),
            vmem((16, hidden), F32),
            [square] * 2,
            [row] * 2,
            [vmem((pairs, 2 * WIN, WIN), BF16)],
            [row],
            [square] * 2,
            [low] * 2,
            [low] * 2,
            pltpu.SemaphoreType.DMA((16,)),
            pltpu.SemaphoreType.DMA((2,)),
        ],
        compiler_params=params(62),
        cost_estimate=cost(2 * 9 * rows * width * (3 * width + 8 * width), 3e7),
        name="rest_part",
    )(place, table, *vectors, x, cot, halo, triple, attended, stats, w_in, w_out, w_ex, w_sh)


def input_gradient(after, gain1, x, halo, w_in, triple_grad, middle_grad):
    rows, width = x.shape
    total = triple_grad.shape[0]
    vmem = pltpu.VMEM
    return pl.pallas_call(
        kernel_input,
        out_shape=(shape((rows, width), F32), shape((TILE, width), F32)),
        in_specs=[ANY, VMEM] + [ANY] * 5,
        out_specs=(ANY, ANY),
        scratch_shapes=[
            vmem((total, width), BF16),
            vmem(w_in.shape, BF16),
            vmem((total, 3 * width), BF16),
            vmem((total, width), F32),
            pltpu.SemaphoreType.DMA((4,)),
            pltpu.SemaphoreType.DMA((total // WIDE, 8)),
        ],
        compiler_params=params(58),
        cost_estimate=cost(2 * rows * width * 9 * width, 1.4e7),
        name="input_gradient",
    )(after, gain1, x, halo, w_in, triple_grad, middle_grad)


def layer_result(after, table, b_sh, middle, hidden, w_sh):
    total, width = middle.shape
    vmem = pltpu.VMEM
    return pl.pallas_call(
        kernel_result,
        out_shape=(shape((total - TILE, width), BF16), shape((TILE, width), BF16)),
        in_specs=[ANY, SMEM, VMEM] + [ANY] * 3,
        out_specs=(ANY, ANY),
        scratch_shapes=[
            vmem(middle.shape, F32),
            vmem(hidden.shape, BF16),
            vmem(w_sh.shape, BF16),
            vmem(middle.shape, BF16),
            pltpu.SemaphoreType.DMA((2,)),
            pltpu.SemaphoreType.DMA((total // WIDE, 8)),
        ],
        compiler_params=params(58),
        cost_estimate=cost(2 * total * width * 8 * width, 1.3e7),
        name="layer_result",
    )(after, table, b_sh, middle, hidden, w_sh)


def add_halves(mine, other):
    return pl.pallas_call(
        kernel_add,
        out_shape=shape(mine.shape, BF16),
        in_specs=[VMEM, VMEM],
        out_specs=VMEM,
        compiler_params=params(58),
        cost_estimate=cost(mine.size, mine.size * 6),
        name="add_halves",
    )(mine, other)


def sum_parts(after, parts):
    return pl.pallas_call(
        partial(kernel_sum, len(after)),
        out_shape=shape(parts.shape, BF16),
        in_specs=[ANY] * (len(after) + 1),
        out_specs=ANY,
        scratch_shapes=[
            pltpu.VMEM(parts.shape, BF16),
            pltpu.VMEM(parts.shape[1:], BF16),
            pltpu.SemaphoreType.DMA((5,)),
        ],
        compiler_params=params(58),
        cost_estimate=cost(parts.size, parts.size * 4),
        name="sum_parts",
    )(*after, parts)


def unpack_call(kernel, name, place, mine, other, shapes):
    return pl.pallas_call(
        kernel,
        out_shape=tuple(shape(dims, F32) for dims in shapes),
        in_specs=[SMEM, VMEM, VMEM],
        out_specs=tuple([VMEM] * len(shapes)),
        compiler_params=params(58),
        cost_estimate=cost(mine.size, mine.size * 12),
        name=name,
    )(place, mine, other)


def same_core_groups():
    packs, parts = lax.axis_size("dp"), lax.axis_size("mp")
    return [[d * parts + m for d in range(c, packs, 2) for m in range(parts)] for c in range(2)]


def swap_cores(block):
    packs = lax.axis_size("dp")
    return lax.ppermute(block, "dp", [(i, i ^ 1) for i in range(packs)])


def exchange(parts):
    return lax.all_to_all(parts, ("dp", "mp"), 0, 0, axis_index_groups=same_core_groups())


def passed(block, distance):
    count = lax.axis_size("mp")
    route = [(i, i + distance) for i in range(count) if 0 <= i + distance < count]
    return lax.ppermute(block, "mp", route)


def take_over(own, other, first):
    row = lax.broadcasted_iota(jnp.int32, (HALO, 1), 0)
    return lax.dynamic_update_slice(own, jnp.where(row < first, other, own[:HALO]), (0, 0))


def body(
    layer_input, segments, cotangent, first_gain, first_shift, inward_weight, inward_bias, outward_weight,
    outward_bias, second_gain, second_shift, expand_weight, expand_bias, shrink_weight, shrink_bias,
):
    rows, width = layer_input.shape
    hidden_width = expand_weight.shape[1]
    position = lax.axis_index("mp")
    core = lax.axis_index("dp") % 2
    pieces = lax.axis_size("dp") * lax.axis_size("mp") // 2
    place = jnp.stack([position, position, core]).astype(jnp.int32)
    gain1, shift1, b_out, gain2, shift2, b_ex, b_sh = (
        first_gain, first_shift, outward_bias, second_gain, second_shift, expand_bias, shrink_bias
    )
    halo = passed(jnp.concatenate([layer_input[:HALO], cotangent[:HALO]], axis=1), -1)
    triple, attended, stats, table = own_part(
        place, segments, gain1, shift1, inward_bias, layer_input, inward_weight
    )
    middle, middle_grad, hidden, triple_grad, mine, other = rest_part(
        place, table, (gain1, shift1, inward_bias, b_out, gain2, shift2, b_ex), layer_input, cotangent, halo, triple,
        attended, stats, inward_weight, outward_weight, expand_weight, shrink_weight, pieces,
    )
    both = add_halves(mine, swap_cores(other))
    parts = exchange(both.reshape(pieces, -1, LANES))
    input_grad, input_halo = input_gradient(both, gain1, layer_input, halo, inward_weight, triple_grad, middle_grad)
    result, result_halo = layer_result(input_halo, table, b_sh, middle, hidden, shrink_weight)
    first = table[GROUPS, 1]
    input_grad = take_over(input_grad, passed(input_halo[:HALO], 1), first)
    result = take_over(result, passed(result_halo[:HALO], 1), first)
    mine = exchange(sum_parts((input_grad, result), parts)).reshape(-1, LANES)
    square, row = (width, width), (width,)
    d_ex, d_sh, d_out, d_in, d_b_in, d_b_sh, d_gain2, d_shift2, d_b_out, d_b_ex, d_gain1, d_shift1 = unpack_call(
        kernel_unpack, "unpack", place, mine, swap_cores(mine),
        ((width, hidden_width), (hidden_width, width), square, (width, 3 * width), (2, width)) + (row,) * 4
        + ((hidden_width,), row, row),
    )
    return (
        result, input_grad, d_gain1, d_shift1, d_in, d_b_in, d_out, d_b_out, d_gain2, d_shift2, d_ex, d_b_ex, d_sh,
        d_b_sh,
    )


def solution(mesh):
    rows = P(("dp", "mp"), None)
    in_specs = (rows, P("dp", None), rows) + (P(),) * 12
    out_specs = (rows, rows) + (P(),) * 12
    return jax.shard_map(body, mesh=mesh, in_specs=in_specs, out_specs=out_specs, check_vma=False)
```

```python
from functools import partial

import jax
import jax.numpy as jnp
from jax import lax
from jax.experimental import pallas as pl
from jax.experimental.pallas import tpu as pltpu
from jax.sharding import PartitionSpec as P

HD = 64
SEQ = 198
EPSILON = 1e-06
MASKED = -1000000000.0
WIN = 256
TILE = 256
HALO = 208
WIDE = 768
OWN = 512
GROUPS = 24
LANES = 128
CHUNK = 256
FEED = 768
BIG = 1 << 20
F32 = jnp.float32
BF16 = jnp.bfloat16
NT = (((1,), (1,)), ((), ()))
TN = (((0,), (0,)), ((), ()))


def row_of(ref):
    return ref[...].reshape(1, -1)


def dot(a, b):
    return jnp.dot(a, b, preferred_element_type=F32)


def dot_nt(a, b):
    return lax.dot_general(a, b, NT, preferred_element_type=F32)


def dot_tn(a, b):
    return lax.dot_general(a, b, TN, preferred_element_type=F32)


def normalize(rows):
    center = jnp.mean(rows, axis=-1, keepdims=True)
    centred = rows - center
    spread = jnp.mean(centred * centred, axis=-1, keepdims=True)
    inverse = lax.rsqrt(spread + EPSILON)
    return centred * inverse, inverse


def normalize_back(upstream, scaled, inverse, gain):
    direct = upstream * gain
    first = jnp.mean(direct, axis=-1, keepdims=True)
    second = jnp.mean(direct * scaled, axis=-1, keepdims=True)
    return inverse * (direct - first - scaled * second)


def gelu_parts(v, half_upstream):
    scaled = v * 0.7071067811865476
    double = 1.0 + lax.erf(scaled)
    bell = jnp.exp2((scaled * scaled) * -1.4426950408889634)
    return (0.5 * v) * double, half_upstream * (double + (v * 0.7978845608028654) * bell)


def image_ends(seg, base, work):
    ident = lax.broadcasted_iota(jnp.int32, (LANES, LANES), 0)
    below = jnp.zeros((LANES, LANES), F32)
    for begin in range(0, seg.shape[1], LANES):
        row = seg[0:1, begin : begin + LANES]
        row = jnp.where(row < 0, BIG, row)
        below = below + jnp.where(row <= ident, 1.0, 0.0)
    ends = jnp.broadcast_to(jnp.sum(below, axis=1, keepdims=True), (LANES, LANES))
    started = jnp.sum(jnp.where(ends < base.astype(F32), 1.0, 0.0), axis=0, keepdims=True)
    work[0:1, :] = ends.T[0:1].astype(jnp.int32)
    work[1:2, :] = started.astype(jnp.int32)


def plan_groups(ends, position, rows, table):
    base = position * rows
    limit = jnp.minimum(base + rows, ends[0, LANES - 1]) - base
    image = jnp.where(position == 0, 0, ends[1, 0] + 1)
    first = jnp.where(position == 0, 0, ends[0, jnp.maximum(image - 1, 0)]) - base

    def body(state):
        at, image, group, window, start, c1, c2 = state
        after = ends[0, jnp.minimum(image, LANES - 1)] - base
        fits = after - window <= WIN

        @pl.when(jnp.logical_not(fits))
        def _():
            write_group(table, group, window, start, c1, c2, at)

        group = jnp.where(fits, group, group + 1)
        new_c1 = jnp.where(fits, jnp.where(at == start, c1, jnp.where(c1 < 0, at, c1)), -1)
        new_c2 = jnp.where(fits, jnp.where(jnp.logical_and(at != start, c1 >= 0), jnp.where(c2 < 0, at, c2), c2), -1)
        start = jnp.where(fits, start, at)
        window = jnp.where(fits, window, (at // 16) * 16)
        return after, image + 1, group, window, start, new_c1, new_c2

    init = (first, image, jnp.int32(0), (first // 16) * 16, first, jnp.int32(-1), jnp.int32(-1))
    at, image, group, window, start, c1, c2 = lax.while_loop(lambda s: s[0] < limit, body, init)
    write_group(table, group, window, start, c1, c2, at)
    table[GROUPS, 0] = group + 1
    table[GROUPS, 1] = first
    table[GROUPS, 2] = at


def write_group(table, group, window, start, c1, c2, end):
    table[group, 0] = window
    table[group, 1] = start - window
    table[group, 2] = jnp.where(c1 < 0, end, c1) - window
    table[group, 3] = jnp.where(c2 < 0, end, c2) - window
    table[group, 4] = end - window


def group_bias(table, group):
    bounds = [table[group, i] for i in range(1, 5)]
    row = lax.broadcasted_iota(jnp.int32, (WIN, LANES), 0)
    col = lax.broadcasted_iota(jnp.int32, (1, WIN), 1)

    def ident(index):
        return sum((index >= b).astype(jnp.int32) for b in bounds)

    row, col = ident(row), ident(col)
    return jnp.concatenate(
        [jnp.where(row == col[:, at : at + LANES], 0.0, MASKED) for at in range(0, WIN, LANES)], axis=1
    )


def head_masks():
    lane = lax.broadcasted_iota(jnp.int32, (WIN, 2 * HD), 1)
    return lane < HD, lane >= HD


def keep_first(ref, window, begin, cols, value):
    head = pl.ds(window, 16)
    old = ref[head, cols]
    row = lax.broadcasted_iota(jnp.int32, (16, 2 * HD), 0)
    ref[head, cols] = jnp.where(row >= begin, value[:16].astype(F32), old.astype(F32)).astype(BF16)
    ref[pl.ds(window + 16, WIN - 16), cols] = value[16:].astype(BF16)


def block_diagonal(pair_t):
    zero = jnp.zeros((HD, pair_t.shape[1]), pair_t.dtype)
    return jnp.concatenate(
        [jnp.concatenate([pair_t[:HD], zero], axis=1), jnp.concatenate([zero, pair_t[HD:]], axis=1)], axis=0
    )


def pipelined(groups, first, second, third, arrive=lambda group, have: have):
    def clamped(group):
        return jnp.minimum(group, groups - 1)

    def half(group, slot):
        first(clamped(group), slot)
        second(clamped(group - 1), 1 - slot)
        third(clamped(group - 2), slot)

    have = arrive(clamped(1), jnp.int32(0))
    first(0, 0)
    first(clamped(1), 1)
    second(0, 0)

    def both(step, have):
        have = arrive(clamped(2 * step + 3), have)
        half(2 * step + 2, 0)
        half(2 * step + 3, 1)
        return have

    have = lax.fori_loop(0, (groups + 1) // 2, both, have)
    arrive(None, have)


def group_rows(table, group, shifted=0):
    return pl.ds(pl.multiple_of(table[group, 0] - shifted, 16), WIN)


def attend_groups(groups, table, triple, attended, stats, scores, peaks, raised, scales, alone=None, shifted=0):
    width = attended.shape[1]
    pairs = range(width // (2 * HD))

    def first(group, slot):
        rows = group_rows(table, group, shifted)
        bias = group_bias(table, group)
        bias = jnp.concatenate([bias, bias], axis=1)
        for pair in pairs:
            query_t = triple[rows, pl.ds(pair * 2 * HD, 2 * HD)].T
            key = triple[rows, pl.ds(width + pair * 2 * HD, 2 * HD)]
            value = dot(key, block_diagonal(query_t)) + bias
            scores[slot][pair] = value
            peaks[slot][pair : pair + 1, :] = jnp.max(value, axis=0, keepdims=True)

    def second(group, slot):
        for pair in pairs:
            peak = peaks[slot][pair : pair + 1, :]
            value = jnp.exp(scores[slot][pair] - peak)
            total = jnp.sum(value, axis=0, keepdims=True)
            raised[slot][pair, :WIN] = value[:, :WIN].astype(BF16)
            raised[slot][pair, WIN:] = value[:, WIN:].astype(BF16)
            scales[slot][pair : pair + 1, :] = 1.0 / total
            lse = peak + jnp.log(total)
            stats[group, pl.ds(2 * pair, 1), :] = lse[:, :WIN]
            stats[group, pl.ds(2 * pair + 1, 1), :] = lse[:, WIN:]

    def third(group, slot):
        rows = group_rows(table, group, shifted)
        for pair in pairs:
            value_t = block_diagonal(triple[rows, pl.ds(2 * width + pair * 2 * HD, 2 * HD)].T)
            out = dot(value_t, raised[slot][pair])
            scale = scales[slot][pair : pair + 1, :]
            out = jnp.concatenate([out[:HD] * scale[:, :WIN], out[HD:] * scale[:, WIN:]], axis=0)
            keep_first(attended, group_rows(table, group).start, table[group, 1], pl.ds(pair * 2 * HD, 2 * HD), out.T)

    if alone is None:
        pipelined(groups, first, second, third)
    else:
        for part in (first, second, third):
            part(alone, 0)


def attend_back_groups(
    groups, table, triple, attended, upstream, stats, triple_grad, scores, agreements, probs_grads, probs, scores_grads,
):
    width = attended.shape[1]
    pairs = range(width // (2 * HD))
    masks = head_masks()

    def columns(pair, block):
        return pl.ds(block * width + pair * 2 * HD, 2 * HD)

    def first(group, slot):
        rows = group_rows(table, group)
        bias = group_bias(table, group)
        bias = jnp.concatenate([bias, bias], axis=1)
        for pair in pairs:
            lse = jnp.concatenate(
                [stats[group, pl.ds(2 * pair, 1), :], stats[group, pl.ds(2 * pair + 1, 1), :]], axis=1
            )
            query_t = triple[rows, columns(pair, 0)].T
            scores[slot][pair] = dot(triple[rows, columns(pair, 1)], block_diagonal(query_t)) + bias - lse
            up_t = upstream[rows, columns(pair, 0)].T
            probs_grads[slot][pair] = dot(triple[rows, columns(pair, 2)], block_diagonal(up_t))
            product = attended[rows, columns(pair, 0)].T.astype(F32) * up_t.astype(F32)
            agreements[slot][pair : pair + 1, :] = jnp.concatenate(
                [jnp.sum(product[:HD], axis=0, keepdims=True), jnp.sum(product[HD:], axis=0, keepdims=True)], axis=1
            )

    def second(group, slot):
        for pair in pairs:
            prob = jnp.exp(scores[slot][pair])
            probs[slot][pair] = prob.astype(BF16)
            agreement = agreements[slot][pair : pair + 1, :]
            scores_grads[slot][pair] = (prob * (probs_grads[slot][pair] - agreement)).astype(BF16)

    def stacked(pair_rows):
        zero = jnp.zeros_like(pair_rows)
        return jnp.concatenate([jnp.where(mask, pair_rows, zero) for mask in masks], axis=0)

    def third(group, slot):
        rows = group_rows(table, group)
        window, begin = rows.start, table[group, 1]
        for pair in pairs:
            scores_grad = scores_grads[slot][pair]
            value_grad = dot(probs[slot][pair], stacked(upstream[rows, columns(pair, 0)]))
            key_grad = dot(scores_grad, stacked(triple[rows, columns(pair, 0)]))
            key_t = block_diagonal(triple[rows, columns(pair, 1)].T)
            query_grad = dot(key_t, jnp.concatenate([scores_grad[:, :WIN], scores_grad[:, WIN:]], axis=0))
            keep_first(triple_grad, window, begin, columns(pair, 0), (query_grad * HD ** (-0.5)).T)
            keep_first(triple_grad, window, begin, columns(pair, 1), key_grad)
            keep_first(triple_grad, window, begin, columns(pair, 2), value_grad)

    pipelined(groups, first, second, third)


def interval(tile, first, end, size=TILE):
    row = lax.broadcasted_iota(jnp.int32, (size, 1), 0) + tile * size
    return jnp.logical_and(row >= first, row < end)


class Mover:
    def __init__(self, sems):
        self.sems = sems
        self.count = 0

    def start(self, source, target):
        copy = pltpu.make_async_copy(source, target, self.sems.at[self.count])
        self.count += 1
        copy.start()
        return copy


def project_rows(rows, gain1, shift1, w_in, b_in, target, spot, scaled_ref, scaled_spot):
    width = rows.shape[1]
    scaled, _inverse = normalize(rows)
    scaled_ref[scaled_spot, :] = scaled.astype(BF16)
    normed = (scaled * row_of(gain1) + row_of(shift1)).astype(BF16)
    q = dot(normed, w_in[:, :width]) + b_in[0:1, :]
    target[spot, :width] = (q.astype(BF16).astype(F32) * HD ** (-0.5)).astype(BF16)
    target[spot, width : 2 * width] = dot(normed, w_in[:, width : 2 * width]).astype(BF16)
    target[spot, 2 * width :] = (dot(normed, w_in[:, 2 * width :]) + b_in[1:2, :]).astype(BF16)


def kernel_own(
    place, seg, gain1, shift1, b_in, x_in, w_in_in,
    triple_out, attended_out, scaled_out, stats, table,
    x, w_in, triple, attended, work, ends, scores, peaks, raised, scales, sems, tile_sems,
):
    rows, width = x_in.shape
    move = Mover(sems)
    early = [move.start(w_in_in, w_in), move.start(x_in, x)]
    image_ends(seg, place[0] * rows, work)
    end_copy = move.start(work, ends)
    attended[...] = jnp.zeros_like(attended)
    spare = pl.ds(rows, triple.shape[0] - rows)
    triple[spare, :] = jnp.zeros((triple.shape[0] - rows, 3 * width), BF16)
    end_copy.wait()
    plan_groups(ends, place[0], rows, table)
    for copy in early:
        copy.wait()

    def step_copy(step):
        spot = pl.ds(pl.multiple_of(step * OWN, OWN), OWN)
        return pltpu.make_async_copy(triple.at[spot], triple_out.at[spot], tile_sems.at[step])

    def step_rows(step, _):
        spot = pl.ds(pl.multiple_of(step * OWN, OWN), OWN)
        project_rows(x[spot, :].astype(F32), gain1, shift1, w_in, b_in, triple, spot, x, spot)
        step_copy(step).start()
        return 0

    lax.fori_loop(0, rows // OWN, step_rows, 0)
    scaled_copy = move.start(x, scaled_out)
    attend_groups(jnp.maximum(table[GROUPS, 0] - 1, 1), table, triple, attended, stats, scores, peaks, raised, scales)
    leaving = move.start(attended, attended_out)
    scaled_copy.wait()
    for step in range(rows // OWN):
        step_copy(step).wait()
    leaving.wait()


def kernel_rest(
    place, table, gain1, shift1, b_in, b_out, gain2, shift2, b_ex,
    x_in, cot_in, halo_in, triple_in, attended_in, scaled_in, stats_in, w_in_in, w_out_in, w_ex_in, w_sh_in,
    middle_out, middle_grad_out, hidden_out, triple_grad_out, mine, other,
    x, back, w_in, w_out, w_ex, w_sh, triple, attended, middle, middle_grad, upstream, hidden, triple_grad, stats,
    d_ex, d_sh, d_out, product, sums, small, scores, peaks, raised, scales, probs_grads, probs, scores_grads,
    edge, sems, tile_sems,
):
    rows, width = x_in.shape
    total = x.shape[0]
    tiles = total // FEED
    normed2, normed_grad = upstream, middle_grad
    move = Mover(sems)
    own, over = pl.ds(0, rows), pl.ds(rows, HALO)
    early = [
        move.start(halo_in.at[:, pl.ds(0, width)], x.at[over]),
        move.start(w_in_in, w_in),
        move.start(stats_in, stats),
        move.start(triple_in, triple.at[own]),
        move.start(attended_in, attended),
    ]
    late = [
        move.start(w_out_in, w_out),
        move.start(x_in, x.at[own]),
        move.start(cot_in, back.at[own]),
        move.start(halo_in.at[:, pl.ds(width, width)], back.at[over]),
        move.start(w_ex_in, w_ex),
        move.start(w_sh_in, w_sh),
    ]
    rest = pl.ds(rows + HALO, total - rows - HALO)
    x[rest, :] = jnp.zeros((total - rows - HALO, width), BF16)
    back[rest, :] = jnp.zeros((total - rows - HALO, width), BF16)
    for ref in (d_ex, d_sh, d_out, product, sums, small, triple_grad):
        ref[...] = jnp.zeros_like(ref)
    groups, first, end = table[GROUPS, 0], table[GROUPS, 1], table[GROUPS, 2]
    for copy in early:
        copy.wait()
    tail = pl.ds(rows, TILE)
    project_rows(x[tail, :].astype(F32), gain1, shift1, w_in, b_in, triple, tail, edge, slice(None))
    attend_groups(groups, table, triple, attended, stats, scores, peaks, raised, scales, alone=groups - 1)
    for copy in late:
        copy.wait()
    leaving = []

    hidden_width = w_ex.shape[1]
    begins = list(range(0, hidden_width, CHUNK))

    def wide_rows(step):
        return pl.ds(pl.multiple_of(step * WIDE, WIDE), WIDE)

    def before_feed(step, _):
        spot = wide_rows(step)
        value = x[spot, :].astype(F32) + dot(attended[spot, :], w_out[...]) + row_of(b_out)
        scaled, _inverse = normalize(value)
        middle[spot, :] = value
        normed2[spot, :] = (scaled * row_of(gain2) + row_of(shift2)).astype(BF16)
        keep = interval(step, first, end, WIDE)
        back[spot, :] = jnp.where(keep, back[spot, :].astype(F32), 0.0).astype(BF16)
        return 0

    def feed(tile, _):
        spot = pl.ds(pl.multiple_of(tile * FEED, FEED), FEED)
        normed = normed2[spot, :]
        back_low = back[spot, :]
        back_half = (0.5 * back_low.astype(F32)).astype(BF16)

        def first_part(begin):
            cols = slice(begin, begin + CHUNK)
            before = dot(normed, w_ex[:, cols]) + b_ex[cols].reshape(1, -1)
            return before, dot_nt(back_half, w_sh[cols, :])

        held = [first_part(begins[0])]
        total_grad = jnp.zeros((FEED, width), F32)
        for index, begin in enumerate(begins):
            cols = slice(begin, begin + CHUNK)
            if index + 1 < len(begins):
                held.append(first_part(begins[index + 1]))
            value, grad = gelu_parts(*held[index])
            value, grad = value.astype(BF16), grad.astype(BF16)
            hidden[spot, cols] = value
            total_grad = total_grad + dot_nt(grad, w_ex[:, cols])
            d_sh[:, cols] += dot_tn(back_low, value)
            d_ex[:, cols] += dot_tn(normed, grad)
            small[4:5, cols] += jnp.sum(grad.astype(F32), axis=0, keepdims=True)
        normed_grad[spot, :] = total_grad
        pltpu.make_async_copy(hidden.at[spot], hidden_out.at[spot], tile_sems.at[0]).start()
        return 0

    def after_feed(step, _):
        spot = wide_rows(step)
        back32 = back[spot, :].astype(F32)
        scaled, inverse = normalize(middle[spot, :])
        upstream2 = normed_grad[spot, :]
        small[0:1, :width] += jnp.sum(back32, axis=0, keepdims=True)
        small[1:2, :width] += jnp.sum(upstream2 * scaled, axis=0, keepdims=True)
        small[2:3, :width] += jnp.sum(upstream2, axis=0, keepdims=True)
        grad = back32 + normalize_back(upstream2, scaled, inverse, row_of(gain2))
        small[3:4, :width] += jnp.sum(grad, axis=0, keepdims=True)
        middle_grad[spot, :] = grad
        grad_low = grad.astype(BF16)
        d_out[...] += dot_tn(attended[spot, :], grad_low)
        upstream[spot, :] = dot_nt(grad_low, w_out[...]).astype(BF16)
        pltpu.make_async_copy(middle_grad.at[spot], middle_grad_out.at[spot], tile_sems.at[1]).start()
        return 0

    lax.fori_loop(0, total // WIDE, before_feed, 0)
    scaled_copy = move.start(scaled_in, x.at[own])
    x[tail, :] = edge[...]
    leaving.append(move.start(middle, middle_out))
    lax.fori_loop(0, tiles, feed, 0)
    lax.fori_loop(0, total // WIDE, after_feed, 0)
    attend_back_groups(
        groups, table, triple, attended, upstream, stats, triple_grad, scores, peaks, probs_grads, probs, scores_grads,
    )
    leaving.append(move.start(triple_grad, triple_grad_out))
    scaled_copy.wait()
    ones = jnp.ones((16, WIDE), BF16)

    def multiply(step, _):
        spot = wide_rows(step)
        grad = triple_grad[spot, :]
        product[...] += dot_tn(x[spot, :], grad)
        sums[...] += dot(ones, grad)
        return 0

    lax.fori_loop(0, total // WIDE, multiply, 0)
    gain = jnp.broadcast_to(row_of(gain1), (LANES, width)).T
    shift = jnp.broadcast_to(row_of(shift1), (LANES, width)).T
    by_gain = jnp.zeros((width, LANES), F32)
    by_shift = jnp.zeros((width, LANES), F32)
    for begin in range(0, 3 * width, LANES):
        cols = slice(begin, begin + LANES)
        block, sum_row = product[:, cols], sums[0:1, cols]
        weight = w_in[:, cols].astype(F32)
        by_gain = by_gain + weight * block
        by_shift = by_shift + weight * sum_row
        product[:, cols] = gain * block + shift * sum_row
    small[5:6, : 3 * width] = sums[0:1, :]
    by_gain = jnp.broadcast_to(jnp.sum(by_gain, axis=1, keepdims=True), (width, LANES)).T
    by_shift = jnp.broadcast_to(jnp.sum(by_shift, axis=1, keepdims=True), (width, LANES)).T
    small[6:7, :width] = by_gain[0:1]
    small[7:8, :width] = by_shift[0:1]
    pack((d_ex, d_out, product), d_sh, small, place[2], mine, other)
    for copy in leaving:
        copy.wait()
    pltpu.make_async_copy(hidden, hidden_out, tile_sems.at[0]).wait()
    pltpu.make_async_copy(middle_grad, middle_grad_out, tile_sems.at[1]).wait()


def pack(grads, turned, small, core, mine, other):
    def fill(half, target):
        at = 0
        for grad in grads:
            count = grad.shape[0] // 2
            rows = pl.ds(pl.multiple_of(half * count, count), count)
            for begin in range(0, grad.shape[1], LANES):
                target[pl.ds(at, count), :] = grad[rows, begin : begin + LANES].astype(BF16)
                at += count
        count, columns = turned.shape[0], turned.shape[1] // 2
        for begin in range(0, columns, LANES):
            cols = pl.ds(pl.multiple_of(half * columns + begin, LANES), LANES)
            target[pl.ds(at, count), :] = turned[:, cols].astype(BF16)
            at += count
        return at

    fill(core, mine)
    at = fill(1 - core, other)
    rest = mine.shape[0] - at
    mine[pl.ds(at, rest), :] = jnp.zeros((rest, LANES), BF16)
    other[pl.ds(at, rest), :] = jnp.zeros((rest, LANES), BF16)
    for index in range(small.shape[1] // LANES):
        value = small[:, index * LANES : (index + 1) * LANES].astype(BF16)
        spot = pl.ds(at + (index // 2) * 16, 16)

        @pl.when(core == index % 2)
        def _():
            mine[spot, :] = value

        @pl.when(core != index % 2)
        def _():
            other[spot, :] = value


def step_copies(arrays, step, sems):
    spot = pl.ds(step * WIDE, WIDE)
    return [
        pltpu.make_async_copy(source.at[spot], target.at[spot], sems.at[step, at])
        for at, (source, target) in enumerate(arrays)
    ]


def leave(value_ref, own_out, halo_out, step, sems):
    rows = own_out.shape[0]
    begin, end = step * WIDE, (step + 1) * WIDE
    own = pl.ds(begin, min(rows, end) - begin)
    copies = [pltpu.make_async_copy(value_ref.at[own], own_out.at[own], sems.at[step, 6])]
    if end > rows:
        copies.append(pltpu.make_async_copy(value_ref.at[pl.ds(rows, end - rows)], halo_out, sems.at[step, 7]))
    for copy in copies:
        copy.start()
    return copies


def kernel_input(
    after, gain1, x_in, halo_in, w_in_in, triple_grad_in, middle_grad_in, out, out_halo,
    x, w_in, triple_grad, middle_grad, sems, step_sems,
):
    rows, width = x_in.shape
    total = x.shape[0]
    move = Mover(sems)
    early = [
        move.start(w_in_in, w_in),
        move.start(x_in, x.at[pl.ds(0, rows)]),
        move.start(halo_in.at[:, pl.ds(0, width)], x.at[pl.ds(rows, HALO)]),
    ]
    arrays = ((triple_grad_in, triple_grad), (middle_grad_in, middle_grad))
    steps = range(total // WIDE)
    parts = [step_copies(arrays, step, step_sems) for step in steps]
    for part in parts:
        for copy in part:
            copy.start()
    x[pl.ds(rows + HALO, total - rows - HALO), :] = jnp.zeros((total - rows - HALO, width), BF16)
    for copy in early:
        copy.wait()
    leaving = []
    for step in steps:
        for copy in parts[step]:
            copy.wait()
        spot = pl.ds(step * WIDE, WIDE)
        scaled, inverse = normalize(x[spot, :].astype(F32))
        normed_grad = dot_nt(triple_grad[spot, :], w_in[...])
        middle_grad[spot, :] = middle_grad[spot, :] + normalize_back(normed_grad, scaled, inverse, row_of(gain1))
        leaving += leave(middle_grad, out, out_halo, step, step_sems)
    for copy in leaving:
        copy.wait()


def kernel_result(
    after, table, b_sh, middle_in, hidden_in, w_sh_in, out, out_halo, middle, hidden, w_sh, value, sems, step_sems,
):
    total = middle.shape[0]
    move = Mover(sems)
    weight_copy = move.start(w_sh_in, w_sh)
    arrays = ((middle_in, middle), (hidden_in, hidden))
    steps = range(total // WIDE)
    parts = [step_copies(arrays, step, step_sems) for step in steps]
    for part in parts:
        for copy in part:
            copy.start()
    weight_copy.wait()
    leaving = []
    for step in steps:
        for copy in parts[step]:
            copy.wait()
        spot = pl.ds(step * WIDE, WIDE)
        keep = interval(step, table[GROUPS, 1], table[GROUPS, 2], WIDE)
        row = middle[spot, :] + row_of(b_sh) + dot(hidden[spot, :], w_sh[...])
        value[spot, :] = jnp.where(keep, row, 0.0).astype(BF16)
        leaving += leave(value, out, out_halo, step, step_sems)
    for copy in leaving:
        copy.wait()


def kernel_add(mine_in, other_in, out, mine, other, sems):
    chunks = sems.shape[0]
    size = mine.shape[0] // chunks

    def copies(chunk):
        spot = pl.ds(chunk * size, size)
        return [
            pltpu.make_async_copy(mine_in.at[spot], mine.at[spot], sems.at[chunk, 0]),
            pltpu.make_async_copy(other_in.at[spot], other.at[spot], sems.at[chunk, 1]),
            pltpu.make_async_copy(mine.at[spot], out.at[spot], sems.at[chunk, 2]),
        ]

    for chunk in range(chunks):
        for copy in copies(chunk)[:2]:
            copy.start()
    for chunk in range(chunks):
        spot = pl.ds(chunk * size, size)
        arriving = copies(chunk)
        for copy in arriving[:2]:
            copy.wait()
        mine[spot, :] = (mine[spot, :].astype(F32) + other[spot, :].astype(F32)).astype(BF16)
        arriving[2].start()
    for chunk in range(chunks):
        copies(chunk)[2].wait()


def kernel_sum(extra, *refs):
    parts_in, out, parts, piece, sems = refs[extra:]
    count = parts.shape[0]
    quarter = max(count // 4, 1)
    copies = []
    for index, begin in enumerate(range(0, count, quarter)):
        spot = pl.ds(begin, quarter)
        copies.append(pltpu.make_async_copy(parts_in.at[spot], parts.at[spot], sems.at[index]))
        copies[-1].start()
    total = jnp.zeros(piece.shape, F32)
    for index, copy in enumerate(copies):
        copy.wait()
        for part in range(index * quarter, (index + 1) * quarter):
            total = total + parts[part].astype(F32)
    piece[...] = total.astype(BF16)
    for part in range(count):
        pltpu.make_async_copy(piece, out.at[part], sems.at[4]).start()
    pltpu.make_async_copy(parts, out, sems.at[4]).wait()


def kernel_unpack_half(where, packed_in, d_ex, d_out, d_in, d_sh, packed, ex, out, inward, sh, sems):
    arrays = ((ex, d_ex), (out, d_out), (inward, d_in), (sh, d_sh))
    sizes = [value.shape[0] * value.shape[1] // LANES for value, _target in arrays]
    begins = [sum(sizes[:index]) for index in range(4)]
    arriving = []
    for index in range(4):
        spot = pl.ds(begins[index], sizes[index])
        arriving.append(pltpu.make_async_copy(packed_in.at[spot], packed.at[spot], sems.at[index]))
        arriving[-1].start()
    half = where[0]
    leaving = []
    for index, (value, target) in enumerate(arrays):
        arriving[index].wait()
        at = begins[index]
        if index < 3:
            count = value.shape[0]
            for begin in range(0, value.shape[1], LANES):
                value[:, begin : begin + LANES] = packed[pl.ds(at, count), :].astype(F32)
                at += count
        else:
            count = value.shape[1]
            for begin in range(0, value.shape[0], LANES):
                value[begin : begin + LANES, :] = packed[pl.ds(at, count), :].astype(F32).T
                at += count
        rows = pl.ds(pl.multiple_of(half * value.shape[0], value.shape[0]), value.shape[0])
        leaving.append(pltpu.make_async_copy(value, target.at[rows], sems.at[4 + index]))
        leaving[-1].start()
    return leaving


def kernel_first_half(where, packed_in, *refs):
    for copy in kernel_unpack_half(where, packed_in, *refs):
        copy.wait()


def kernel_second_half(
    where, packed_in, first_in, kept_ex, kept_out, kept_in, kept_sh,
    d_ex, d_out, d_in, d_sh, b_in, b_sh, gain2, shift2, b_out, b_ex, gain1, shift1,
    packed, ex, out, inward, sh, sems, mine, other, small_sems,
):
    del kept_ex, kept_out, kept_in, kept_sh
    rows = pl.ds(first_in.shape[0] - mine.shape[0], mine.shape[0])
    copies = [
        pltpu.make_async_copy(first_in.at[rows], mine, small_sems.at[0]),
        pltpu.make_async_copy(packed_in.at[rows], other, small_sems.at[1]),
    ]
    for copy in copies:
        copy.start()
    leaving = kernel_unpack_half(where, packed_in, d_ex, d_out, d_in, d_sh, packed, ex, out, inward, sh, sems)
    for copy in copies:
        copy.wait()
    width, columns = b_sh.shape[0], b_ex.shape[0]
    swap = where[0] == 0
    blocks = []
    for index in range(columns // LANES):
        spot = pl.ds(index // 2 * 16, 16)
        pair = mine[spot, :].astype(F32), other[spot, :].astype(F32)
        blocks.append(jnp.where(swap, pair[1 - index % 2], pair[index % 2]))
    small = jnp.concatenate(blocks, axis=1)
    for row, ref in ((0, b_sh), (1, gain2), (2, shift2), (3, b_out), (6, gain1), (7, shift1)):
        ref[...] = small[row, :width]
    b_ex[...] = small[4]
    b_in[0:1, :] = small[5:6, :width]
    b_in[1:2, :] = small[5:6, 2 * width : 3 * width]
    for copy in leaving:
        copy.wait()


def kernel_touch(*refs):
    del refs


VMEM = pl.BlockSpec(memory_space=pltpu.VMEM)
SMEM = pl.BlockSpec(memory_space=pltpu.SMEM)
ANY = pl.BlockSpec(memory_space=pl.ANY)


def params(mib):
    return pltpu.CompilerParams(vmem_limit_bytes=mib * 1024 * 1024)


def cost(flops, moved):
    return pl.CostEstimate(flops=int(flops), bytes_accessed=int(moved), transcendentals=0)


def shape(dims, dtype):
    return jax.ShapeDtypeStruct(dims, dtype)


def packed_rows(columns, small, pieces):
    half = columns // LANES * 192 + (small // LANES + 1) // 2 * 16
    return pieces * (-(-half // (8 * pieces)) * 8)


def attention_scratch(pairs):
    return [
        [pltpu.VMEM((pairs, WIN, 2 * WIN), F32)] * 2,
        [pltpu.VMEM((8, 2 * WIN), F32)] * 2,
        [pltpu.VMEM((pairs, 2 * WIN, WIN), BF16)] * 2,
        [pltpu.VMEM((8, 2 * WIN), F32)] * 2,
    ]


def own_part(place, segments, gain1, shift1, b_in, x, w_in):
    rows, width = x.shape
    total = rows + TILE
    vmem = pltpu.VMEM
    return pl.pallas_call(
        kernel_own,
        out_shape=(
            shape((rows, 3 * width), BF16),
            shape((total, width), BF16),
            shape((rows, width), BF16),
            shape((GROUPS, 8, WIN), F32),
            shape((GROUPS + 1, 8), jnp.int32),
        ),
        in_specs=[SMEM] + [VMEM] * 4 + [ANY] * 2,
        out_specs=(ANY, ANY, ANY, VMEM, SMEM),
        scratch_shapes=[
            vmem((rows, width), BF16),
            vmem(w_in.shape, BF16),
            vmem((total, 3 * width), BF16),
            vmem((total, width), BF16),
            vmem((8, LANES), jnp.int32),
            pltpu.SMEM((8, LANES), jnp.int32),
            *attention_scratch(width // (2 * HD)),
            pltpu.SemaphoreType.DMA((8,)),
            pltpu.SemaphoreType.DMA((rows // OWN,)),
        ],
        compiler_params=params(63),
        cost_estimate=cost(2 * 6 * rows * width * 3 * width, 1e7),
        name="own_part",
    )(place, segments, gain1, shift1, b_in, x, w_in)


def rest_part(place, table, vectors, x, cot, halo, triple, attended, scaled, stats, w_in, w_out, w_ex, w_sh, pieces):
    rows, width = x.shape
    total = rows + TILE
    hidden = w_ex.shape[1]
    packed = packed_rows(2 * hidden + 4 * width, hidden, pieces)
    vmem = pltpu.VMEM
    pairs = width // (2 * HD)
    square, row = vmem((pairs, WIN, 2 * WIN), F32), vmem((8, 2 * WIN), F32)
    low = vmem((pairs, WIN, 2 * WIN), BF16)
    return pl.pallas_call(
        kernel_rest,
        out_shape=(
            shape((total, width), F32),
            shape((total, width), F32),
            shape((total, hidden), BF16),
            shape((total, 3 * width), BF16),
            shape((packed, LANES), BF16),
            shape((packed, LANES), BF16),
        ),
        in_specs=[SMEM, SMEM] + [VMEM] * 7 + [ANY] * 11,
        out_specs=tuple([ANY] * 4 + [VMEM] * 2),
        scratch_shapes=[
            vmem((total, width), BF16),
            vmem((total, width), BF16),
            vmem(w_in.shape, BF16),
            vmem(w_out.shape, BF16),
            vmem(w_ex.shape, BF16),
            vmem(w_sh.shape, BF16),
            vmem((total, 3 * width), BF16),
            vmem((total, width), BF16),
            vmem((total, width), F32),
            vmem((total, width), F32),
            vmem((total, width), BF16),
            vmem((total, hidden), BF16),
            vmem((total, 3 * width), BF16),
            vmem((GROUPS, 8, WIN), F32),
            vmem((width, hidden), F32),
            vmem((width, hidden), F32),
            vmem((width, width), F32),
            vmem((width, 3 * width), F32),
            vmem((16, 3 * width), F32),
            vmem((16, hidden), F32),
            [square] * 2,
            [row] * 2,
            [vmem((pairs, 2 * WIN, WIN), BF16)],
            [row],
            [square] * 2,
            [low] * 2,
            [low] * 2,
            vmem((TILE, width), BF16),
            pltpu.SemaphoreType.DMA((16,)),
            pltpu.SemaphoreType.DMA((2,)),
        ],
        compiler_params=params(62),
        cost_estimate=cost(2 * 9 * rows * width * (3 * width + 8 * width), 3e7),
        name="rest_part",
    )(place, table, *vectors, x, cot, halo, triple, attended, scaled, stats, w_in, w_out, w_ex, w_sh)


def input_gradient(after, gain1, x, halo, w_in, triple_grad, middle_grad):
    rows, width = x.shape
    total = triple_grad.shape[0]
    vmem = pltpu.VMEM
    return pl.pallas_call(
        kernel_input,
        out_shape=(shape((rows, width), F32), shape((TILE, width), F32)),
        in_specs=[ANY, VMEM] + [ANY] * 5,
        out_specs=(ANY, ANY),
        scratch_shapes=[
            vmem((total, width), BF16),
            vmem(w_in.shape, BF16),
            vmem((total, 3 * width), BF16),
            vmem((total, width), F32),
            pltpu.SemaphoreType.DMA((4,)),
            pltpu.SemaphoreType.DMA((total // WIDE, 8)),
        ],
        compiler_params=params(63),
        cost_estimate=cost(2 * rows * width * 9 * width, 1.4e7),
        name="input_gradient",
    )(after, gain1, x, halo, w_in, triple_grad, middle_grad)


def layer_result(after, table, b_sh, middle, hidden, w_sh):
    total, width = middle.shape
    vmem = pltpu.VMEM
    return pl.pallas_call(
        kernel_result,
        out_shape=(shape((total - TILE, width), BF16), shape((TILE, width), BF16)),
        in_specs=[ANY, SMEM, VMEM] + [ANY] * 3,
        out_specs=(ANY, ANY),
        scratch_shapes=[
            vmem(middle.shape, F32),
            vmem(hidden.shape, BF16),
            vmem(w_sh.shape, BF16),
            vmem(middle.shape, BF16),
            pltpu.SemaphoreType.DMA((2,)),
            pltpu.SemaphoreType.DMA((total // WIDE, 8)),
        ],
        compiler_params=params(63),
        cost_estimate=cost(2 * total * width * 8 * width, 1.3e7),
        name="layer_result",
    )(after, table, b_sh, middle, hidden, w_sh)


def add_halves(mine, other):
    return pl.pallas_call(
        kernel_add,
        out_shape=shape(mine.shape, BF16),
        in_specs=[ANY, ANY],
        out_specs=ANY,
        scratch_shapes=[
            pltpu.VMEM(mine.shape, BF16), pltpu.VMEM(mine.shape, BF16), pltpu.SemaphoreType.DMA((4, 3)),
        ],
        compiler_params=params(63),
        cost_estimate=cost(mine.size, mine.size * 6),
        name="add_halves",
    )(mine, other)


def sum_parts(after, parts):
    return pl.pallas_call(
        partial(kernel_sum, len(after)),
        out_shape=shape(parts.shape, BF16),
        in_specs=[ANY] * (len(after) + 1),
        out_specs=ANY,
        scratch_shapes=[
            pltpu.VMEM(parts.shape, BF16),
            pltpu.VMEM(parts.shape[1:], BF16),
            pltpu.SemaphoreType.DMA((5,)),
        ],
        compiler_params=params(63),
        cost_estimate=cost(parts.size, parts.size * 4),
        name="sum_parts",
    )(*after, parts)


def half_shapes(width, hidden):
    dims = ((width, hidden), (width, width), (width, 3 * width), (hidden, width))
    scratch = [pltpu.VMEM((rows // 2, columns), F32) for rows, columns in dims]
    return tuple(shape(dim, F32) for dim in dims), [*scratch, pltpu.SemaphoreType.DMA((8,))]


def unpack_first(half, packed, width, hidden):
    shapes, scratch = half_shapes(width, hidden)
    return pl.pallas_call(
        kernel_first_half,
        out_shape=shapes,
        in_specs=[SMEM, ANY],
        out_specs=(ANY,) * 4,
        scratch_shapes=[pltpu.VMEM(packed.shape, BF16), *scratch],
        compiler_params=params(63),
        cost_estimate=cost(packed.size, packed.size * 6),
        name="unpack_first",
    )(half, packed)


def unpack_second(half, packed, first, kept, used, width, hidden):
    shapes, scratch = half_shapes(width, hidden)
    rows = first.shape[0] - used
    small = tuple(shape(dims, F32) for dims in ((2, width),) + ((width,),) * 4 + ((hidden,), (width,), (width,)))
    return pl.pallas_call(
        kernel_second_half,
        out_shape=shapes + small,
        in_specs=[SMEM] + [ANY] * 6,
        out_specs=(ANY,) * 4 + (VMEM,) * 8,
        scratch_shapes=[
            pltpu.VMEM(packed.shape, BF16), *scratch, pltpu.VMEM((rows, LANES), BF16), pltpu.VMEM((rows, LANES), BF16),
            pltpu.SemaphoreType.DMA((2,)),
        ],
        input_output_aliases={3: 0, 4: 1, 5: 2, 6: 3},
        compiler_params=params(63),
        cost_estimate=cost(packed.size, packed.size * 6),
        name="unpack_second",
    )(half, packed, first, *kept)


def touch(value, *after):
    return pl.pallas_call(
        kernel_touch,
        out_shape=shape(value.shape, value.dtype),
        in_specs=[ANY] * (1 + len(after)),
        out_specs=ANY,
        input_output_aliases={0: 0},
        name="touch",
    )(value, *after)


def same_core_groups():
    packs, parts = lax.axis_size("dp"), lax.axis_size("mp")
    return [[d * parts + m for d in range(c, packs, 2) for m in range(parts)] for c in range(2)]


def swap_cores(block):
    packs = lax.axis_size("dp")
    return lax.ppermute(block, "dp", [(i, i ^ 1) for i in range(packs)])


def exchange(parts):
    return lax.all_to_all(parts, ("dp", "mp"), 0, 0, axis_index_groups=same_core_groups())


def passed(block, distance):
    count = lax.axis_size("mp")
    route = [(i, i + distance) for i in range(count) if 0 <= i + distance < count]
    return lax.ppermute(block, "mp", route)


def take_over(own, other, first):
    row = lax.broadcasted_iota(jnp.int32, (HALO, 1), 0)
    return lax.dynamic_update_slice(own, jnp.where(row < first, other, own[:HALO]), (0, 0))


def body(
    layer_input, segments, cotangent, first_gain, first_shift, inward_weight, inward_bias, outward_weight,
    outward_bias, second_gain, second_shift, expand_weight, expand_bias, shrink_weight, shrink_bias,
):
    rows, width = layer_input.shape
    hidden_width = expand_weight.shape[1]
    position = lax.axis_index("mp")
    core = lax.axis_index("dp") % 2
    pieces = lax.axis_size("dp") * lax.axis_size("mp") // 2
    place = jnp.stack([position, position, core]).astype(jnp.int32)
    gain1, shift1, b_out, gain2, shift2, b_ex, b_sh = (
        first_gain, first_shift, outward_bias, second_gain, second_shift, expand_bias, shrink_bias
    )
    halo = passed(jnp.concatenate([layer_input[:HALO], cotangent[:HALO]], axis=1), -1)
    triple, attended, scaled, stats, table = own_part(
        place, segments, gain1, shift1, inward_bias, layer_input, inward_weight
    )
    middle, middle_grad, hidden, triple_grad, mine, other = rest_part(
        place, table, (gain1, shift1, inward_bias, b_out, gain2, shift2, b_ex), layer_input, cotangent, halo, triple,
        attended, scaled, stats, inward_weight, outward_weight, expand_weight, shrink_weight, pieces,
    )
    both = add_halves(mine, swap_cores(other))
    parts = exchange(both.reshape(pieces, -1, LANES))
    input_grad, input_halo = input_gradient(both, gain1, layer_input, halo, inward_weight, triple_grad, middle_grad)
    result, result_halo = layer_result(input_halo, table, b_sh, middle, hidden, shrink_weight)
    summed = sum_parts((input_halo, result_halo), parts)
    mine = exchange(summed).reshape(-1, LANES)
    first = table[GROUPS, 1]
    input_grad = take_over(input_grad, passed(touch(input_halo, summed)[:HALO], 1), first)
    result = take_over(result, passed(touch(result_halo, summed)[:HALO], 1), first)
    mine = touch(mine, input_grad, result)
    other = swap_cores(mine)
    used = 192 * (2 * hidden_width + 4 * width) // LANES
    half = unpack_first(place[2:], mine, width, hidden_width)
    d_ex, d_out, d_in, d_sh, d_b_in, d_b_sh, d_gain2, d_shift2, d_b_out, d_b_ex, d_gain1, d_shift1 = unpack_second(
        1 - place[2:], other, mine, half, used, width, hidden_width
    )
    return (
        result, input_grad, d_gain1, d_shift1, d_in, d_b_in, d_out, d_b_out, d_gain2, d_shift2, d_ex, d_b_ex, d_sh,
        d_b_sh,
    )


def solution(mesh):
    rows = P(("dp", "mp"), None)
    in_specs = (rows, P("dp", None), rows) + (P(),) * 12
    out_specs = (rows, rows) + (P(),) * 12
    return jax.shard_map(body, mesh=mesh, in_specs=in_specs, out_specs=out_specs, check_vma=False)
```

```python
from functools import partial

import jax
import jax.numpy as jnp
from jax import lax
from jax.experimental import pallas as pl
from jax.experimental.pallas import tpu as pltpu
from jax.sharding import PartitionSpec as P

HD = 64
SEQ = 198
EPSILON = 1e-06
MASKED = -1000000000.0
LOG2E = 1.4426950408889634
WIN = 256
TILE = 256
HALO = 208
WIDE = 768
OWN = 1024
GROUPS = 24
LANES = 128
CHUNK = 256
FEED = 768
BIG = 1 << 20
F32 = jnp.float32
BF16 = jnp.bfloat16
NT = (((1,), (1,)), ((), ()))
TN = (((0,), (0,)), ((), ()))


def row_of(ref):
    return ref[...].reshape(1, -1)


def dot(a, b):
    return jnp.dot(a, b, preferred_element_type=F32)


def dot_nt(a, b):
    return lax.dot_general(a, b, NT, preferred_element_type=F32)


def dot_tn(a, b):
    return lax.dot_general(a, b, TN, preferred_element_type=F32)


def normalize(rows):
    center = jnp.mean(rows, axis=-1, keepdims=True)
    centred = rows - center
    spread = jnp.mean(centred * centred, axis=-1, keepdims=True)
    inverse = lax.rsqrt(spread + EPSILON)
    return centred * inverse, inverse


def normalize_back(upstream, scaled, inverse, gain):
    direct = upstream * gain
    first = jnp.mean(direct, axis=-1, keepdims=True)
    second = jnp.mean(direct * scaled, axis=-1, keepdims=True)
    return inverse * (direct - first - scaled * second)


def gelu_parts(v, half_upstream):
    scaled = v * 0.7071067811865476
    double = 1.0 + lax.erf(scaled)
    bell = jnp.exp2((scaled * scaled) * -1.4426950408889634)
    return (0.5 * v) * double, half_upstream * (double + (v * 0.7978845608028654) * bell)


def image_ends(seg, base, work):
    ident = lax.broadcasted_iota(jnp.int32, (LANES, LANES), 0)
    below = jnp.zeros((LANES, LANES), F32)
    for begin in range(0, seg.shape[1], LANES):
        row = seg[0:1, begin : begin + LANES]
        row = jnp.where(row < 0, BIG, row)
        below = below + jnp.where(row <= ident, 1.0, 0.0)
    ends = jnp.broadcast_to(jnp.sum(below, axis=1, keepdims=True), (LANES, LANES))
    started = jnp.sum(jnp.where(ends < base.astype(F32), 1.0, 0.0), axis=0, keepdims=True)
    work[0:1, :] = ends.T[0:1].astype(jnp.int32)
    work[1:2, :] = started.astype(jnp.int32)


def plan_groups(ends, position, rows, table):
    base = position * rows
    limit = jnp.minimum(base + rows, ends[0, LANES - 1]) - base
    image = jnp.where(position == 0, 0, ends[1, 0] + 1)
    first = jnp.where(position == 0, 0, ends[0, jnp.maximum(image - 1, 0)]) - base

    def body(state):
        at, image, group, window, start, c1, c2 = state
        after = ends[0, jnp.minimum(image, LANES - 1)] - base
        fits = after - window <= WIN

        @pl.when(jnp.logical_not(fits))
        def _():
            write_group(table, group, window, start, c1, c2, at)

        group = jnp.where(fits, group, group + 1)
        new_c1 = jnp.where(fits, jnp.where(at == start, c1, jnp.where(c1 < 0, at, c1)), -1)
        new_c2 = jnp.where(fits, jnp.where(jnp.logical_and(at != start, c1 >= 0), jnp.where(c2 < 0, at, c2), c2), -1)
        start = jnp.where(fits, start, at)
        window = jnp.where(fits, window, (at // 16) * 16)
        return after, image + 1, group, window, start, new_c1, new_c2

    init = (first, image, jnp.int32(0), (first // 16) * 16, first, jnp.int32(-1), jnp.int32(-1))
    at, image, group, window, start, c1, c2 = lax.while_loop(lambda s: s[0] < limit, body, init)
    write_group(table, group, window, start, c1, c2, at)
    table[GROUPS, 0] = group + 1
    table[GROUPS, 1] = first
    table[GROUPS, 2] = at


def write_group(table, group, window, start, c1, c2, end):
    table[group, 0] = window
    table[group, 1] = start - window
    table[group, 2] = jnp.where(c1 < 0, end, c1) - window
    table[group, 3] = jnp.where(c2 < 0, end, c2) - window
    table[group, 4] = end - window


def group_bias(table, group):
    bounds = [table[group, i] for i in range(1, 5)]
    row = lax.broadcasted_iota(jnp.int32, (WIN, LANES), 0)
    col = lax.broadcasted_iota(jnp.int32, (1, WIN), 1)

    def ident(index):
        return sum((index >= b).astype(jnp.int32) for b in bounds)

    row, col = ident(row), ident(col)
    return jnp.concatenate(
        [jnp.where(row == col[:, at : at + LANES], 0.0, MASKED) for at in range(0, WIN, LANES)], axis=1
    )


def group_mask_factors(table, group):
    bounds = [table[group, i] for i in range(1, 5)]

    def ident(index):
        return sum((index >= b).astype(jnp.int32) for b in bounds)

    row = ident(lax.broadcasted_iota(jnp.int32, (WIN, LANES), 0))
    left = jnp.where(row == lax.broadcasted_iota(jnp.int32, (WIN, LANES), 1), 1.0, 0.0).astype(BF16)
    col = ident(lax.broadcasted_iota(jnp.int32, (1, WIN), 1))
    kind = lax.broadcasted_iota(jnp.int32, (16, WIN), 0)
    right = jnp.where(kind == col, 0.0, MASKED).astype(BF16)
    right = jnp.concatenate([right, jnp.zeros((LANES - 16, WIN), BF16)], axis=0)
    return left, jnp.concatenate([right, right], axis=1)


def head_masks():
    lane = lax.broadcasted_iota(jnp.int32, (WIN, 2 * HD), 1)
    return lane < HD, lane >= HD


def keep_first(ref, window, begin, cols, value):
    head = pl.ds(window, 16)
    old = ref[head, cols]
    row = lax.broadcasted_iota(jnp.int32, (16, 2 * HD), 0)
    ref[head, cols] = jnp.where(row >= begin, value[:16].astype(F32), old.astype(F32)).astype(BF16)
    ref[pl.ds(window + 16, WIN - 16), cols] = value[16:].astype(BF16)


def block_diagonal(pair_t):
    zero = jnp.zeros((HD, pair_t.shape[1]), pair_t.dtype)
    return jnp.concatenate(
        [jnp.concatenate([pair_t[:HD], zero], axis=1), jnp.concatenate([zero, pair_t[HD:]], axis=1)], axis=0
    )


def pipelined(groups, first, second, third, arrive=lambda group, have: have):
    def clamped(group):
        return jnp.minimum(group, groups - 1)

    def half(group, slot):
        first(clamped(group), slot)
        second(clamped(group - 1), 1 - slot)
        third(clamped(group - 2), slot)

    have = arrive(clamped(1), jnp.int32(0))
    first(0, 0)
    first(clamped(1), 1)
    second(0, 0)

    def both(step, have):
        have = arrive(clamped(2 * step + 3), have)
        half(2 * step + 2, 0)
        half(2 * step + 3, 1)
        return have

    have = lax.fori_loop(0, (groups + 1) // 2, both, have)
    arrive(None, have)


def group_rows(table, group, shifted=0):
    return pl.ds(pl.multiple_of(table[group, 0] - shifted, 16), WIN)


def attend_groups(groups, table, triple, attended, stats, scores, peaks, raised, scales, alone=None, shifted=0):
    width = attended.shape[1]
    pairs = range(width // (2 * HD))

    def first(group, slot):
        rows = group_rows(table, group, shifted)
        left, right = group_mask_factors(table, group)
        for pair in pairs:
            query_t = triple[rows, pl.ds(pair * 2 * HD, 2 * HD)].T
            key = triple[rows, pl.ds(width + pair * 2 * HD, 2 * HD)]
            value = dot(
                jnp.concatenate([key, left], axis=1), jnp.concatenate([block_diagonal(query_t), right], axis=0)
            )
            scores[slot][pair] = value
            peaks[slot][pair : pair + 1, :] = jnp.max(value, axis=0, keepdims=True)

    def second(group, slot):
        for pair in pairs:
            peak = peaks[slot][pair : pair + 1, :]
            value = jnp.exp2(scores[slot][pair] - peak)
            total = jnp.sum(value, axis=0, keepdims=True)
            raised[slot][pair, :WIN] = value[:, :WIN].astype(BF16)
            raised[slot][pair, WIN:] = value[:, WIN:].astype(BF16)
            scales[slot][pair : pair + 1, :] = 1.0 / total
            lse = peak + LOG2E * jnp.log(total)
            stats[group, pl.ds(2 * pair, 1), :] = lse[:, :WIN]
            stats[group, pl.ds(2 * pair + 1, 1), :] = lse[:, WIN:]

    def third(group, slot):
        rows = group_rows(table, group, shifted)
        for pair in pairs:
            value_t = block_diagonal(triple[rows, pl.ds(2 * width + pair * 2 * HD, 2 * HD)].T)
            out = dot(value_t, raised[slot][pair])
            scale = scales[slot][pair : pair + 1, :]
            out = jnp.concatenate([out[:HD] * scale[:, :WIN], out[HD:] * scale[:, WIN:]], axis=0)
            keep_first(attended, group_rows(table, group).start, table[group, 1], pl.ds(pair * 2 * HD, 2 * HD), out.T)

    if alone is None:
        pipelined(groups, first, second, third)
    else:
        for part in (first, second, third):
            part(alone, 0)


def attend_back_groups(groups, table, triple, attended, upstream, stats, triple_grad, probs, scores_grads):
    width = attended.shape[1]
    pairs = range(width // (2 * HD))
    masks = head_masks()

    def columns(pair, block):
        return pl.ds(block * width + pair * 2 * HD, 2 * HD)

    def first(group, slot):
        rows = group_rows(table, group)
        bias = group_bias(table, group)
        bias = jnp.concatenate([bias, bias], axis=1)
        for pair in pairs:
            lse = jnp.concatenate(
                [stats[group, pl.ds(2 * pair, 1), :], stats[group, pl.ds(2 * pair + 1, 1), :]], axis=1
            )
            query_t = triple[rows, columns(pair, 0)].T
            up_t = upstream[rows, columns(pair, 0)].T
            product = attended[rows, columns(pair, 0)].T.astype(F32) * up_t.astype(F32)
            agreement = jnp.concatenate(
                [jnp.sum(product[:HD], axis=0, keepdims=True), jnp.sum(product[HD:], axis=0, keepdims=True)], axis=1
            )
            scores = dot(triple[rows, columns(pair, 1)], block_diagonal(query_t))
            probs_grad = dot(triple[rows, columns(pair, 2)], block_diagonal(up_t))
            prob = jnp.exp2(scores + bias - lse)
            probs[slot][pair] = prob.astype(BF16)
            scores_grads[slot][pair] = (prob * (probs_grad - agreement)).astype(BF16)

    def stacked(pair_rows):
        zero = jnp.zeros_like(pair_rows)
        return jnp.concatenate([jnp.where(mask, pair_rows, zero) for mask in masks], axis=0)

    def second(group, slot):
        rows = group_rows(table, group)
        window, begin = rows.start, table[group, 1]
        for pair in pairs:
            scores_grad = scores_grads[slot][pair]
            value_grad = dot(probs[slot][pair], stacked(upstream[rows, columns(pair, 0)]))
            key_grad = dot(scores_grad, stacked(triple[rows, columns(pair, 0)]))
            key_t = block_diagonal(triple[rows, columns(pair, 1)].T)
            query_grad = dot(key_t, jnp.concatenate([scores_grad[:, :WIN], scores_grad[:, WIN:]], axis=0))
            keep_first(triple_grad, window, begin, columns(pair, 0), (query_grad * HD ** (-0.5)).T)
            keep_first(triple_grad, window, begin, columns(pair, 1), key_grad * (1.0 / LOG2E))
            keep_first(triple_grad, window, begin, columns(pair, 2), value_grad)

    def clamped(group):
        return jnp.minimum(group, groups - 1)

    def half(group, slot):
        first(clamped(group), slot)
        second(clamped(group - 1), 1 - slot)

    first(0, 0)

    def both(step, _):
        half(2 * step + 1, 1)
        half(2 * step + 2, 0)
        return 0

    lax.fori_loop(0, (groups + 1) // 2, both, 0)


def interval(tile, first, end, size=TILE):
    row = lax.broadcasted_iota(jnp.int32, (size, 1), 0) + tile * size
    return jnp.logical_and(row >= first, row < end)


class Mover:
    def __init__(self, sems):
        self.sems = sems
        self.count = 0

    def start(self, source, target):
        copy = pltpu.make_async_copy(source, target, self.sems.at[self.count])
        self.count += 1
        copy.start()
        return copy


def project_rows(rows, gain1, shift1, w_in, b_in, target, spot, scaled_ref, scaled_spot):
    width = rows.shape[1]
    scaled, _inverse = normalize(rows)
    scaled_ref[scaled_spot, :] = scaled.astype(BF16)
    normed = (scaled * row_of(gain1) + row_of(shift1)).astype(BF16)
    q = dot(normed, w_in[:, :width]) + b_in[0:1, :]
    target[spot, :width] = (q.astype(BF16).astype(F32) * (HD ** (-0.5) * LOG2E)).astype(BF16)
    target[spot, width : 2 * width] = dot(normed, w_in[:, width : 2 * width]).astype(BF16)
    target[spot, 2 * width :] = (dot(normed, w_in[:, 2 * width :]) + b_in[1:2, :]).astype(BF16)


def kernel_own(
    place, seg_in, gain1_in, shift1_in, b_in_in, x_in, w_in_in,
    triple_out, attended_out, scaled_out, stats, table,
    seg, gain1, shift1, b_in, x, w_in, triple, attended, work, ends, scores, peaks, raised, scales, sems, tile_sems,
):
    rows, width = x_in.shape
    move = Mover(sems)
    seg_copy = move.start(seg_in, seg)
    early = [
        move.start(gain1_in, gain1), move.start(shift1_in, shift1), move.start(b_in_in, b_in),
        move.start(x_in, x), move.start(w_in_in, w_in),
    ]
    seg_copy.wait()
    image_ends(seg, place[0] * rows, work)
    end_copy = move.start(work, ends)
    attended[...] = jnp.zeros_like(attended)
    spare = pl.ds(rows, triple.shape[0] - rows)
    triple[spare, :] = jnp.zeros((triple.shape[0] - rows, 3 * width), BF16)
    end_copy.wait()
    plan_groups(ends, place[0], rows, table)
    for copy in early:
        copy.wait()

    def step_copy(step):
        spot = pl.ds(pl.multiple_of(step * OWN, OWN), OWN)
        return pltpu.make_async_copy(triple.at[spot], triple_out.at[spot], tile_sems.at[step])

    def step_rows(step, _):
        spot = pl.ds(pl.multiple_of(step * OWN, OWN), OWN)
        project_rows(x[spot, :].astype(F32), gain1, shift1, w_in, b_in, triple, spot, x, spot)
        step_copy(step).start()
        return 0

    lax.fori_loop(0, rows // OWN, step_rows, 0)
    scaled_copy = move.start(x, scaled_out)
    attend_groups(jnp.maximum(table[GROUPS, 0] - 1, 1), table, triple, attended, stats, scores, peaks, raised, scales)
    leaving = move.start(attended, attended_out)
    scaled_copy.wait()
    for step in range(rows // OWN):
        step_copy(step).wait()
    leaving.wait()


def kernel_rest(
    place, table, *refs
):
    vectors_in, refs = refs[:7], refs[7:]
    vectors, refs = refs[-7:], refs[:-7]
    rest_body(place, table, vectors_in, vectors, *refs)


def rest_body(
    place, table, vectors_in, vectors,
    x_in, cot_in, halo_in, triple_in, attended_in, scaled_in, stats_in, w_in_in, w_out_in, w_ex_in, w_sh_in,
    middle_out, middle_grad_out, hidden_out, triple_grad_out, mine_out, other_out,
    x, back, w_in, w_out, w_ex, w_sh, triple, attended, middle, middle_grad, upstream, hidden, triple_grad, stats,
    d_ex, d_sh, d_out, product, sums, small, scores, peaks, raised, scales, probs, scores_grads,
    edge, mine, other, sems, tile_sems,
):
    rows, width = x_in.shape
    total = x.shape[0]
    tiles = total // FEED
    normed2, normed_grad = upstream, middle_grad
    move = Mover(sems)
    own, over = pl.ds(0, rows), pl.ds(rows, HALO)
    gain1, shift1, b_in, b_out, gain2, shift2, b_ex = vectors
    vector_copies = [move.start(source, target) for source, target in zip(vectors_in, vectors)]
    near, far = pl.ds(2 * WIDE, rows - 2 * WIDE), pl.ds(0, 2 * WIDE)
    early = [
        move.start(halo_in.at[:, pl.ds(0, width)], x.at[over]),
        move.start(w_in_in, w_in),
        move.start(triple_in.at[near], triple.at[near]),
        move.start(stats_in, stats),
        move.start(attended_in, attended),
    ] + vector_copies
    late = [
        move.start(w_out_in, w_out),
        move.start(x_in, x.at[own]),
        move.start(cot_in, back.at[own]),
        move.start(halo_in.at[:, pl.ds(width, width)], back.at[over]),
        move.start(w_ex_in, w_ex),
        move.start(w_sh_in, w_sh),
    ]
    last = move.start(triple_in.at[far], triple.at[far])
    rest = pl.ds(rows + HALO, total - rows - HALO)
    x[rest, :] = jnp.zeros((total - rows - HALO, width), BF16)
    back[rest, :] = jnp.zeros((total - rows - HALO, width), BF16)
    for ref in (d_ex, d_sh, d_out, product, sums, small, triple_grad):
        ref[...] = jnp.zeros_like(ref)
    groups, first, end = table[GROUPS, 0], table[GROUPS, 1], table[GROUPS, 2]
    for copy in early:
        copy.wait()
    tail = pl.ds(rows, TILE)
    project_rows(x[tail, :].astype(F32), gain1, shift1, w_in, b_in, triple, tail, edge, slice(None))
    attend_groups(groups, table, triple, attended, stats, scores, peaks, raised, scales, alone=groups - 1)
    for copy in late:
        copy.wait()
    leaving = []

    hidden_width = w_ex.shape[1]
    begins = list(range(0, hidden_width, CHUNK))

    def wide_rows(step):
        return pl.ds(pl.multiple_of(step * WIDE, WIDE), WIDE)

    def before_feed(step, _):
        spot = wide_rows(step)
        value = x[spot, :].astype(F32) + dot(attended[spot, :], w_out[...]) + row_of(b_out)
        scaled, _inverse = normalize(value)
        middle[spot, :] = value
        normed2[spot, :] = (scaled * row_of(gain2) + row_of(shift2)).astype(BF16)
        keep = interval(step, first, end, WIDE)
        back[spot, :] = jnp.where(keep, back[spot, :].astype(F32), 0.0).astype(BF16)
        return 0

    def feed(tile, _):
        spot = pl.ds(pl.multiple_of(tile * FEED, FEED), FEED)
        normed = normed2[spot, :]
        back_low = back[spot, :]
        back_half = (0.5 * back_low.astype(F32)).astype(BF16)

        def first_part(begin):
            cols = slice(begin, begin + CHUNK)
            before = dot(normed, w_ex[:, cols]) + b_ex[cols].reshape(1, -1)
            return before, dot_nt(back_half, w_sh[cols, :])

        held = [first_part(begins[0])]
        total_grad = jnp.zeros((width, FEED), F32)
        for index, begin in enumerate(begins):
            cols = slice(begin, begin + CHUNK)
            if index + 1 < len(begins):
                held.append(first_part(begins[index + 1]))
            value, grad = gelu_parts(*held[index])
            value, grad = value.astype(BF16), grad.astype(BF16)
            hidden[spot, cols] = value
            total_grad = total_grad + dot_nt(w_ex[:, cols], grad)
            d_sh[:, cols] += dot_tn(back_low, value)
            d_ex[:, cols] += dot_tn(normed, grad)
            small[4:5, cols] += jnp.sum(grad.astype(F32), axis=0, keepdims=True)
        normed_grad[spot, :] = total_grad.T
        pltpu.make_async_copy(hidden.at[spot], hidden_out.at[spot], tile_sems.at[0]).start()
        return 0

    def after_feed(step, _):
        spot = wide_rows(step)
        back32 = back[spot, :].astype(F32)
        scaled, inverse = normalize(middle[spot, :])
        upstream2 = normed_grad[spot, :]
        small[0:1, :width] += jnp.sum(back32, axis=0, keepdims=True)
        small[1:2, :width] += jnp.sum(upstream2 * scaled, axis=0, keepdims=True)
        small[2:3, :width] += jnp.sum(upstream2, axis=0, keepdims=True)
        grad = back32 + normalize_back(upstream2, scaled, inverse, row_of(gain2))
        small[3:4, :width] += jnp.sum(grad, axis=0, keepdims=True)
        middle_grad[spot, :] = grad
        grad_low = grad.astype(BF16)
        d_out[...] += dot_tn(attended[spot, :], grad_low)
        upstream[spot, :] = dot_nt(grad_low, w_out[...]).astype(BF16)
        pltpu.make_async_copy(middle_grad.at[spot], middle_grad_out.at[spot], tile_sems.at[1]).start()
        return 0

    lax.fori_loop(0, total // WIDE, before_feed, 0)
    scaled_copy = move.start(scaled_in, x.at[own])
    x[tail, :] = edge[...]
    leaving.append(move.start(middle, middle_out))
    lax.fori_loop(0, tiles, feed, 0)
    lax.fori_loop(0, total // WIDE, after_feed, 0)
    core = place[2]
    for half, target in ((core, mine), (1 - core, other)):
        at = pack((d_out,), half, target, pack_turned(d_sh, half, target, pack((d_ex,), half, target, 0)))
    ready = pl.ds(0, at)
    leaving += [move.start(mine.at[ready], mine_out.at[ready]), move.start(other.at[ready], other_out.at[ready])]
    last.wait()
    attend_back_groups(
        groups, table, triple, attended, upstream, stats, triple_grad, probs, scores_grads
    )
    leaving.append(move.start(triple_grad, triple_grad_out))
    scaled_copy.wait()
    ones = jnp.ones((16, WIDE), BF16)

    def multiply(step, _):
        spot = wide_rows(step)
        grad = triple_grad[spot, :]
        product[...] += dot_tn(x[spot, :], grad)
        sums[...] += dot(ones, grad)
        return 0

    lax.fori_loop(0, total // WIDE, multiply, 0)
    gain = jnp.broadcast_to(row_of(gain1), (LANES, width)).T
    shift = jnp.broadcast_to(row_of(shift1), (LANES, width)).T
    by_gain = jnp.zeros((width, LANES), F32)
    by_shift = jnp.zeros((width, LANES), F32)
    for begin in range(0, 3 * width, LANES):
        cols = slice(begin, begin + LANES)
        block, sum_row = product[:, cols], sums[0:1, cols]
        weight = w_in[:, cols].astype(F32)
        by_gain = by_gain + weight * block
        by_shift = by_shift + weight * sum_row
        product[:, cols] = gain * block + shift * sum_row
    small[5:6, : 3 * width] = sums[0:1, :]
    by_gain = jnp.broadcast_to(jnp.sum(by_gain, axis=1, keepdims=True), (width, LANES)).T
    by_shift = jnp.broadcast_to(jnp.sum(by_shift, axis=1, keepdims=True), (width, LANES)).T
    small[6:7, :width] = by_gain[0:1]
    small[7:8, :width] = by_shift[0:1]
    begin = at
    for half, target in ((core, mine), (1 - core, other)):
        at = pack((product,), half, target, begin)
    pack_small(small, core, mine, other, at)
    ready = pl.ds(begin, mine.shape[0] - begin)
    leaving += [move.start(mine.at[ready], mine_out.at[ready]), move.start(other.at[ready], other_out.at[ready])]
    for copy in leaving:
        copy.wait()
    pltpu.make_async_copy(hidden, hidden_out, tile_sems.at[0]).wait()
    pltpu.make_async_copy(middle_grad, middle_grad_out, tile_sems.at[1]).wait()


def pack(grads, half, target, at):
    for grad in grads:
        count = grad.shape[0] // 2
        rows = pl.ds(pl.multiple_of(half * count, count), count)
        for begin in range(0, grad.shape[1], LANES):
            target[pl.ds(at, count), :] = grad[rows, begin : begin + LANES].astype(BF16)
            at += count
    return at


def pack_turned(grad, half, target, at):
    count, columns = grad.shape[0], grad.shape[1] // 2
    for begin in range(0, columns, LANES):
        cols = pl.ds(pl.multiple_of(half * columns + begin, LANES), LANES)
        target[pl.ds(at, count), :] = grad[:, cols].astype(BF16)
        at += count
    return at


def pack_small(small, core, mine, other, at):
    rest = mine.shape[0] - at
    mine[pl.ds(at, rest), :] = jnp.zeros((rest, LANES), BF16)
    other[pl.ds(at, rest), :] = jnp.zeros((rest, LANES), BF16)
    for index in range(small.shape[1] // LANES):
        value = small[:, index * LANES : (index + 1) * LANES].astype(BF16)
        spot = pl.ds(at + (index // 2) * 16, 16)

        @pl.when(core == index % 2)
        def _():
            mine[spot, :] = value

        @pl.when(core != index % 2)
        def _():
            other[spot, :] = value


def step_copies(arrays, step, sems):
    spot = pl.ds(step * WIDE, WIDE)
    return [
        pltpu.make_async_copy(source.at[spot], target.at[spot], sems.at[step, at])
        for at, (source, target) in enumerate(arrays)
    ]


def leave(value_ref, own_out, halo_out, step, sems):
    rows = own_out.shape[0]
    begin, end = step * WIDE, (step + 1) * WIDE
    own = pl.ds(begin, min(rows, end) - begin)
    copies = [pltpu.make_async_copy(value_ref.at[own], own_out.at[own], sems.at[step, 6])]
    if end > rows:
        copies.append(pltpu.make_async_copy(value_ref.at[pl.ds(rows, end - rows)], halo_out, sems.at[step, 7]))
    for copy in copies:
        copy.start()
    return copies


def kernel_input(
    after, gain1, x_in, halo_in, w_in_in, triple_grad_in, middle_grad_in, out, out_halo,
    x, w_in, triple_grad, middle_grad, sems, step_sems,
):
    rows, width = x_in.shape
    total = x.shape[0]
    move = Mover(sems)
    early = [
        move.start(w_in_in, w_in),
        move.start(x_in, x.at[pl.ds(0, rows)]),
        move.start(halo_in.at[:, pl.ds(0, width)], x.at[pl.ds(rows, HALO)]),
    ]
    arrays = ((triple_grad_in, triple_grad), (middle_grad_in, middle_grad))
    steps = range(total // WIDE)
    parts = [step_copies(arrays, step, step_sems) for step in steps]
    for part in parts:
        for copy in part:
            copy.start()
    x[pl.ds(rows + HALO, total - rows - HALO), :] = jnp.zeros((total - rows - HALO, width), BF16)
    for copy in early:
        copy.wait()
    leaving = []
    for step in steps:
        for copy in parts[step]:
            copy.wait()
        spot = pl.ds(step * WIDE, WIDE)
        scaled, inverse = normalize(x[spot, :].astype(F32))
        normed_grad = dot_nt(triple_grad[spot, :], w_in[...])
        middle_grad[spot, :] = middle_grad[spot, :] + normalize_back(normed_grad, scaled, inverse, row_of(gain1))
        leaving += leave(middle_grad, out, out_halo, step, step_sems)
    for copy in leaving:
        copy.wait()


def kernel_result(
    after, table, b_sh, middle_in, hidden_in, w_sh_in, out, out_halo, middle, hidden, w_sh, value, sems, step_sems,
):
    total = middle.shape[0]
    move = Mover(sems)
    weight_copy = move.start(w_sh_in, w_sh)
    arrays = ((middle_in, middle), (hidden_in, hidden))
    steps = range(total // WIDE)
    parts = [step_copies(arrays, step, step_sems) for step in steps]
    for part in parts:
        for copy in part:
            copy.start()
    weight_copy.wait()
    leaving = []
    for step in steps:
        for copy in parts[step]:
            copy.wait()
        spot = pl.ds(step * WIDE, WIDE)
        keep = interval(step, table[GROUPS, 1], table[GROUPS, 2], WIDE)
        row = middle[spot, :] + row_of(b_sh) + dot(hidden[spot, :], w_sh[...])
        value[spot, :] = jnp.where(keep, row, 0.0).astype(BF16)
        leaving += leave(value, out, out_halo, step, step_sems)
    for copy in leaving:
        copy.wait()


def kernel_add(mine_in, other_in, out, mine, other, sems):
    chunks = sems.shape[0]
    size = mine.shape[0] // chunks

    def copies(chunk):
        spot = pl.ds(chunk * size, size)
        return [
            pltpu.make_async_copy(mine_in.at[spot], mine.at[spot], sems.at[chunk, 0]),
            pltpu.make_async_copy(other_in.at[spot], other.at[spot], sems.at[chunk, 1]),
            pltpu.make_async_copy(mine.at[spot], out.at[spot], sems.at[chunk, 2]),
        ]

    for chunk in range(chunks):
        for copy in copies(chunk)[:2]:
            copy.start()
    for chunk in range(chunks):
        spot = pl.ds(chunk * size, size)
        arriving = copies(chunk)
        for copy in arriving[:2]:
            copy.wait()
        mine[spot, :] = (mine[spot, :].astype(F32) + other[spot, :].astype(F32)).astype(BF16)
        arriving[2].start()
    for chunk in range(chunks):
        copies(chunk)[2].wait()


def kernel_sum(extra, *refs):
    parts_in, out, parts, piece, sems = refs[extra:]
    count = parts.shape[0]
    quarter = max(count // 4, 1)
    copies = []
    for index, begin in enumerate(range(0, count, quarter)):
        spot = pl.ds(begin, quarter)
        copies.append(pltpu.make_async_copy(parts_in.at[spot], parts.at[spot], sems.at[index]))
        copies[-1].start()
    total = jnp.zeros(piece.shape, F32)
    for index, copy in enumerate(copies):
        copy.wait()
        for part in range(index * quarter, (index + 1) * quarter):
            total = total + parts[part].astype(F32)
    piece[...] = total.astype(BF16)
    for part in range(count):
        pltpu.make_async_copy(piece, out.at[part], sems.at[4]).start()
    pltpu.make_async_copy(parts, out, sems.at[4]).wait()


def kernel_unpack_half(where, packed_in, d_ex, d_out, d_in, d_sh, packed, ex, out, inward, sh, sems):
    arrays = ((ex, d_ex), (sh, d_sh), (out, d_out), (inward, d_in))
    sizes = [value.shape[0] * value.shape[1] // LANES for value, _target in arrays]
    begins = [sum(sizes[:index]) for index in range(4)]
    arriving = []
    for index in range(4):
        spot = pl.ds(begins[index], sizes[index])
        arriving.append(pltpu.make_async_copy(packed_in.at[spot], packed.at[spot], sems.at[index]))
        arriving[-1].start()
    half = where[0]
    leaving = []
    for index, (value, target) in enumerate(arrays):
        arriving[index].wait()
        at = begins[index]
        if index != 1:
            count = value.shape[0]
            for begin in range(0, value.shape[1], LANES):
                value[:, begin : begin + LANES] = packed[pl.ds(at, count), :].astype(F32)
                at += count
        else:
            count = value.shape[1]
            for begin in range(0, value.shape[0], LANES):
                value[begin : begin + LANES, :] = packed[pl.ds(at, count), :].astype(F32).T
                at += count
        rows = pl.ds(pl.multiple_of(half * value.shape[0], value.shape[0]), value.shape[0])
        leaving.append(pltpu.make_async_copy(value, target.at[rows], sems.at[4 + index]))
        leaving[-1].start()
    return leaving


def kernel_first_half(where, packed_in, *refs):
    for copy in kernel_unpack_half(where, packed_in, *refs):
        copy.wait()


def kernel_second_half(
    where, packed_in, first_in, kept_ex, kept_out, kept_in, kept_sh,
    d_ex, d_out, d_in, d_sh, b_in, b_sh, gain2, shift2, b_out, b_ex, gain1, shift1,
    packed, ex, out, inward, sh, sems, mine, other, small_sems,
):
    del kept_ex, kept_out, kept_in, kept_sh
    rows = pl.ds(first_in.shape[0] - mine.shape[0], mine.shape[0])
    copies = [
        pltpu.make_async_copy(first_in.at[rows], mine, small_sems.at[0]),
        pltpu.make_async_copy(packed_in.at[rows], other, small_sems.at[1]),
    ]
    for copy in copies:
        copy.start()
    leaving = kernel_unpack_half(where, packed_in, d_ex, d_out, d_in, d_sh, packed, ex, out, inward, sh, sems)
    for copy in copies:
        copy.wait()
    width, columns = b_sh.shape[0], b_ex.shape[0]
    swap = where[0] == 0
    blocks = []
    for index in range(columns // LANES):
        spot = pl.ds(index // 2 * 16, 16)
        pair = mine[spot, :].astype(F32), other[spot, :].astype(F32)
        blocks.append(jnp.where(swap, pair[1 - index % 2], pair[index % 2]))
    small = jnp.concatenate(blocks, axis=1)
    for row, ref in ((0, b_sh), (1, gain2), (2, shift2), (3, b_out), (6, gain1), (7, shift1)):
        ref[...] = small[row, :width]
    b_ex[...] = small[4]
    b_in[0:1, :] = small[5:6, :width]
    b_in[1:2, :] = small[5:6, 2 * width : 3 * width]
    for copy in leaving:
        copy.wait()


def kernel_touch(*refs):
    del refs


VMEM = pl.BlockSpec(memory_space=pltpu.VMEM)
SMEM = pl.BlockSpec(memory_space=pltpu.SMEM)
ANY = pl.BlockSpec(memory_space=pl.ANY)


def params(mib):
    return pltpu.CompilerParams(vmem_limit_bytes=mib * 1024 * 1024)


def cost(flops, moved):
    return pl.CostEstimate(flops=int(flops), bytes_accessed=int(moved), transcendentals=0)


def shape(dims, dtype):
    return jax.ShapeDtypeStruct(dims, dtype)


def packed_rows(columns, small, pieces):
    half = columns // LANES * 192 + (small // LANES + 1) // 2 * 16
    return pieces * (-(-half // (8 * pieces)) * 8)


def attention_scratch(pairs):
    return [
        [pltpu.VMEM((pairs, WIN, 2 * WIN), F32)] * 2,
        [pltpu.VMEM((8, 2 * WIN), F32)] * 2,
        [pltpu.VMEM((pairs, 2 * WIN, WIN), BF16)] * 2,
        [pltpu.VMEM((8, 2 * WIN), F32)] * 2,
    ]


def own_part(place, segments, gain1, shift1, b_in, x, w_in):
    rows, width = x.shape
    total = rows + TILE
    vmem = pltpu.VMEM
    return pl.pallas_call(
        kernel_own,
        out_shape=(
            shape((rows, 3 * width), BF16),
            shape((total, width), BF16),
            shape((rows, width), BF16),
            shape((GROUPS, 8, WIN), F32),
            shape((GROUPS + 1, 8), jnp.int32),
        ),
        in_specs=[SMEM] + [ANY] * 6,
        out_specs=(ANY, ANY, ANY, VMEM, SMEM),
        scratch_shapes=[
            vmem(segments.shape, jnp.int32),
            vmem(gain1.shape, F32),
            vmem(shift1.shape, F32),
            vmem(b_in.shape, F32),
            vmem((rows, width), BF16),
            vmem(w_in.shape, BF16),
            vmem((total, 3 * width), BF16),
            vmem((total, width), BF16),
            vmem((8, LANES), jnp.int32),
            pltpu.SMEM((8, LANES), jnp.int32),
            *attention_scratch(width // (2 * HD)),
            pltpu.SemaphoreType.DMA((16,)),
            pltpu.SemaphoreType.DMA((rows // OWN,)),
        ],
        compiler_params=params(63),
        cost_estimate=cost(2 * 6 * rows * width * 3 * width, 1e7),
        name="own_part",
    )(place, segments, gain1, shift1, b_in, x, w_in)


def rest_part(place, table, vectors, x, cot, halo, triple, attended, scaled, stats, w_in, w_out, w_ex, w_sh, pieces):
    rows, width = x.shape
    total = rows + TILE
    hidden = w_ex.shape[1]
    packed = packed_rows(2 * hidden + 4 * width, hidden, pieces)
    vmem = pltpu.VMEM
    pairs = width // (2 * HD)
    square, row = vmem((pairs, WIN, 2 * WIN), F32), vmem((8, 2 * WIN), F32)
    low = vmem((pairs, WIN, 2 * WIN), BF16)
    return pl.pallas_call(
        kernel_rest,
        out_shape=(
            shape((total, width), F32),
            shape((total, width), F32),
            shape((total, hidden), BF16),
            shape((total, 3 * width), BF16),
            shape((packed, LANES), BF16),
            shape((packed, LANES), BF16),
        ),
        in_specs=[SMEM, SMEM] + [ANY] * 18,
        out_specs=tuple([ANY] * 6),
        scratch_shapes=[
            vmem((total, width), BF16),
            vmem((total, width), BF16),
            vmem(w_in.shape, BF16),
            vmem(w_out.shape, BF16),
            vmem(w_ex.shape, BF16),
            vmem(w_sh.shape, BF16),
            vmem((total, 3 * width), BF16),
            vmem((total, width), BF16),
            vmem((total, width), F32),
            vmem((total, width), F32),
            vmem((total, width), BF16),
            vmem((total, hidden), BF16),
            vmem((total, 3 * width), BF16),
            vmem((GROUPS, 8, WIN), F32),
            vmem((width, hidden), F32),
            vmem((width, hidden), F32),
            vmem((width, width), F32),
            vmem((width, 3 * width), F32),
            vmem((16, 3 * width), F32),
            vmem((16, hidden), F32),
            [square],
            [row],
            [vmem((pairs, 2 * WIN, WIN), BF16)],
            [row],
            [low] * 2,
            [low] * 2,
            vmem((TILE, width), BF16),
            vmem((packed, LANES), BF16),
            vmem((packed, LANES), BF16),
            pltpu.SemaphoreType.DMA((40,)),
            pltpu.SemaphoreType.DMA((2,)),
            *[vmem(v.shape, F32) for v in vectors],
        ],
        compiler_params=params(62),
        cost_estimate=cost(2 * 9 * rows * width * (3 * width + 8 * width), 3e7),
        name="rest_part",
    )(place, table, *vectors, x, cot, halo, triple, attended, scaled, stats, w_in, w_out, w_ex, w_sh)


def input_gradient(after, gain1, x, halo, w_in, triple_grad, middle_grad):
    rows, width = x.shape
    total = triple_grad.shape[0]
    vmem = pltpu.VMEM
    return pl.pallas_call(
        kernel_input,
        out_shape=(shape((rows, width), F32), shape((TILE, width), F32)),
        in_specs=[ANY, VMEM] + [ANY] * 5,
        out_specs=(ANY, ANY),
        scratch_shapes=[
            vmem((total, width), BF16),
            vmem(w_in.shape, BF16),
            vmem((total, 3 * width), BF16),
            vmem((total, width), F32),
            pltpu.SemaphoreType.DMA((4,)),
            pltpu.SemaphoreType.DMA((total // WIDE, 8)),
        ],
        compiler_params=params(63),
        cost_estimate=cost(2 * rows * width * 9 * width, 1.4e7),
        name="input_gradient",
    )(after, gain1, x, halo, w_in, triple_grad, middle_grad)


def layer_result(after, table, b_sh, middle, hidden, w_sh):
    total, width = middle.shape
    vmem = pltpu.VMEM
    return pl.pallas_call(
        kernel_result,
        out_shape=(shape((total - TILE, width), BF16), shape((TILE, width), BF16)),
        in_specs=[ANY, SMEM, VMEM] + [ANY] * 3,
        out_specs=(ANY, ANY),
        scratch_shapes=[
            vmem(middle.shape, F32),
            vmem(hidden.shape, BF16),
            vmem(w_sh.shape, BF16),
            vmem(middle.shape, BF16),
            pltpu.SemaphoreType.DMA((2,)),
            pltpu.SemaphoreType.DMA((total // WIDE, 8)),
        ],
        compiler_params=params(63),
        cost_estimate=cost(2 * total * width * 8 * width, 1.3e7),
        name="layer_result",
    )(after, table, b_sh, middle, hidden, w_sh)


def add_halves(mine, other):
    return pl.pallas_call(
        kernel_add,
        out_shape=shape(mine.shape, BF16),
        in_specs=[ANY, ANY],
        out_specs=ANY,
        scratch_shapes=[
            pltpu.VMEM(mine.shape, BF16), pltpu.VMEM(mine.shape, BF16), pltpu.SemaphoreType.DMA((4, 3)),
        ],
        compiler_params=params(63),
        cost_estimate=cost(mine.size, mine.size * 6),
        name="add_halves",
    )(mine, other)


def sum_parts(after, parts):
    return pl.pallas_call(
        partial(kernel_sum, len(after)),
        out_shape=shape(parts.shape, BF16),
        in_specs=[ANY] * (len(after) + 1),
        out_specs=ANY,
        scratch_shapes=[
            pltpu.VMEM(parts.shape, BF16),
            pltpu.VMEM(parts.shape[1:], BF16),
            pltpu.SemaphoreType.DMA((5,)),
        ],
        compiler_params=params(63),
        cost_estimate=cost(parts.size, parts.size * 4),
        name="sum_parts",
    )(*after, parts)


def half_shapes(width, hidden):
    dims = ((width, hidden), (width, width), (width, 3 * width), (hidden, width))
    scratch = [pltpu.VMEM((rows // 2, columns), F32) for rows, columns in dims]
    return tuple(shape(dim, F32) for dim in dims), [*scratch, pltpu.SemaphoreType.DMA((8,))]


def unpack_first(half, packed, width, hidden):
    shapes, scratch = half_shapes(width, hidden)
    return pl.pallas_call(
        kernel_first_half,
        out_shape=shapes,
        in_specs=[SMEM, ANY],
        out_specs=(ANY,) * 4,
        scratch_shapes=[pltpu.VMEM(packed.shape, BF16), *scratch],
        compiler_params=params(63),
        cost_estimate=cost(packed.size, packed.size * 6),
        name="unpack_first",
    )(half, packed)


def unpack_second(half, packed, first, kept, used, width, hidden):
    shapes, scratch = half_shapes(width, hidden)
    rows = first.shape[0] - used
    small = tuple(shape(dims, F32) for dims in ((2, width),) + ((width,),) * 4 + ((hidden,), (width,), (width,)))
    return pl.pallas_call(
        kernel_second_half,
        out_shape=shapes + small,
        in_specs=[SMEM] + [ANY] * 6,
        out_specs=(ANY,) * 4 + (VMEM,) * 8,
        scratch_shapes=[
            pltpu.VMEM(packed.shape, BF16), *scratch, pltpu.VMEM((rows, LANES), BF16), pltpu.VMEM((rows, LANES), BF16),
            pltpu.SemaphoreType.DMA((2,)),
        ],
        input_output_aliases={3: 0, 4: 1, 5: 2, 6: 3},
        compiler_params=params(63),
        cost_estimate=cost(packed.size, packed.size * 6),
        name="unpack_second",
    )(half, packed, first, *kept)


def touch(value, *after):
    return pl.pallas_call(
        kernel_touch,
        out_shape=shape(value.shape, value.dtype),
        in_specs=[ANY] * (1 + len(after)),
        out_specs=ANY,
        input_output_aliases={0: 0},
        name="touch",
    )(value, *after)


def same_core_groups():
    packs, parts = lax.axis_size("dp"), lax.axis_size("mp")
    return [[d * parts + m for d in range(c, packs, 2) for m in range(parts)] for c in range(2)]


def swap_cores(block):
    packs = lax.axis_size("dp")
    return lax.ppermute(block, "dp", [(i, i ^ 1) for i in range(packs)])


def exchange(parts):
    return lax.all_to_all(parts, ("dp", "mp"), 0, 0, axis_index_groups=same_core_groups())


def passed(block, distance):
    count = lax.axis_size("mp")
    route = [(i, i + distance) for i in range(count) if 0 <= i + distance < count]
    return lax.ppermute(block, "mp", route)


def kernel_take_over(table, own_in, other_in, own_out, own, other, sems):
    rows = pl.ds(0, HALO)
    copies = [
        pltpu.make_async_copy(own_in.at[rows], own, sems.at[0]), pltpu.make_async_copy(other_in, other, sems.at[1])
    ]
    for copy in copies:
        copy.start()
    for copy in copies:
        copy.wait()
    row = lax.broadcasted_iota(jnp.int32, (HALO, 1), 0)
    mixed = jnp.where(row < table[GROUPS, 1], other[...].astype(F32), own[...].astype(F32))
    own[...] = mixed.astype(own.dtype)
    copy = pltpu.make_async_copy(own, own_out.at[rows], sems.at[2])
    copy.start()
    copy.wait()


def take_over(table, own, other):
    return pl.pallas_call(
        kernel_take_over,
        out_shape=shape(own.shape, own.dtype),
        in_specs=[SMEM, ANY, ANY],
        out_specs=ANY,
        scratch_shapes=[
            pltpu.VMEM(other.shape, own.dtype), pltpu.VMEM(other.shape, own.dtype), pltpu.SemaphoreType.DMA((3,)),
        ],
        input_output_aliases={1: 0},
        compiler_params=params(63),
        name="take_over",
    )(table, own, other)


def body(
    layer_input, segments, cotangent, first_gain, first_shift, inward_weight, inward_bias, outward_weight,
    outward_bias, second_gain, second_shift, expand_weight, expand_bias, shrink_weight, shrink_bias,
):
    rows, width = layer_input.shape
    hidden_width = expand_weight.shape[1]
    position = lax.axis_index("mp")
    core = lax.axis_index("dp") % 2
    pieces = lax.axis_size("dp") * lax.axis_size("mp") // 2
    place = jnp.stack([position, position, core]).astype(jnp.int32)
    gain1, shift1, b_out, gain2, shift2, b_ex, b_sh = (
        first_gain, first_shift, outward_bias, second_gain, second_shift, expand_bias, shrink_bias
    )
    halo = passed(jnp.concatenate([layer_input[:HALO], cotangent[:HALO]], axis=1), -1)
    triple, attended, scaled, stats, table = own_part(
        place, segments, gain1, shift1, inward_bias, layer_input, inward_weight
    )
    middle, middle_grad, hidden, triple_grad, mine, other = rest_part(
        place, table, (gain1, shift1, inward_bias, b_out, gain2, shift2, b_ex), layer_input, cotangent, halo, triple,
        attended, scaled, stats, inward_weight, outward_weight, expand_weight, shrink_weight, pieces,
    )
    both = add_halves(mine, swap_cores(other))
    parts = exchange(both.reshape(pieces, -1, LANES))
    input_grad, input_halo = input_gradient(both, gain1, layer_input, halo, inward_weight, triple_grad, middle_grad)
    result, result_halo = layer_result(input_halo, table, b_sh, middle, hidden, shrink_weight)
    input_other = passed(input_halo[:HALO], 1)
    summed = sum_parts((input_other, result_halo), parts)
    mine = exchange(summed).reshape(-1, LANES)
    input_grad = take_over(table, input_grad, touch(input_other, summed))
    result = take_over(table, result, passed(touch(result_halo, summed)[:HALO], 1))
    mine = touch(mine, input_grad, result)
    other = swap_cores(mine)
    used = 192 * (2 * hidden_width + 4 * width) // LANES
    half = unpack_first(place[2:], mine, width, hidden_width)
    d_ex, d_out, d_in, d_sh, d_b_in, d_b_sh, d_gain2, d_shift2, d_b_out, d_b_ex, d_gain1, d_shift1 = unpack_second(
        1 - place[2:], other, mine, half, used, width, hidden_width
    )
    return (
        result, input_grad, d_gain1, d_shift1, d_in, d_b_in, d_out, d_b_out, d_gain2, d_shift2, d_ex, d_b_ex, d_sh,
        d_b_sh,
    )


def solution(mesh):
    rows = P(("dp", "mp"), None)
    in_specs = (rows, P("dp", None), rows) + (P(),) * 12
    out_specs = (rows, rows) + (P(),) * 12
    return jax.shard_map(body, mesh=mesh, in_specs=in_specs, out_specs=out_specs, check_vma=False)
```

```python
from functools import partial

import jax
import jax.numpy as jnp
from jax import lax
from jax.experimental import pallas as pl
from jax.experimental.pallas import tpu as pltpu
from jax.sharding import PartitionSpec as P

HD = 64
SEQ = 198
EPSILON = 1e-06
MASKED = -1000000000.0
LOG2E = 1.4426950408889634
WIN = 256
TILE = 256
HALO = 208
WIDE = 768
OWN = 1024
GROUPS = 24
SLOTS = 5
LANES = 128
CHUNK = 256
FEED = 768
BIG = 1 << 20
F32 = jnp.float32
BF16 = jnp.bfloat16
NT = (((1,), (1,)), ((), ()))
TN = (((0,), (0,)), ((), ()))


def row_of(ref):
    return ref[...].reshape(1, -1)


def dot(a, b):
    return jnp.dot(a, b, preferred_element_type=F32)


def dot_nt(a, b):
    return lax.dot_general(a, b, NT, preferred_element_type=F32)


def dot_tn(a, b):
    return lax.dot_general(a, b, TN, preferred_element_type=F32)


def normalize(rows):
    center = jnp.mean(rows, axis=-1, keepdims=True)
    centred = rows - center
    spread = jnp.mean(centred * centred, axis=-1, keepdims=True)
    inverse = lax.rsqrt(spread + EPSILON)
    return centred * inverse, inverse


def normalize_back(upstream, scaled, inverse, gain):
    direct = upstream * gain
    first = jnp.mean(direct, axis=-1, keepdims=True)
    second = jnp.mean(direct * scaled, axis=-1, keepdims=True)
    return inverse * (direct - first - scaled * second)


def gelu_parts(v, half_upstream):
    scaled = v * 0.7071067811865476
    double = 1.0 + lax.erf(scaled)
    bell = jnp.exp2((scaled * scaled) * -1.4426950408889634)
    return (0.5 * v) * double, half_upstream * (double + (v * 0.7978845608028654) * bell)


def image_ends(seg, base, work):
    ident = lax.broadcasted_iota(jnp.int32, (LANES, LANES), 0)
    below = jnp.zeros((LANES, LANES), F32)
    for begin in range(0, seg.shape[1], LANES):
        row = seg[0:1, begin : begin + LANES]
        row = jnp.where(row < 0, BIG, row)
        below = below + jnp.where(row <= ident, 1.0, 0.0)
    ends = jnp.broadcast_to(jnp.sum(below, axis=1, keepdims=True), (LANES, LANES))
    started = jnp.sum(jnp.where(ends < base.astype(F32), 1.0, 0.0), axis=0, keepdims=True)
    work[0:1, :] = ends.T[0:1].astype(jnp.int32)
    work[1:2, :] = started.astype(jnp.int32)


def plan_groups(ends, position, rows, table):
    base = position * rows
    limit = jnp.minimum(base + rows, ends[0, LANES - 1]) - base
    image = jnp.where(position == 0, 0, ends[1, 0] + 1)
    first = jnp.where(position == 0, 0, ends[0, jnp.maximum(image - 1, 0)]) - base

    def body(state):
        at, image, group, window, start, c1, c2 = state
        after = ends[0, jnp.minimum(image, LANES - 1)] - base
        fits = after - window <= WIN

        @pl.when(jnp.logical_not(fits))
        def _():
            write_group(table, group, window, start, c1, c2, at)

        group = jnp.where(fits, group, group + 1)
        new_c1 = jnp.where(fits, jnp.where(at == start, c1, jnp.where(c1 < 0, at, c1)), -1)
        new_c2 = jnp.where(fits, jnp.where(jnp.logical_and(at != start, c1 >= 0), jnp.where(c2 < 0, at, c2), c2), -1)
        start = jnp.where(fits, start, at)
        window = jnp.where(fits, window, (at // 16) * 16)
        return after, image + 1, group, window, start, new_c1, new_c2

    init = (first, image, jnp.int32(0), (first // 16) * 16, first, jnp.int32(-1), jnp.int32(-1))
    at, image, group, window, start, c1, c2 = lax.while_loop(lambda s: s[0] < limit, body, init)
    write_group(table, group, window, start, c1, c2, at)
    table[GROUPS, 0] = group + 1
    table[GROUPS, 1] = first
    table[GROUPS, 2] = at


def write_group(table, group, window, start, c1, c2, end):
    table[group, 0] = window
    table[group, 1] = start - window
    table[group, 2] = jnp.where(c1 < 0, end, c1) - window
    table[group, 3] = jnp.where(c2 < 0, end, c2) - window
    table[group, 4] = end - window


def group_bias(table, group):
    bounds = [table[group, i] for i in range(1, 5)]
    row = lax.broadcasted_iota(jnp.int32, (WIN, LANES), 0)
    col = lax.broadcasted_iota(jnp.int32, (1, WIN), 1)

    def ident(index):
        return sum((index >= b).astype(jnp.int32) for b in bounds)

    row, col = ident(row), ident(col)
    return jnp.concatenate(
        [jnp.where(row == col[:, at : at + LANES], 0.0, MASKED) for at in range(0, WIN, LANES)], axis=1
    )


def group_mask_factors(table, group):
    bounds = [table[group, i] for i in range(1, 5)]

    def ident(index):
        return sum((index >= b).astype(jnp.int32) for b in bounds)

    row = ident(lax.broadcasted_iota(jnp.int32, (WIN, LANES), 0))
    left = jnp.where(row == lax.broadcasted_iota(jnp.int32, (WIN, LANES), 1), 1.0, 0.0).astype(BF16)
    col = ident(lax.broadcasted_iota(jnp.int32, (1, WIN), 1))
    kind = lax.broadcasted_iota(jnp.int32, (16, WIN), 0)
    right = jnp.where(kind == col, 0.0, MASKED).astype(BF16)
    right = jnp.concatenate([right, jnp.zeros((LANES - 16, WIN), BF16)], axis=0)
    return left, jnp.concatenate([right, right], axis=1)


def head_masks():
    lane = lax.broadcasted_iota(jnp.int32, (WIN, 2 * HD), 1)
    return lane < HD, lane >= HD


def keep_first(ref, window, begin, cols, value):
    head = pl.ds(window, 16)
    old = ref[head, cols]
    row = lax.broadcasted_iota(jnp.int32, (16, 2 * HD), 0)
    ref[head, cols] = jnp.where(row >= begin, value[:16].astype(F32), old.astype(F32)).astype(BF16)
    ref[pl.ds(window + 16, WIN - 16), cols] = value[16:].astype(BF16)


def block_diagonal(pair_t):
    zero = jnp.zeros((HD, pair_t.shape[1]), pair_t.dtype)
    return jnp.concatenate(
        [jnp.concatenate([pair_t[:HD], zero], axis=1), jnp.concatenate([zero, pair_t[HD:]], axis=1)], axis=0
    )


def pipelined(groups, first, second, third, keep_copy):
    def clamped(group):
        return jnp.minimum(group, groups - 1)

    def half(group, slot):
        first(clamped(group), slot)
        second(clamped(group - 1), 1 - slot)
        third(clamped(group - 2), slot)

    first(0, 0)
    first(clamped(1), 1)
    second(0, 0)
    steps = (groups + 1) // 2

    def both(step, _):
        keep_copy(clamped(2 * step)).start()

        @pl.when(step > 0)
        def _():
            keep_copy(clamped(2 * step - 1)).start()

        half(2 * step + 2, 0)
        half(2 * step + 3, 1)
        return 0

    lax.fori_loop(0, steps, both, 0)
    keep_copy(clamped(2 * steps - 1)).start()

    def settle(_, carry):
        keep_copy(0).wait()
        return carry

    return lambda: lax.fori_loop(0, 2 * steps, settle, 0)


def group_rows(table, group):
    return pl.ds(pl.multiple_of(table[group, 0], 16), WIN)


def attend_groups(groups, table, triple, attended, stats, scores, peaks, raised, scales, alone=None, kept=None, keep_copy=None):
    width = attended.shape[1]
    pairs = range(width // (2 * HD))

    def first(group, slot):
        rows = group_rows(table, group)
        left, right = group_mask_factors(table, group)
        for pair in pairs:
            query_t = triple[rows, pl.ds(pair * 2 * HD, 2 * HD)].T
            key = triple[rows, pl.ds(width + pair * 2 * HD, 2 * HD)]
            value = dot(
                jnp.concatenate([key, left], axis=1), jnp.concatenate([block_diagonal(query_t), right], axis=0)
            )
            scores[slot][pair] = value
            peaks[slot][pair : pair + 1, :] = jnp.max(value, axis=0, keepdims=True)

    def second(group, slot):
        for pair in pairs:
            peak = peaks[slot][pair : pair + 1, :]
            value = jnp.exp2(scores[slot][pair] - peak)
            total = jnp.sum(value, axis=0, keepdims=True)
            low = value.astype(BF16)
            raised[slot][pair, :WIN] = low[:, :WIN]
            raised[slot][pair, WIN:] = low[:, WIN:]
            if kept is not None:
                kept[group, pair, :WIN] = low[:, :WIN]
                kept[group, pair, WIN:] = low[:, WIN:]
            scale = 1.0 / total
            scales[slot][pair : pair + 1, :] = scale
            stats[group, pl.ds(2 * pair, 1), :] = scale[:, :WIN]
            stats[group, pl.ds(2 * pair + 1, 1), :] = scale[:, WIN:]

    def third(group, slot):
        rows = group_rows(table, group)
        for pair in pairs:
            value_t = block_diagonal(triple[rows, pl.ds(2 * width + pair * 2 * HD, 2 * HD)].T)
            out = dot(value_t, raised[slot][pair])
            scale = scales[slot][pair : pair + 1, :]
            out = jnp.concatenate([out[:HD] * scale[:, :WIN], out[HD:] * scale[:, WIN:]], axis=0)
            keep_first(attended, rows.start, table[group, 1], pl.ds(pair * 2 * HD, 2 * HD), out.T)

    if alone is None:
        return pipelined(groups, first, second, third, keep_copy)
    for part in (first, second, third):
        part(alone, 0)
    return None


def attend_back_groups(
    groups, table, triple, attended, upstream, stats, triple_grad, scores_grads, scaled_up, kept, kept_copy
):
    width = attended.shape[1]
    pairs = range(width // (2 * HD))
    masks = head_masks()

    def columns(pair, block):
        return pl.ds(block * width + pair * 2 * HD, 2 * HD)

    def side_by_side(turn, pair):
        low = kept[lax.rem(turn, SLOTS), pair]
        return jnp.concatenate([low[:WIN], low[WIN:]], axis=1)

    def first(turn, group, slot):
        rows = group_rows(table, group)
        for pair in pairs:
            scale = [jnp.broadcast_to(stats[group, pl.ds(2 * pair + h, 1), :], (HD, WIN)) for h in range(2)]
            up_t = upstream[rows, columns(pair, 0)].T.astype(F32) * jnp.concatenate(scale, axis=0)
            product = attended[rows, columns(pair, 0)].T.astype(F32) * up_t
            agreement = jnp.concatenate(
                [jnp.sum(product[:HD], axis=0, keepdims=True), jnp.sum(product[HD:], axis=0, keepdims=True)], axis=1
            )
            up_low = up_t.astype(BF16)
            scaled_up[slot][pair] = up_low
            probs_grad = dot(triple[rows, columns(pair, 2)], block_diagonal(up_low))
            prob = side_by_side(turn, pair).astype(F32)
            scores_grads[slot][pair] = (prob * (probs_grad - agreement)).astype(BF16)

    def stacked(pair_rows):
        zero = jnp.zeros_like(pair_rows)
        return jnp.concatenate([jnp.where(mask, pair_rows, zero) for mask in masks], axis=0)

    def second(turn, group, slot):
        rows = group_rows(table, group)
        window, begin = rows.start, table[group, 1]
        for pair in pairs:
            scores_grad = scores_grads[slot][pair]
            value_grad = dot_nt(side_by_side(turn, pair), block_diagonal(scaled_up[slot][pair]))
            key_grad = dot(scores_grad, stacked(triple[rows, columns(pair, 0)]))
            key_t = block_diagonal(triple[rows, columns(pair, 1)].T)
            query_grad = dot(key_t, jnp.concatenate([scores_grad[:, :WIN], scores_grad[:, WIN:]], axis=0))
            keep_first(triple_grad, window, begin, columns(pair, 0), (query_grad * HD ** (-0.5)).T)
            keep_first(triple_grad, window, begin, columns(pair, 1), key_grad * (1.0 / LOG2E))
            keep_first(triple_grad, window, begin, columns(pair, 2), value_grad)

    def clamped(turn):
        return jnp.minimum(turn, groups - 1)

    def half(turn, slot):
        first(turn, clamped(turn), slot)
        second(turn - 1, clamped(turn - 1), 1 - slot)

    steps = (groups + 1) // 2

    def fetch(turn):
        kept_copy(clamped(turn), lax.rem(turn, SLOTS))

    def arrived(turn):
        kept_copy(None, lax.rem(turn, SLOTS))

    arrived(jnp.int32(0))
    first(jnp.int32(0), 0, 0)

    def both(step, _):
        @pl.when(step + 1 < steps)
        def _():
            fetch(2 * step + 3)
            fetch(2 * step + 4)

        arrived(2 * step + 1)
        arrived(2 * step + 2)
        half(2 * step + 1, 1)
        half(2 * step + 2, 0)
        return 0

    lax.fori_loop(0, steps, both, 0)


def interval(tile, first, end, size=TILE):
    row = lax.broadcasted_iota(jnp.int32, (size, 1), 0) + tile * size
    return jnp.logical_and(row >= first, row < end)


class Mover:
    def __init__(self, sems):
        self.sems = sems
        self.count = 0

    def start(self, source, target):
        copy = pltpu.make_async_copy(source, target, self.sems.at[self.count])
        self.count += 1
        copy.start()
        return copy


def project_rows(rows, gain1, shift1, w_in, b_in, target, spot, scaled_ref, scaled_spot):
    width = rows.shape[1]
    scaled, _inverse = normalize(rows)
    scaled_ref[scaled_spot, :] = scaled.astype(BF16)
    normed = (scaled * row_of(gain1) + row_of(shift1)).astype(BF16)
    q = dot(normed, w_in[:, :width]) + b_in[0:1, :]
    target[spot, :width] = (q.astype(BF16).astype(F32) * (HD ** (-0.5) * LOG2E)).astype(BF16)
    target[spot, width : 2 * width] = dot(normed, w_in[:, width : 2 * width]).astype(BF16)
    target[spot, 2 * width :] = (dot(normed, w_in[:, 2 * width :]) + b_in[1:2, :]).astype(BF16)


def kernel_own(
    seg_in, gain1_in, shift1_in, b_in_in, x_in, w_in_in,
    triple_out, attended_out, scaled_out, raised_out, stats, table,
    seg, gain1, shift1, b_in, x, w_in, triple, attended, work, ends, scores, peaks, raised, scales, kept, sems, tile_sems,
):
    rows, width = x_in.shape
    move = Mover(sems)
    seg_copy = move.start(seg_in, seg)
    early = [
        move.start(gain1_in, gain1), move.start(shift1_in, shift1), move.start(b_in_in, b_in),
        move.start(x_in, x), move.start(w_in_in, w_in),
    ]
    seg_copy.wait()
    image_ends(seg, lax.axis_index("mp") * rows, work)
    end_copy = move.start(work, ends)
    attended[...] = jnp.zeros_like(attended)
    spare = pl.ds(rows, triple.shape[0] - rows)
    triple[spare, :] = jnp.zeros((triple.shape[0] - rows, 3 * width), BF16)
    for copy in early:
        copy.wait()

    def step_copy(step):
        spot = pl.ds(pl.multiple_of(step * OWN, OWN), OWN)
        return pltpu.make_async_copy(triple.at[spot], triple_out.at[spot], tile_sems.at[step])

    def step_rows(step, _):
        spot = pl.ds(pl.multiple_of(step * OWN, OWN), OWN)
        project_rows(x[spot, :].astype(F32), gain1, shift1, w_in, b_in, triple, spot, x, spot)
        step_copy(step).start()
        return 0

    lax.fori_loop(0, rows // OWN, step_rows, 0)
    scaled_copy = move.start(x, scaled_out)
    end_copy.wait()
    plan_groups(ends, lax.axis_index("mp"), rows, table)

    def keep_copy(group):
        return pltpu.make_async_copy(kept.at[group], raised_out.at[group], tile_sems.at[rows // OWN])

    settle = attend_groups(
        jnp.maximum(table[GROUPS, 0] - 1, 1), table, triple, attended, stats, scores, peaks, raised, scales,
        kept=kept, keep_copy=keep_copy,
    )
    leaving = move.start(attended, attended_out)
    scaled_copy.wait()
    settle()
    for step in range(rows // OWN):
        step_copy(step).wait()
    leaving.wait()


def kernel_rest(
    table, *refs
):
    vectors_in, refs = refs[:7], refs[7:]
    vectors, refs = refs[-7:], refs[:-7]
    rest_body(table, vectors_in, vectors, *refs)


def rest_body(
    table, vectors_in, vectors,
    x_in, cot_in, halo_in, triple_in, attended_in, scaled_in, raised_in, stats_in, w_in_in, w_out_in, w_ex_in, w_sh_in,
    middle_out, middle_grad_out, hidden_out, triple_grad_out, edge_out, mine_out, other_out,
    x, back, w_in, w_out, w_ex, w_sh, triple, attended, middle, middle_grad, upstream, hidden, triple_grad, stats,
    d_ex, d_sh, d_out, product, sums, small, scores, peaks, raised, scales, scaled_up, scores_grads,
    kept, edge, mine, other, sems, tile_sems, kept_sems,
):
    rows, width = x_in.shape
    total = x.shape[0]
    tiles = total // FEED
    normed2, normed_grad = upstream, middle_grad
    move = Mover(sems)
    own, over = pl.ds(0, rows), pl.ds(rows, HALO)
    gain1, shift1, b_in, b_out, gain2, shift2, b_ex = vectors
    near, far = pl.ds(2 * WIDE, rows - 2 * WIDE), pl.ds(0, 2 * WIDE)
    first_copies = [move.start(halo_in.at[:, pl.ds(0, width)], x.at[over])]
    first_copies += [move.start(source, target) for source, target in zip(vectors_in, vectors)]
    first_copies.append(move.start(w_in_in, w_in))
    early = [
        move.start(triple_in.at[near], triple.at[near]),
        move.start(stats_in, stats),
        move.start(attended_in, attended),
    ]
    late = [
        move.start(w_out_in, w_out),
        move.start(x_in, x.at[own]),
        move.start(cot_in, back.at[own]),
        move.start(halo_in.at[:, pl.ds(width, width)], back.at[over]),
    ]
    weight_copies = [move.start(w_ex_in, w_ex), move.start(w_sh_in, w_sh)]
    last = move.start(triple_in.at[far], triple.at[far])
    rest = pl.ds(rows + HALO, total - rows - HALO)
    x[rest, :] = jnp.zeros((total - rows - HALO, width), BF16)
    back[rest, :] = jnp.zeros((total - rows - HALO, width), BF16)
    for ref in (d_ex, d_sh, d_out, product, sums, small, triple_grad):
        ref[...] = jnp.zeros_like(ref)
    groups, first, end = table[GROUPS, 0], table[GROUPS, 1], table[GROUPS, 2]
    for copy in first_copies:
        copy.wait()
    tail = pl.ds(rows, TILE)
    edge_copy = move.start(x.at[tail], edge_out)
    project_rows(x[tail, :].astype(F32), gain1, shift1, w_in, b_in, triple, tail, edge, slice(None))
    for copy in early:
        copy.wait()
    attend_groups(groups, table, triple, attended, stats, scores, peaks, raised, scales, alone=groups - 1)
    def kept_copy(group, slot):
        if group is None:
            pltpu.make_async_copy(raised[0], kept.at[slot], kept_sems.at[slot]).wait()
            return

        @pl.when(group == groups - 1)
        def _():
            pltpu.make_async_copy(raised[0], kept.at[slot], kept_sems.at[slot]).start()

        @pl.when(group != groups - 1)
        def _():
            pltpu.make_async_copy(raised_in.at[group], kept.at[slot], kept_sems.at[slot]).start()

    for turn in range(3):
        kept_copy(jnp.int32(turn), turn)
    for copy in late:
        copy.wait()
    leaving = []

    hidden_width = w_ex.shape[1]
    begins = list(range(0, hidden_width, CHUNK))

    def wide_rows(step):
        return pl.ds(pl.multiple_of(step * WIDE, WIDE), WIDE)

    def before_feed(step, _):
        spot = wide_rows(step)
        value = x[spot, :].astype(F32) + dot(attended[spot, :], w_out[...]) + row_of(b_out)
        scaled, _inverse = normalize(value)
        middle[spot, :] = value
        normed2[spot, :] = (scaled * row_of(gain2) + row_of(shift2)).astype(BF16)
        keep = interval(step, first, end, WIDE)
        back[spot, :] = jnp.where(keep, back[spot, :].astype(F32), 0.0).astype(BF16)
        return 0

    def feed(tile, _):
        spot = pl.ds(pl.multiple_of(tile * FEED, FEED), FEED)
        normed = normed2[spot, :]
        back_low = back[spot, :]
        back_half = (0.5 * back_low.astype(F32)).astype(BF16)

        def first_part(begin):
            cols = slice(begin, begin + CHUNK)
            before = dot(normed, w_ex[:, cols]) + b_ex[cols].reshape(1, -1)
            return before, dot_nt(back_half, w_sh[cols, :])

        held = [first_part(begins[0])]
        total_grad = jnp.zeros((width, FEED), F32)
        for index, begin in enumerate(begins):
            cols = slice(begin, begin + CHUNK)
            if index + 1 < len(begins):
                held.append(first_part(begins[index + 1]))
            value, grad = gelu_parts(*held[index])
            value, grad = value.astype(BF16), grad.astype(BF16)
            hidden[spot, cols] = value
            total_grad = total_grad + dot_nt(w_ex[:, cols], grad)
            d_sh[:, cols] += dot_tn(back_low, value)
            d_ex[:, cols] += dot_tn(normed, grad)
            small[4:5, cols] += jnp.sum(grad.astype(F32), axis=0, keepdims=True)
        normed_grad[spot, :] = total_grad.T
        pltpu.make_async_copy(hidden.at[spot], hidden_out.at[spot], tile_sems.at[0]).start()
        return 0

    def after_feed(step, _):
        spot = wide_rows(step)
        back32 = back[spot, :].astype(F32)
        scaled, inverse = normalize(middle[spot, :])
        upstream2 = normed_grad[spot, :]
        small[0:1, :width] += jnp.sum(back32, axis=0, keepdims=True)
        small[1:2, :width] += jnp.sum(upstream2 * scaled, axis=0, keepdims=True)
        small[2:3, :width] += jnp.sum(upstream2, axis=0, keepdims=True)
        grad = back32 + normalize_back(upstream2, scaled, inverse, row_of(gain2))
        small[3:4, :width] += jnp.sum(grad, axis=0, keepdims=True)
        middle_grad[spot, :] = grad
        grad_low = grad.astype(BF16)
        d_out[...] += dot_tn(attended[spot, :], grad_low)
        upstream[spot, :] = dot_nt(grad_low, w_out[...]).astype(BF16)
        pltpu.make_async_copy(middle_grad.at[spot], middle_grad_out.at[spot], tile_sems.at[1]).start()
        return 0

    lax.fori_loop(0, total // WIDE, before_feed, 0)
    for copy in weight_copies:
        copy.wait()
    edge_copy.wait()
    scaled_copy = move.start(scaled_in, x.at[own])
    x[tail, :] = edge[...]
    leaving.append(move.start(middle, middle_out))
    lax.fori_loop(0, tiles, feed, 0)
    lax.fori_loop(0, total // WIDE, after_feed, 0)
    core = lax.rem(lax.axis_index("dp"), 2)
    for half, target in ((core, mine), (1 - core, other)):
        at = pack((d_out,), half, target, pack_turned(d_sh, half, target, pack((d_ex,), half, target, 0)))
    ready = pl.ds(0, at)
    leaving += [move.start(mine.at[ready], mine_out.at[ready]), move.start(other.at[ready], other_out.at[ready])]
    last.wait()
    attend_back_groups(
        groups, table, triple, attended, upstream, stats, triple_grad, scores_grads, scaled_up, kept, kept_copy
    )
    leaving.append(move.start(triple_grad, triple_grad_out))
    scaled_copy.wait()
    ones = jnp.ones((16, WIDE), BF16)

    def multiply(step, _):
        spot = wide_rows(step)
        grad = triple_grad[spot, :]
        product[...] += dot_tn(x[spot, :], grad)
        sums[...] += dot(ones, grad)
        return 0

    lax.fori_loop(0, total // WIDE, multiply, 0)
    gain = jnp.broadcast_to(row_of(gain1), (LANES, width)).T
    shift = jnp.broadcast_to(row_of(shift1), (LANES, width)).T
    by_gain = jnp.zeros((width, LANES), F32)
    by_shift = jnp.zeros((width, LANES), F32)
    for begin in range(0, 3 * width, LANES):
        cols = slice(begin, begin + LANES)
        block, sum_row = product[:, cols], sums[0:1, cols]
        weight = w_in[:, cols].astype(F32)
        by_gain = by_gain + weight * block
        by_shift = by_shift + weight * sum_row
        product[:, cols] = gain * block + shift * sum_row
    small[5:6, : 3 * width] = sums[0:1, :]
    by_gain = jnp.broadcast_to(jnp.sum(by_gain, axis=1, keepdims=True), (width, LANES)).T
    by_shift = jnp.broadcast_to(jnp.sum(by_shift, axis=1, keepdims=True), (width, LANES)).T
    small[6:7, :width] = by_gain[0:1]
    small[7:8, :width] = by_shift[0:1]
    begin = at
    for half, target in ((core, mine), (1 - core, other)):
        at = pack((product,), half, target, begin)
    pack_small(small, core, mine, other, at)
    ready = pl.ds(begin, mine.shape[0] - begin)
    leaving += [move.start(mine.at[ready], mine_out.at[ready]), move.start(other.at[ready], other_out.at[ready])]
    for copy in leaving:
        copy.wait()
    pltpu.make_async_copy(hidden, hidden_out, tile_sems.at[0]).wait()
    pltpu.make_async_copy(middle_grad, middle_grad_out, tile_sems.at[1]).wait()


def pack(grads, half, target, at):
    for grad in grads:
        count = grad.shape[0] // 2
        rows = pl.ds(pl.multiple_of(half * count, count), count)
        for begin in range(0, grad.shape[1], LANES):
            target[pl.ds(at, count), :] = grad[rows, begin : begin + LANES].astype(BF16)
            at += count
    return at


def pack_turned(grad, half, target, at):
    count, columns = grad.shape[0], grad.shape[1] // 2
    for begin in range(0, columns, LANES):
        cols = pl.ds(pl.multiple_of(half * columns + begin, LANES), LANES)
        target[pl.ds(at, count), :] = grad[:, cols].astype(BF16)
        at += count
    return at


def pack_small(small, core, mine, other, at):
    rest = mine.shape[0] - at
    mine[pl.ds(at, rest), :] = jnp.zeros((rest, LANES), BF16)
    other[pl.ds(at, rest), :] = jnp.zeros((rest, LANES), BF16)
    for index in range(small.shape[1] // LANES):
        value = small[:, index * LANES : (index + 1) * LANES].astype(BF16)
        spot = pl.ds(at + (index // 2) * 16, 16)

        @pl.when(core == index % 2)
        def _():
            mine[spot, :] = value

        @pl.when(core != index % 2)
        def _():
            other[spot, :] = value


def step_copies(arrays, step, sems):
    spot = pl.ds(step * WIDE, WIDE)
    return [
        pltpu.make_async_copy(source.at[spot], target.at[spot], sems.at[step, at])
        for at, (source, target) in enumerate(arrays)
    ]


def leave(value_ref, own_out, halo_out, step, sems):
    rows = own_out.shape[0]
    begin, end = step * WIDE, (step + 1) * WIDE
    own = pl.ds(begin, min(rows, end) - begin)
    copies = [pltpu.make_async_copy(value_ref.at[own], own_out.at[own], sems.at[step, 6])]
    if end > rows:
        copies.append(pltpu.make_async_copy(value_ref.at[pl.ds(rows, end - rows)], halo_out, sems.at[step, 7]))
    for copy in copies:
        copy.start()
    return copies


def kernel_input(
    after, gain1, x_in, edge_in, w_in_in, triple_grad_in, middle_grad_in, out, out_halo,
    x, w_in, triple_grad, middle_grad, sems, step_sems,
):
    rows, width = x_in.shape
    total = x.shape[0]
    move = Mover(sems)
    early = [
        move.start(w_in_in, w_in),
        move.start(x_in, x.at[pl.ds(0, rows)]),
        move.start(edge_in, x.at[pl.ds(rows, TILE)]),
    ]
    arrays = ((triple_grad_in, triple_grad), (middle_grad_in, middle_grad))
    steps = range(total // WIDE)
    parts = [step_copies(arrays, step, step_sems) for step in steps]
    for part in parts:
        for copy in part:
            copy.start()
    for copy in early:
        copy.wait()
    leaving = []
    for step in steps:
        for copy in parts[step]:
            copy.wait()
        spot = pl.ds(step * WIDE, WIDE)
        scaled, inverse = normalize(x[spot, :].astype(F32))
        normed_grad = dot_nt(triple_grad[spot, :], w_in[...])
        middle_grad[spot, :] = middle_grad[spot, :] + normalize_back(normed_grad, scaled, inverse, row_of(gain1))
        leaving += leave(middle_grad, out, out_halo, step, step_sems)
    for copy in leaving:
        copy.wait()


def kernel_result(
    after, table, b_sh, middle_in, hidden_in, w_sh_in, out, out_halo, middle, hidden, w_sh, value, sems, step_sems,
):
    total = middle.shape[0]
    move = Mover(sems)
    weight_copy = move.start(w_sh_in, w_sh)
    arrays = ((middle_in, middle), (hidden_in, hidden))
    steps = range(total // WIDE)
    parts = [step_copies(arrays, step, step_sems) for step in steps]
    for part in parts:
        for copy in part:
            copy.start()
    weight_copy.wait()
    leaving = []
    for step in steps:
        for copy in parts[step]:
            copy.wait()
        spot = pl.ds(step * WIDE, WIDE)
        keep = interval(step, table[GROUPS, 1], table[GROUPS, 2], WIDE)
        row = middle[spot, :] + row_of(b_sh) + dot(hidden[spot, :], w_sh[...])
        value[spot, :] = jnp.where(keep, row, 0.0).astype(BF16)
        leaving += leave(value, out, out_halo, step, step_sems)
    for copy in leaving:
        copy.wait()


def kernel_add(mine_in, other_in, out, mine, other, sems):
    chunks = sems.shape[0]
    size = mine.shape[0] // chunks

    def copies(chunk):
        spot = pl.ds(chunk * size, size)
        return [
            pltpu.make_async_copy(mine_in.at[spot], mine.at[spot], sems.at[chunk, 0]),
            pltpu.make_async_copy(other_in.at[spot], other.at[spot], sems.at[chunk, 1]),
            pltpu.make_async_copy(mine.at[spot], out.at[spot], sems.at[chunk, 2]),
        ]

    for chunk in range(chunks):
        for copy in copies(chunk)[:2]:
            copy.start()
    for chunk in range(chunks):
        spot = pl.ds(chunk * size, size)
        arriving = copies(chunk)
        for copy in arriving[:2]:
            copy.wait()
        mine[spot, :] = (mine[spot, :].astype(F32) + other[spot, :].astype(F32)).astype(BF16)
        arriving[2].start()
    for chunk in range(chunks):
        copies(chunk)[2].wait()


def kernel_sum(extra, *refs):
    parts_in, out, parts, piece, sems = refs[extra:]
    count = parts.shape[0]
    quarter = max(count // 4, 1)
    copies = []
    for index, begin in enumerate(range(0, count, quarter)):
        spot = pl.ds(begin, quarter)
        copies.append(pltpu.make_async_copy(parts_in.at[spot], parts.at[spot], sems.at[index]))
        copies[-1].start()
    total = jnp.zeros(piece.shape, F32)
    for index, copy in enumerate(copies):
        copy.wait()
        for part in range(index * quarter, (index + 1) * quarter):
            total = total + parts[part].astype(F32)
    piece[...] = total.astype(BF16)
    for part in range(count):
        pltpu.make_async_copy(piece, out.at[part], sems.at[4]).start()
    pltpu.make_async_copy(parts, out, sems.at[4]).wait()


def kernel_unpack_half(half, packed_in, d_ex, d_out, d_in, d_sh, packed, ex, out, inward, sh, sems):
    arrays = ((ex, d_ex), (sh, d_sh), (out, d_out), (inward, d_in))
    sizes = [value.shape[0] * value.shape[1] // LANES for value, _target in arrays]
    begins = [sum(sizes[:index]) for index in range(4)]
    arriving = []
    for index in range(4):
        spot = pl.ds(begins[index], sizes[index])
        arriving.append(pltpu.make_async_copy(packed_in.at[spot], packed.at[spot], sems.at[index]))
        arriving[-1].start()
    leaving = []
    for index, (value, target) in enumerate(arrays):
        arriving[index].wait()
        at = begins[index]
        if index != 1:
            count = value.shape[0]
            for begin in range(0, value.shape[1], LANES):
                value[:, begin : begin + LANES] = packed[pl.ds(at, count), :].astype(F32)
                at += count
        else:
            count = value.shape[1]
            for begin in range(0, value.shape[0], LANES):
                value[begin : begin + LANES, :] = packed[pl.ds(at, count), :].astype(F32).T
                at += count
        rows = pl.ds(pl.multiple_of(half * value.shape[0], value.shape[0]), value.shape[0])
        leaving.append(pltpu.make_async_copy(value, target.at[rows], sems.at[4 + index]))
        leaving[-1].start()
    return leaving


def own_core():
    return lax.rem(lax.axis_index("dp"), 2)


def kernel_first_half(packed_in, *refs):
    for copy in kernel_unpack_half(own_core(), packed_in, *refs):
        copy.wait()


def kernel_second_half(
    packed_in, first_in, kept_ex, kept_out, kept_in, kept_sh,
    d_ex, d_out, d_in, d_sh, b_in, b_sh, gain2, shift2, b_out, b_ex, gain1, shift1,
    packed, ex, out, inward, sh, sems, mine, other, small_sems,
):
    del kept_ex, kept_out, kept_in, kept_sh
    rows = pl.ds(first_in.shape[0] - mine.shape[0], mine.shape[0])
    copies = [
        pltpu.make_async_copy(first_in.at[rows], mine, small_sems.at[0]),
        pltpu.make_async_copy(packed_in.at[rows], other, small_sems.at[1]),
    ]
    for copy in copies:
        copy.start()
    core = own_core()
    leaving = kernel_unpack_half(
        1 - core, packed_in, d_ex, d_out, d_in, d_sh, packed, ex, out, inward, sh, sems
    )
    for copy in copies:
        copy.wait()
    width, columns = b_sh.shape[0], b_ex.shape[0]
    swap = core == 1
    blocks = []
    for index in range(columns // LANES):
        spot = pl.ds(index // 2 * 16, 16)
        pair = mine[spot, :].astype(F32), other[spot, :].astype(F32)
        blocks.append(jnp.where(swap, pair[1 - index % 2], pair[index % 2]))
    small = jnp.concatenate(blocks, axis=1)
    for row, ref in ((0, b_sh), (1, gain2), (2, shift2), (3, b_out), (6, gain1), (7, shift1)):
        ref[...] = small[row, :width]
    b_ex[...] = small[4]
    b_in[0:1, :] = small[5:6, :width]
    b_in[1:2, :] = small[5:6, 2 * width : 3 * width]
    for copy in leaving:
        copy.wait()


def kernel_touch(*refs):
    del refs


VMEM = pl.BlockSpec(memory_space=pltpu.VMEM)
SMEM = pl.BlockSpec(memory_space=pltpu.SMEM)
ANY = pl.BlockSpec(memory_space=pl.ANY)


def params(mib):
    return pltpu.CompilerParams(vmem_limit_bytes=mib * 1024 * 1024)


def cost(flops, moved):
    return pl.CostEstimate(flops=int(flops), bytes_accessed=int(moved), transcendentals=0)


def shape(dims, dtype):
    return jax.ShapeDtypeStruct(dims, dtype)


def packed_rows(columns, small, pieces):
    half = columns // LANES * 192 + (small // LANES + 1) // 2 * 16
    return pieces * (-(-half // (8 * pieces)) * 8)


def attention_scratch(pairs):
    return [
        [pltpu.VMEM((pairs, WIN, 2 * WIN), F32)] * 2,
        [pltpu.VMEM((8, 2 * WIN), F32)] * 2,
        [pltpu.VMEM((pairs, 2 * WIN, WIN), BF16)] * 2,
        [pltpu.VMEM((8, 2 * WIN), F32)] * 2,
    ]


def own_part(segments, gain1, shift1, b_in, x, w_in):
    rows, width = x.shape
    total = rows + TILE
    pairs = width // (2 * HD)
    vmem = pltpu.VMEM
    return pl.pallas_call(
        kernel_own,
        out_shape=(
            shape((rows, 3 * width), BF16),
            shape((total, width), BF16),
            shape((rows, width), BF16),
            shape((GROUPS, pairs, 2 * WIN, WIN), BF16),
            shape((GROUPS, 8, WIN), F32),
            shape((GROUPS + 1, 8), jnp.int32),
        ),
        in_specs=[ANY] * 6,
        out_specs=(ANY, ANY, ANY, ANY, VMEM, SMEM),
        scratch_shapes=[
            vmem(segments.shape, jnp.int32),
            vmem(gain1.shape, F32),
            vmem(shift1.shape, F32),
            vmem(b_in.shape, F32),
            vmem((rows, width), BF16),
            vmem(w_in.shape, BF16),
            vmem((total, 3 * width), BF16),
            vmem((total, width), BF16),
            vmem((8, LANES), jnp.int32),
            pltpu.SMEM((8, LANES), jnp.int32),
            *attention_scratch(pairs),
            vmem((GROUPS, pairs, 2 * WIN, WIN), BF16),
            pltpu.SemaphoreType.DMA((16,)),
            pltpu.SemaphoreType.DMA((rows // OWN + 1,)),
        ],
        compiler_params=params(63),
        cost_estimate=cost(2 * 6 * rows * width * 3 * width, 1e7),
        name="own_part",
    )(segments, gain1, shift1, b_in, x, w_in)


def rest_part(table, vectors, x, cot, halo, triple, attended, scaled, raised, stats, w_in, w_out, w_ex, w_sh, pieces):
    rows, width = x.shape
    total = rows + TILE
    hidden = w_ex.shape[1]
    packed = packed_rows(2 * hidden + 4 * width, hidden, pieces)
    vmem = pltpu.VMEM
    pairs = width // (2 * HD)
    square, row = vmem((pairs, WIN, 2 * WIN), F32), vmem((8, 2 * WIN), F32)
    low = vmem((pairs, WIN, 2 * WIN), BF16)
    return pl.pallas_call(
        kernel_rest,
        out_shape=(
            shape((total, width), F32),
            shape((total, width), F32),
            shape((total, hidden), BF16),
            shape((total, 3 * width), BF16),
            shape((TILE, width), BF16),
            shape((packed, LANES), BF16),
            shape((packed, LANES), BF16),
        ),
        in_specs=[SMEM] + [ANY] * 19,
        out_specs=tuple([ANY] * 7),
        scratch_shapes=[
            vmem((total, width), BF16),
            vmem((total, width), BF16),
            vmem(w_in.shape, BF16),
            vmem(w_out.shape, BF16),
            vmem(w_ex.shape, BF16),
            vmem(w_sh.shape, BF16),
            vmem((total, 3 * width), BF16),
            vmem((total, width), BF16),
            vmem((total, width), F32),
            vmem((total, width), F32),
            vmem((total, width), BF16),
            vmem((total, hidden), BF16),
            vmem((total, 3 * width), BF16),
            vmem((GROUPS, 8, WIN), F32),
            vmem((width, hidden), F32),
            vmem((width, hidden), F32),
            vmem((width, width), F32),
            vmem((width, 3 * width), F32),
            vmem((16, 3 * width), F32),
            vmem((16, hidden), F32),
            [square],
            [row],
            [vmem((pairs, 2 * WIN, WIN), BF16)],
            [row],
            [vmem((pairs, 2 * HD, WIN), BF16)] * 2,
            [low] * 2,
            vmem((SLOTS, pairs, 2 * WIN, WIN), BF16),
            vmem((TILE, width), BF16),
            vmem((packed, LANES), BF16),
            vmem((packed, LANES), BF16),
            pltpu.SemaphoreType.DMA((40,)),
            pltpu.SemaphoreType.DMA((2,)),
            pltpu.SemaphoreType.DMA((SLOTS,)),
            *[vmem(v.shape, F32) for v in vectors],
        ],
        compiler_params=params(62),
        cost_estimate=cost(2 * 9 * rows * width * (3 * width + 8 * width), 3e7),
        name="rest_part",
    )(table, *vectors, x, cot, halo, triple, attended, scaled, raised, stats, w_in, w_out, w_ex, w_sh)


def input_gradient(after, gain1, x, halo, w_in, triple_grad, middle_grad):
    rows, width = x.shape
    total = triple_grad.shape[0]
    vmem = pltpu.VMEM
    return pl.pallas_call(
        kernel_input,
        out_shape=(shape((rows, width), F32), shape((TILE, width), F32)),
        in_specs=[ANY, VMEM] + [ANY] * 5,
        out_specs=(ANY, ANY),
        scratch_shapes=[
            vmem((total, width), BF16),
            vmem(w_in.shape, BF16),
            vmem((total, 3 * width), BF16),
            vmem((total, width), F32),
            pltpu.SemaphoreType.DMA((4,)),
            pltpu.SemaphoreType.DMA((total // WIDE, 8)),
        ],
        compiler_params=params(63),
        cost_estimate=cost(2 * rows * width * 9 * width, 1.4e7),
        name="input_gradient",
    )(after, gain1, x, halo, w_in, triple_grad, middle_grad)


def layer_result(after, table, b_sh, middle, hidden, w_sh):
    total, width = middle.shape
    vmem = pltpu.VMEM
    return pl.pallas_call(
        kernel_result,
        out_shape=(shape((total - TILE, width), BF16), shape((TILE, width), BF16)),
        in_specs=[ANY, SMEM, VMEM] + [ANY] * 3,
        out_specs=(ANY, ANY),
        scratch_shapes=[
            vmem(middle.shape, F32),
            vmem(hidden.shape, BF16),
            vmem(w_sh.shape, BF16),
            vmem(middle.shape, BF16),
            pltpu.SemaphoreType.DMA((2,)),
            pltpu.SemaphoreType.DMA((total // WIDE, 8)),
        ],
        compiler_params=params(63),
        cost_estimate=cost(2 * total * width * 8 * width, 1.3e7),
        name="layer_result",
    )(after, table, b_sh, middle, hidden, w_sh)


def add_halves(mine, other):
    return pl.pallas_call(
        kernel_add,
        out_shape=shape(mine.shape, BF16),
        in_specs=[ANY, ANY],
        out_specs=ANY,
        scratch_shapes=[
            pltpu.VMEM(mine.shape, BF16), pltpu.VMEM(mine.shape, BF16), pltpu.SemaphoreType.DMA((4, 3)),
        ],
        compiler_params=params(63),
        cost_estimate=cost(mine.size, mine.size * 6),
        name="add_halves",
    )(mine, other)


def sum_parts(after, parts):
    return pl.pallas_call(
        partial(kernel_sum, len(after)),
        out_shape=shape(parts.shape, BF16),
        in_specs=[ANY] * (len(after) + 1),
        out_specs=ANY,
        scratch_shapes=[
            pltpu.VMEM(parts.shape, BF16),
            pltpu.VMEM(parts.shape[1:], BF16),
            pltpu.SemaphoreType.DMA((5,)),
        ],
        compiler_params=params(63),
        cost_estimate=cost(parts.size, parts.size * 4),
        name="sum_parts",
    )(*after, parts)


def half_shapes(width, hidden):
    dims = ((width, hidden), (width, width), (width, 3 * width), (hidden, width))
    scratch = [pltpu.VMEM((rows // 2, columns), F32) for rows, columns in dims]
    return tuple(shape(dim, F32) for dim in dims), [*scratch, pltpu.SemaphoreType.DMA((8,))]


def unpack_first(packed, width, hidden):
    shapes, scratch = half_shapes(width, hidden)
    return pl.pallas_call(
        kernel_first_half,
        out_shape=shapes,
        in_specs=[ANY],
        out_specs=(ANY,) * 4,
        scratch_shapes=[pltpu.VMEM(packed.shape, BF16), *scratch],
        compiler_params=params(63),
        cost_estimate=cost(packed.size, packed.size * 6),
        name="unpack_first",
    )(packed)


def unpack_second(packed, first, kept, used, width, hidden):
    shapes, scratch = half_shapes(width, hidden)
    rows = first.shape[0] - used
    small = tuple(shape(dims, F32) for dims in ((2, width),) + ((width,),) * 4 + ((hidden,), (width,), (width,)))
    return pl.pallas_call(
        kernel_second_half,
        out_shape=shapes + small,
        in_specs=[ANY] * 6,
        out_specs=(ANY,) * 4 + (VMEM,) * 8,
        scratch_shapes=[
            pltpu.VMEM(packed.shape, BF16), *scratch, pltpu.VMEM((rows, LANES), BF16), pltpu.VMEM((rows, LANES), BF16),
            pltpu.SemaphoreType.DMA((2,)),
        ],
        input_output_aliases={2: 0, 3: 1, 4: 2, 5: 3},
        compiler_params=params(63),
        cost_estimate=cost(packed.size, packed.size * 6),
        name="unpack_second",
    )(packed, first, *kept)


def touch(value, *after):
    return pl.pallas_call(
        kernel_touch,
        out_shape=shape(value.shape, value.dtype),
        in_specs=[ANY] * (1 + len(after)),
        out_specs=ANY,
        input_output_aliases={0: 0},
        name="touch",
    )(value, *after)


def same_core_groups():
    packs, parts = lax.axis_size("dp"), lax.axis_size("mp")
    return [[d * parts + m for d in range(c, packs, 2) for m in range(parts)] for c in range(2)]


def swap_cores(block):
    packs = lax.axis_size("dp")
    return lax.ppermute(block, "dp", [(i, i ^ 1) for i in range(packs)])


def exchange(parts):
    return lax.all_to_all(parts, ("dp", "mp"), 0, 0, axis_index_groups=same_core_groups())


def passed(block, distance):
    count = lax.axis_size("mp")
    route = [(i, i + distance) for i in range(count) if 0 <= i + distance < count]
    return lax.ppermute(block, "mp", route)


def kernel_take_over(table, own_in, other_in, own_out, own, other, sems):
    rows = pl.ds(0, HALO)
    copies = [
        pltpu.make_async_copy(own_in.at[rows], own, sems.at[0]), pltpu.make_async_copy(other_in, other, sems.at[1])
    ]
    for copy in copies:
        copy.start()
    for copy in copies:
        copy.wait()
    row = lax.broadcasted_iota(jnp.int32, (HALO, 1), 0)
    mixed = jnp.where(row < table[GROUPS, 1], other[...].astype(F32), own[...].astype(F32))
    own[...] = mixed.astype(own.dtype)
    copy = pltpu.make_async_copy(own, own_out.at[rows], sems.at[2])
    copy.start()
    copy.wait()


def take_over(table, own, other):
    return pl.pallas_call(
        kernel_take_over,
        out_shape=shape(own.shape, own.dtype),
        in_specs=[SMEM, ANY, ANY],
        out_specs=ANY,
        scratch_shapes=[
            pltpu.VMEM(other.shape, own.dtype), pltpu.VMEM(other.shape, own.dtype), pltpu.SemaphoreType.DMA((3,)),
        ],
        input_output_aliases={1: 0},
        compiler_params=params(63),
        name="take_over",
    )(table, own, other)


def body(
    layer_input, segments, cotangent, first_gain, first_shift, inward_weight, inward_bias, outward_weight,
    outward_bias, second_gain, second_shift, expand_weight, expand_bias, shrink_weight, shrink_bias,
):
    rows, width = layer_input.shape
    hidden_width = expand_weight.shape[1]
    pieces = lax.axis_size("dp") * lax.axis_size("mp") // 2
    gain1, shift1, b_out, gain2, shift2, b_ex, b_sh = (
        first_gain, first_shift, outward_bias, second_gain, second_shift, expand_bias, shrink_bias
    )
    halo = passed(jnp.concatenate([layer_input[:HALO], cotangent[:HALO]], axis=1), -1)
    triple, attended, scaled, raised, stats, table = own_part(
        segments, gain1, shift1, inward_bias, layer_input, inward_weight
    )
    middle, middle_grad, hidden, triple_grad, edge, mine, other = rest_part(
        table, (gain1, shift1, inward_bias, b_out, gain2, shift2, b_ex), layer_input, cotangent, halo, triple,
        attended, scaled, raised, stats, inward_weight, outward_weight, expand_weight, shrink_weight, pieces,
    )
    both = add_halves(mine, swap_cores(other))
    parts = exchange(both.reshape(pieces, -1, LANES))
    input_grad, input_halo = input_gradient(both, gain1, layer_input, edge, inward_weight, triple_grad, middle_grad)
    result, result_halo = layer_result(input_halo, table, b_sh, middle, hidden, shrink_weight)
    input_other = passed(input_halo[:HALO], 1)
    summed = sum_parts((input_other, result_halo), parts)
    mine = exchange(summed).reshape(-1, LANES)
    input_grad = take_over(table, input_grad, touch(input_other, summed))
    result = take_over(table, result, passed(touch(result_halo, summed)[:HALO], 1))
    mine = touch(mine, input_grad, result)
    other = swap_cores(mine)
    used = 192 * (2 * hidden_width + 4 * width) // LANES
    half = unpack_first(mine, width, hidden_width)
    d_ex, d_out, d_in, d_sh, d_b_in, d_b_sh, d_gain2, d_shift2, d_b_out, d_b_ex, d_gain1, d_shift1 = unpack_second(
        other, mine, half, used, width, hidden_width
    )
    return (
        result, input_grad, d_gain1, d_shift1, d_in, d_b_in, d_out, d_b_out, d_gain2, d_shift2, d_ex, d_b_ex, d_sh,
        d_b_sh,
    )


def solution(mesh):
    rows = P(("dp", "mp"), None)
    in_specs = (rows, P("dp", None), rows) + (P(),) * 12
    out_specs = (rows, rows) + (P(),) * 12
    return jax.shard_map(body, mesh=mesh, in_specs=in_specs, out_specs=out_specs, check_vma=False)
```

```python
from functools import partial

import jax
import jax.numpy as jnp
from jax import lax
from jax.experimental import pallas as pl
from jax.experimental.pallas import tpu as pltpu
from jax.sharding import PartitionSpec as P

HD = 64
SEQ = 198
EPSILON = 1e-06
MASKED = -1000000000.0
LOG2E = 1.4426950408889634
WIN = 256
TILE = 256
HALO = 208
WIDE = 768
OWN = 1024
GROUPS = 24
SLOTS = 5
LANES = 128
CHUNK = 256
FEED = 768
BIG = 1 << 20
F32 = jnp.float32
BF16 = jnp.bfloat16
NT = (((1,), (1,)), ((), ()))
TN = (((0,), (0,)), ((), ()))


def row_of(ref):
    return ref[...].reshape(1, -1)


def dot(a, b):
    return jnp.dot(a, b, preferred_element_type=F32)


def dot_nt(a, b):
    return lax.dot_general(a, b, NT, preferred_element_type=F32)


def dot_tn(a, b):
    return lax.dot_general(a, b, TN, preferred_element_type=F32)


def normalize(rows):
    center = jnp.mean(rows, axis=-1, keepdims=True)
    centred = rows - center
    spread = jnp.mean(centred * centred, axis=-1, keepdims=True)
    inverse = lax.rsqrt(spread + EPSILON)
    return centred * inverse, inverse


def normalize_back(upstream, scaled, inverse, gain):
    direct = upstream * gain
    first = jnp.mean(direct, axis=-1, keepdims=True)
    second = jnp.mean(direct * scaled, axis=-1, keepdims=True)
    return inverse * (direct - first - scaled * second)


def gelu_parts(v, half_upstream):
    scaled = v * 0.7071067811865476
    double = 1.0 + lax.erf(scaled)
    bell = jnp.exp2((scaled * scaled) * -1.4426950408889634)
    return (0.5 * v) * double, half_upstream * (double + (v * 0.7978845608028654) * bell)


def image_ends(seg, base, work):
    ident = lax.broadcasted_iota(jnp.int32, (LANES, LANES), 0)
    below = jnp.zeros((LANES, LANES), F32)
    for begin in range(0, seg.shape[1], LANES):
        row = seg[0:1, begin : begin + LANES]
        row = jnp.where(row < 0, BIG, row)
        below = below + jnp.where(row <= ident, 1.0, 0.0)
    ends = jnp.broadcast_to(jnp.sum(below, axis=1, keepdims=True), (LANES, LANES))
    started = jnp.sum(jnp.where(ends < base.astype(F32), 1.0, 0.0), axis=0, keepdims=True)
    work[0:1, :] = ends.T[0:1].astype(jnp.int32)
    work[1:2, :] = started.astype(jnp.int32)


def plan_groups(ends, position, rows, table):
    base = position * rows
    limit = jnp.minimum(base + rows, ends[0, LANES - 1]) - base
    image = jnp.where(position == 0, 0, ends[1, 0] + 1)
    first = jnp.where(position == 0, 0, ends[0, jnp.maximum(image - 1, 0)]) - base

    def body(state):
        at, image, group, window, start, c1, c2 = state
        after = ends[0, jnp.minimum(image, LANES - 1)] - base
        fits = after - window <= WIN

        @pl.when(jnp.logical_not(fits))
        def _():
            write_group(table, group, window, start, c1, c2, at)

        group = jnp.where(fits, group, group + 1)
        new_c1 = jnp.where(fits, jnp.where(at == start, c1, jnp.where(c1 < 0, at, c1)), -1)
        new_c2 = jnp.where(fits, jnp.where(jnp.logical_and(at != start, c1 >= 0), jnp.where(c2 < 0, at, c2), c2), -1)
        start = jnp.where(fits, start, at)
        window = jnp.where(fits, window, (at // 16) * 16)
        return after, image + 1, group, window, start, new_c1, new_c2

    init = (first, image, jnp.int32(0), (first // 16) * 16, first, jnp.int32(-1), jnp.int32(-1))
    at, image, group, window, start, c1, c2 = lax.while_loop(lambda s: s[0] < limit, body, init)
    write_group(table, group, window, start, c1, c2, at)
    table[GROUPS, 0] = group + 1
    table[GROUPS, 1] = first
    table[GROUPS, 2] = at


def write_group(table, group, window, start, c1, c2, end):
    table[group, 0] = window
    table[group, 1] = start - window
    table[group, 2] = jnp.where(c1 < 0, end, c1) - window
    table[group, 3] = jnp.where(c2 < 0, end, c2) - window
    table[group, 4] = end - window


def group_bias(table, group):
    bounds = [table[group, i] for i in range(1, 5)]
    row = lax.broadcasted_iota(jnp.int32, (WIN, LANES), 0)
    col = lax.broadcasted_iota(jnp.int32, (1, WIN), 1)

    def ident(index):
        return sum((index >= b).astype(jnp.int32) for b in bounds)

    row, col = ident(row), ident(col)
    return jnp.concatenate(
        [jnp.where(row == col[:, at : at + LANES], 0.0, MASKED) for at in range(0, WIN, LANES)], axis=1
    )


def group_mask_factors(table, group):
    bounds = [table[group, i] for i in range(1, 5)]

    def ident(index):
        return sum((index >= b).astype(jnp.int32) for b in bounds)

    row = ident(lax.broadcasted_iota(jnp.int32, (WIN, LANES), 0))
    left = jnp.where(row == lax.broadcasted_iota(jnp.int32, (WIN, LANES), 1), 1.0, 0.0).astype(BF16)
    col = ident(lax.broadcasted_iota(jnp.int32, (1, WIN), 1))
    kind = lax.broadcasted_iota(jnp.int32, (16, WIN), 0)
    right = jnp.where(kind == col, 0.0, MASKED).astype(BF16)
    right = jnp.concatenate([right, jnp.zeros((LANES - 16, WIN), BF16)], axis=0)
    return left, jnp.concatenate([right, right], axis=1)


def head_masks():
    lane = lax.broadcasted_iota(jnp.int32, (WIN, 2 * HD), 1)
    return lane < HD, lane >= HD


def keep_first(ref, window, begin, cols, value):
    head = pl.ds(window, 16)
    old = ref[head, cols]
    row = lax.broadcasted_iota(jnp.int32, (16, 2 * HD), 0)
    ref[head, cols] = jnp.where(row >= begin, value[:16].astype(F32), old.astype(F32)).astype(BF16)
    ref[pl.ds(window + 16, WIN - 16), cols] = value[16:].astype(BF16)


def block_diagonal(pair_t):
    zero = jnp.zeros((HD, pair_t.shape[1]), pair_t.dtype)
    return jnp.concatenate(
        [jnp.concatenate([pair_t[:HD], zero], axis=1), jnp.concatenate([zero, pair_t[HD:]], axis=1)], axis=0
    )


def pipelined(groups, first, second, third, keep_copy):
    def clamped(group):
        return jnp.minimum(group, groups - 1)

    def half(group, slot):
        first(clamped(group), slot)
        second(clamped(group - 1), 1 - slot)
        third(clamped(group - 2), slot)

    first(0, 0)
    first(clamped(1), 1)
    second(0, 0)
    steps = (groups + 1) // 2

    def both(step, _):
        keep_copy(clamped(2 * step)).start()

        @pl.when(step > 0)
        def _():
            keep_copy(clamped(2 * step - 1)).start()

        half(2 * step + 2, 0)
        half(2 * step + 3, 1)
        return 0

    lax.fori_loop(0, steps, both, 0)
    keep_copy(clamped(2 * steps - 1)).start()

    def settle(_, carry):
        keep_copy(0).wait()
        return carry

    return lambda: lax.fori_loop(0, 2 * steps, settle, 0)


def group_rows(table, group):
    return pl.ds(pl.multiple_of(table[group, 0], 16), WIN)


def attend_groups(groups, table, triple, attended, stats, scores, peaks, raised, scales, alone=None, kept=None, keep_copy=None):
    width = attended.shape[1]
    pairs = range(width // (2 * HD))

    def first(group, slot):
        rows = group_rows(table, group)
        left, right = group_mask_factors(table, group)
        for pair in pairs:
            query_t = triple[rows, pl.ds(pair * 2 * HD, 2 * HD)].T
            key = triple[rows, pl.ds(width + pair * 2 * HD, 2 * HD)]
            value = dot(
                jnp.concatenate([key, left], axis=1), jnp.concatenate([block_diagonal(query_t), right], axis=0)
            )
            scores[slot][pair] = value
            peaks[slot][pair : pair + 1, :] = jnp.max(value, axis=0, keepdims=True)

    def second(group, slot):
        for pair in pairs:
            peak = peaks[slot][pair : pair + 1, :]
            value = jnp.exp2(scores[slot][pair] - peak)
            total = jnp.sum(value, axis=0, keepdims=True)
            low = value.astype(BF16)
            raised[slot][pair, :WIN] = low[:, :WIN]
            raised[slot][pair, WIN:] = low[:, WIN:]
            if kept is not None:
                kept[group, pair, :WIN] = low[:, :WIN]
                kept[group, pair, WIN:] = low[:, WIN:]
            scale = 1.0 / total
            scales[slot][pair : pair + 1, :] = scale
            stats[group, pl.ds(2 * pair, 1), :] = scale[:, :WIN]
            stats[group, pl.ds(2 * pair + 1, 1), :] = scale[:, WIN:]

    def third(group, slot):
        rows = group_rows(table, group)
        for pair in pairs:
            value_t = block_diagonal(triple[rows, pl.ds(2 * width + pair * 2 * HD, 2 * HD)].T)
            out = dot(value_t, raised[slot][pair])
            scale = scales[slot][pair : pair + 1, :]
            out = jnp.concatenate([out[:HD] * scale[:, :WIN], out[HD:] * scale[:, WIN:]], axis=0)
            keep_first(attended, rows.start, table[group, 1], pl.ds(pair * 2 * HD, 2 * HD), out.T)

    if alone is None:
        return pipelined(groups, first, second, third, keep_copy)
    for part in (first, second, third):
        part(alone, 0)
    return None


def attend_back_groups(
    groups, table, triple, attended, upstream, stats, triple_grad, scores_grads, scaled_up, kept, kept_copy
):
    width = attended.shape[1]
    pairs = range(width // (2 * HD))
    masks = head_masks()

    def columns(pair, block):
        return pl.ds(block * width + pair * 2 * HD, 2 * HD)

    def side_by_side(turn, pair):
        low = kept[lax.rem(turn, SLOTS), pair]
        return jnp.concatenate([low[:WIN], low[WIN:]], axis=1)

    def first(turn, group, slot):
        rows = group_rows(table, group)
        for pair in pairs:
            scale = [jnp.broadcast_to(stats[group, pl.ds(2 * pair + h, 1), :], (HD, WIN)) for h in range(2)]
            up_t = upstream[rows, columns(pair, 0)].T.astype(F32) * jnp.concatenate(scale, axis=0)
            product = attended[rows, columns(pair, 0)].T.astype(F32) * up_t
            agreement = jnp.concatenate(
                [jnp.sum(product[:HD], axis=0, keepdims=True), jnp.sum(product[HD:], axis=0, keepdims=True)], axis=1
            )
            up_low = up_t.astype(BF16)
            scaled_up[slot][pair] = up_low
            probs_grad = dot(triple[rows, columns(pair, 2)], block_diagonal(up_low))
            prob = side_by_side(turn, pair).astype(F32)
            scores_grads[slot][pair] = (prob * (probs_grad - agreement)).astype(BF16)

    def stacked(pair_rows):
        zero = jnp.zeros_like(pair_rows)
        return jnp.concatenate([jnp.where(mask, pair_rows, zero) for mask in masks], axis=0)

    def second(turn, group, slot):
        rows = group_rows(table, group)
        window, begin = rows.start, table[group, 1]
        for pair in pairs:
            scores_grad = scores_grads[slot][pair]
            value_grad = dot_nt(side_by_side(turn, pair), block_diagonal(scaled_up[slot][pair]))
            key_grad = dot(scores_grad, stacked(triple[rows, columns(pair, 0)]))
            key_t = block_diagonal(triple[rows, columns(pair, 1)].T)
            query_grad = dot(key_t, jnp.concatenate([scores_grad[:, :WIN], scores_grad[:, WIN:]], axis=0))
            keep_first(triple_grad, window, begin, columns(pair, 0), (query_grad * HD ** (-0.5)).T)
            keep_first(triple_grad, window, begin, columns(pair, 1), key_grad * (1.0 / LOG2E))
            keep_first(triple_grad, window, begin, columns(pair, 2), value_grad)

    def clamped(turn):
        return jnp.minimum(turn, groups - 1)

    def half(turn, slot):
        first(turn, clamped(turn), slot)
        second(turn - 1, clamped(turn - 1), 1 - slot)

    steps = (groups + 1) // 2

    def fetch(turn):
        kept_copy(clamped(turn), lax.rem(turn, SLOTS))

    def arrived(turn):
        kept_copy(None, lax.rem(turn, SLOTS))

    arrived(jnp.int32(0))
    first(jnp.int32(0), 0, 0)

    def both(step, _):
        @pl.when(step + 1 < steps)
        def _():
            fetch(2 * step + 3)
            fetch(2 * step + 4)

        arrived(2 * step + 1)
        arrived(2 * step + 2)
        half(2 * step + 1, 1)
        half(2 * step + 2, 0)
        return 0

    lax.fori_loop(0, steps, both, 0)


def interval(tile, first, end, size=TILE):
    row = lax.broadcasted_iota(jnp.int32, (size, 1), 0) + tile * size
    return jnp.logical_and(row >= first, row < end)


class Mover:
    def __init__(self, sems):
        self.sems = sems
        self.count = 0

    def start(self, source, target):
        copy = pltpu.make_async_copy(source, target, self.sems.at[self.count])
        self.count += 1
        copy.start()
        return copy


def project_rows(rows, gain1, shift1, w_in, b_in, target, spot, scaled_ref, scaled_spot):
    width = rows.shape[1]
    scaled, _inverse = normalize(rows)
    scaled_ref[scaled_spot, :] = scaled.astype(BF16)
    normed = (scaled * row_of(gain1) + row_of(shift1)).astype(BF16)
    q = dot(normed, w_in[:, :width]) + b_in[0:1, :]
    target[spot, :width] = (q.astype(BF16).astype(F32) * (HD ** (-0.5) * LOG2E)).astype(BF16)
    target[spot, width : 2 * width] = dot(normed, w_in[:, width : 2 * width]).astype(BF16)
    target[spot, 2 * width :] = (dot(normed, w_in[:, 2 * width :]) + b_in[1:2, :]).astype(BF16)


def kernel_own(
    seg_in, gain1_in, shift1_in, b_in_in, x_in, w_in_in,
    triple_out, attended_out, scaled_out, raised_out, stats, table,
    seg, gain1, shift1, b_in, x, w_in, triple, attended, work, ends, scores, peaks, raised, scales, kept, sems, tile_sems,
):
    rows, width = x_in.shape
    move = Mover(sems)
    seg_copy = move.start(seg_in, seg)
    early = [
        move.start(gain1_in, gain1), move.start(shift1_in, shift1), move.start(b_in_in, b_in),
        move.start(x_in, x), move.start(w_in_in, w_in),
    ]
    seg_copy.wait()
    image_ends(seg, lax.axis_index("mp") * rows, work)
    end_copy = move.start(work, ends)
    attended[...] = jnp.zeros_like(attended)
    spare = pl.ds(rows, triple.shape[0] - rows)
    triple[spare, :] = jnp.zeros((triple.shape[0] - rows, 3 * width), BF16)
    for copy in early:
        copy.wait()

    def step_copy(step):
        spot = pl.ds(pl.multiple_of(step * OWN, OWN), OWN)
        return pltpu.make_async_copy(triple.at[spot], triple_out.at[spot], tile_sems.at[step])

    def step_rows(step, _):
        spot = pl.ds(pl.multiple_of(step * OWN, OWN), OWN)
        project_rows(x[spot, :].astype(F32), gain1, shift1, w_in, b_in, triple, spot, x, spot)
        step_copy(step).start()
        return 0

    lax.fori_loop(0, rows // OWN, step_rows, 0)
    scaled_copy = move.start(x, scaled_out)
    end_copy.wait()
    plan_groups(ends, lax.axis_index("mp"), rows, table)

    def keep_copy(group):
        return pltpu.make_async_copy(kept.at[group], raised_out.at[group], tile_sems.at[rows // OWN])

    settle = attend_groups(
        jnp.maximum(table[GROUPS, 0] - 1, 1), table, triple, attended, stats, scores, peaks, raised, scales,
        kept=kept, keep_copy=keep_copy,
    )
    leaving = move.start(attended, attended_out)
    scaled_copy.wait()
    settle()
    for step in range(rows // OWN):
        step_copy(step).wait()
    leaving.wait()


def kernel_rest(
    table, *refs
):
    vectors_in, refs = refs[:7], refs[7:]
    vectors, refs = refs[-7:], refs[:-7]
    rest_body(table, vectors_in, vectors, *refs)


def rest_body(
    table, vectors_in, vectors,
    x_in, cot_in, halo_in, triple_in, attended_in, scaled_in, raised_in, stats_in, w_in_in, w_out_in, w_ex_in, w_sh_in,
    middle_out, middle_grad_out, hidden_out, triple_grad_out, edge_out, mine_out, other_out,
    x, back, w_in, w_out, w_ex, w_sh, triple, attended, middle, middle_grad, upstream, hidden, triple_grad, stats,
    d_ex, d_sh, d_out, product, sums, small, scores, peaks, raised, scales, scaled_up, scores_grads,
    kept, edge, mine, other, sems, tile_sems, kept_sems,
):
    rows, width = x_in.shape
    total = x.shape[0]
    tiles = total // FEED
    normed2, normed_grad = upstream, middle_grad
    move = Mover(sems)
    own, over = pl.ds(0, rows), pl.ds(rows, HALO)
    gain1, shift1, b_in, b_out, gain2, shift2, b_ex = vectors
    near, far = pl.ds(2 * WIDE, rows - 2 * WIDE), pl.ds(0, 2 * WIDE)
    first_copies = [move.start(halo_in.at[pl.ds(0, HALO)], x.at[over])]
    first_copies += [move.start(source, target) for source, target in zip(vectors_in, vectors)]
    first_copies.append(move.start(w_in_in, w_in))
    early = [
        move.start(triple_in.at[near], triple.at[near]),
        move.start(stats_in, stats),
        move.start(attended_in, attended),
    ]
    late = [
        move.start(w_out_in, w_out),
        move.start(x_in, x.at[own]),
        move.start(cot_in, back.at[own]),
        move.start(halo_in.at[pl.ds(HALO, HALO)], back.at[over]),
    ]
    weight_copies = [move.start(w_ex_in, w_ex), move.start(w_sh_in, w_sh)]
    last = move.start(triple_in.at[far], triple.at[far])
    rest = pl.ds(rows + HALO, total - rows - HALO)
    x[rest, :] = jnp.zeros((total - rows - HALO, width), BF16)
    back[rest, :] = jnp.zeros((total - rows - HALO, width), BF16)
    for ref in (d_ex, d_sh, d_out, product, sums, small, triple_grad):
        ref[...] = jnp.zeros_like(ref)
    groups, first, end = table[GROUPS, 0], table[GROUPS, 1], table[GROUPS, 2]
    for copy in first_copies:
        copy.wait()
    tail = pl.ds(rows, TILE)
    edge_copy = move.start(x.at[tail], edge_out)
    project_rows(x[tail, :].astype(F32), gain1, shift1, w_in, b_in, triple, tail, edge, slice(None))
    for copy in early:
        copy.wait()
    attend_groups(groups, table, triple, attended, stats, scores, peaks, raised, scales, alone=groups - 1)
    def kept_copy(group, slot):
        if group is None:
            pltpu.make_async_copy(raised[0], kept.at[slot], kept_sems.at[slot]).wait()
            return

        @pl.when(group == groups - 1)
        def _():
            pltpu.make_async_copy(raised[0], kept.at[slot], kept_sems.at[slot]).start()

        @pl.when(group != groups - 1)
        def _():
            pltpu.make_async_copy(raised_in.at[group], kept.at[slot], kept_sems.at[slot]).start()

    for turn in range(3):
        kept_copy(jnp.int32(turn), turn)
    for copy in late:
        copy.wait()
    leaving = []

    hidden_width = w_ex.shape[1]
    begins = list(range(0, hidden_width, CHUNK))

    def wide_rows(step):
        return pl.ds(pl.multiple_of(step * WIDE, WIDE), WIDE)

    def before_feed(step, _):
        spot = wide_rows(step)
        value = x[spot, :].astype(F32) + dot(attended[spot, :], w_out[...]) + row_of(b_out)
        scaled, _inverse = normalize(value)
        middle[spot, :] = value
        normed2[spot, :] = (scaled * row_of(gain2) + row_of(shift2)).astype(BF16)
        keep = interval(step, first, end, WIDE)
        back[spot, :] = jnp.where(keep, back[spot, :].astype(F32), 0.0).astype(BF16)
        return 0

    def feed(tile, _):
        spot = pl.ds(pl.multiple_of(tile * FEED, FEED), FEED)
        normed = normed2[spot, :]
        back_low = back[spot, :]
        back_half = (0.5 * back_low.astype(F32)).astype(BF16)

        def first_part(begin):
            cols = slice(begin, begin + CHUNK)
            before = dot(normed, w_ex[:, cols]) + b_ex[cols].reshape(1, -1)
            return before, dot_nt(back_half, w_sh[cols, :])

        held = [first_part(begins[0])]
        total_grad = jnp.zeros((width, FEED), F32)
        for index, begin in enumerate(begins):
            cols = slice(begin, begin + CHUNK)
            if index + 1 < len(begins):
                held.append(first_part(begins[index + 1]))
            value, grad = gelu_parts(*held[index])
            value, grad = value.astype(BF16), grad.astype(BF16)
            hidden[spot, cols] = value
            total_grad = total_grad + dot_nt(w_ex[:, cols], grad)
            d_sh[:, cols] += dot_tn(back_low, value)
            d_ex[:, cols] += dot_tn(normed, grad)
            small[4:5, cols] += jnp.sum(grad.astype(F32), axis=0, keepdims=True)
        normed_grad[spot, :] = total_grad.T
        pltpu.make_async_copy(hidden.at[spot], hidden_out.at[spot], tile_sems.at[0]).start()
        return 0

    def after_feed(step, _):
        spot = wide_rows(step)
        back32 = back[spot, :].astype(F32)
        scaled, inverse = normalize(middle[spot, :])
        upstream2 = normed_grad[spot, :]
        small[0:1, :width] += jnp.sum(back32, axis=0, keepdims=True)
        small[1:2, :width] += jnp.sum(upstream2 * scaled, axis=0, keepdims=True)
        small[2:3, :width] += jnp.sum(upstream2, axis=0, keepdims=True)
        grad = back32 + normalize_back(upstream2, scaled, inverse, row_of(gain2))
        small[3:4, :width] += jnp.sum(grad, axis=0, keepdims=True)
        middle_grad[spot, :] = grad
        grad_low = grad.astype(BF16)
        d_out[...] += dot_tn(attended[spot, :], grad_low)
        upstream[spot, :] = dot_nt(grad_low, w_out[...]).astype(BF16)
        pltpu.make_async_copy(middle_grad.at[spot], middle_grad_out.at[spot], tile_sems.at[1]).start()
        return 0

    lax.fori_loop(0, total // WIDE, before_feed, 0)
    for copy in weight_copies:
        copy.wait()
    edge_copy.wait()
    scaled_copy = move.start(scaled_in, x.at[own])
    x[tail, :] = edge[...]
    leaving.append(move.start(middle, middle_out))
    lax.fori_loop(0, tiles, feed, 0)
    lax.fori_loop(0, total // WIDE, after_feed, 0)
    core = lax.rem(lax.axis_index("dp"), 2)
    for half, target in ((core, mine), (1 - core, other)):
        at = pack((d_out,), half, target, pack_turned(d_sh, half, target, pack((d_ex,), half, target, 0)))
    ready = pl.ds(0, at)
    leaving += [move.start(mine.at[ready], mine_out.at[ready]), move.start(other.at[ready], other_out.at[ready])]
    last.wait()
    attend_back_groups(
        groups, table, triple, attended, upstream, stats, triple_grad, scores_grads, scaled_up, kept, kept_copy
    )
    leaving.append(move.start(triple_grad, triple_grad_out))
    scaled_copy.wait()
    ones = jnp.ones((16, WIDE), BF16)

    def multiply(step, _):
        spot = wide_rows(step)
        grad = triple_grad[spot, :]
        product[...] += dot_tn(x[spot, :], grad)
        sums[...] += dot(ones, grad)
        return 0

    lax.fori_loop(0, total // WIDE, multiply, 0)
    gain = jnp.broadcast_to(row_of(gain1), (LANES, width)).T
    shift = jnp.broadcast_to(row_of(shift1), (LANES, width)).T
    by_gain = jnp.zeros((width, LANES), F32)
    by_shift = jnp.zeros((width, LANES), F32)
    for begin in range(0, 3 * width, LANES):
        cols = slice(begin, begin + LANES)
        block, sum_row = product[:, cols], sums[0:1, cols]
        weight = w_in[:, cols].astype(F32)
        by_gain = by_gain + weight * block
        by_shift = by_shift + weight * sum_row
        product[:, cols] = gain * block + shift * sum_row
    small[5:6, : 3 * width] = sums[0:1, :]
    by_gain = jnp.broadcast_to(jnp.sum(by_gain, axis=1, keepdims=True), (width, LANES)).T
    by_shift = jnp.broadcast_to(jnp.sum(by_shift, axis=1, keepdims=True), (width, LANES)).T
    small[6:7, :width] = by_gain[0:1]
    small[7:8, :width] = by_shift[0:1]
    begin = at
    for half, target in ((core, mine), (1 - core, other)):
        at = pack((product,), half, target, begin)
    pack_small(small, core, mine, other, at)
    ready = pl.ds(begin, mine.shape[0] - begin)
    leaving += [move.start(mine.at[ready], mine_out.at[ready]), move.start(other.at[ready], other_out.at[ready])]
    for copy in leaving:
        copy.wait()
    pltpu.make_async_copy(hidden, hidden_out, tile_sems.at[0]).wait()
    pltpu.make_async_copy(middle_grad, middle_grad_out, tile_sems.at[1]).wait()


def pack(grads, half, target, at):
    for grad in grads:
        count = grad.shape[0] // 2
        rows = pl.ds(pl.multiple_of(half * count, count), count)
        for begin in range(0, grad.shape[1], LANES):
            target[pl.ds(at, count), :] = grad[rows, begin : begin + LANES].astype(BF16)
            at += count
    return at


def pack_turned(grad, half, target, at):
    count, columns = grad.shape[0], grad.shape[1] // 2
    for begin in range(0, columns, LANES):
        cols = pl.ds(pl.multiple_of(half * columns + begin, LANES), LANES)
        target[pl.ds(at, count), :] = grad[:, cols].astype(BF16)
        at += count
    return at


def pack_small(small, core, mine, other, at):
    rest = mine.shape[0] - at
    mine[pl.ds(at, rest), :] = jnp.zeros((rest, LANES), BF16)
    other[pl.ds(at, rest), :] = jnp.zeros((rest, LANES), BF16)
    for index in range(small.shape[1] // LANES):
        value = small[:, index * LANES : (index + 1) * LANES].astype(BF16)
        spot = pl.ds(at + (index // 2) * 16, 16)

        @pl.when(core == index % 2)
        def _():
            mine[spot, :] = value

        @pl.when(core != index % 2)
        def _():
            other[spot, :] = value


def step_copies(arrays, step, sems, skip=0):
    spot = pl.ds(step * WIDE, WIDE)
    return [
        pltpu.make_async_copy(source.at[spot], target.at[spot], sems.at[step, skip + at])
        for at, (source, target) in enumerate(arrays)
    ]


def leave(value_ref, own_out, step, sem):
    rows = own_out.shape[0]
    begin = step * WIDE
    own = pl.ds(begin, min(rows, begin + WIDE) - begin)
    copy = pltpu.make_async_copy(value_ref.at[own], own_out.at[own], sem)
    copy.start()
    return copy


def kernel_rows(
    after, table, gain1, b_sh, x_in, edge_in, w_in_in, triple_grad_in, middle_grad_in, middle_in, hidden_in, w_sh_in,
    input_out, result_out, halo_out,
    x, w_in, triple_grad, middle_grad, middle, hidden, w_sh, result, halo, sems, step_sems,
):
    del after
    rows, width = x_in.shape
    total = x.shape[0]
    move = Mover(sems)
    early = [
        move.start(w_in_in, w_in),
        move.start(x_in, x.at[pl.ds(0, rows)]),
        move.start(edge_in, x.at[pl.ds(rows, TILE)]),
    ]
    arrays = ((triple_grad_in, triple_grad), (middle_grad_in, middle_grad), (middle_in, middle), (hidden_in, hidden))
    steps = range(total // WIDE)
    parts = [step_copies(arrays[:2], step, step_sems) for step in steps]
    for part in parts:
        for copy in part:
            copy.start()
    weight_copy = move.start(w_sh_in, w_sh)
    more = [step_copies(arrays[2:], step, step_sems, 2) for step in steps]
    for part in more:
        for copy in part:
            copy.start()
    for copy in early:
        copy.wait()
    leaving = []
    for step in steps:
        for copy in parts[step]:
            copy.wait()
        spot = pl.ds(step * WIDE, WIDE)
        scaled, inverse = normalize(x[spot, :].astype(F32))
        normed_grad = dot_nt(triple_grad[spot, :], w_in[...])
        middle_grad[spot, :] = middle_grad[spot, :] + normalize_back(normed_grad, scaled, inverse, row_of(gain1))
        leaving.append(leave(middle_grad, input_out, step, step_sems.at[step, 4]))
    weight_copy.wait()
    for step in steps:
        for copy in more[step]:
            copy.wait()
        spot = pl.ds(step * WIDE, WIDE)
        keep = interval(step, table[GROUPS, 1], table[GROUPS, 2], WIDE)
        row = middle[spot, :] + row_of(b_sh) + dot(hidden[spot, :], w_sh[...])
        result[spot, :] = jnp.where(keep, row, 0.0).astype(BF16)
        leaving.append(leave(result, result_out, step, step_sems.at[step, 5]))
    over = pl.ds(rows, HALO)
    halo[:HALO, :] = middle_grad[over, :].astype(BF16)
    halo[HALO:, :] = result[over, :]
    leaving.append(move.start(halo, halo_out))
    for copy in leaving:
        copy.wait()


def kernel_add(mine_in, other_in, out, mine, other, sems):
    chunks = sems.shape[0]
    size = mine.shape[0] // chunks

    def copies(chunk):
        spot = pl.ds(chunk * size, size)
        return [
            pltpu.make_async_copy(mine_in.at[spot], mine.at[spot], sems.at[chunk, 0]),
            pltpu.make_async_copy(other_in.at[spot], other.at[spot], sems.at[chunk, 1]),
            pltpu.make_async_copy(mine.at[spot], out.at[spot], sems.at[chunk, 2]),
        ]

    for chunk in range(chunks):
        for copy in copies(chunk)[:2]:
            copy.start()
    for chunk in range(chunks):
        spot = pl.ds(chunk * size, size)
        arriving = copies(chunk)
        for copy in arriving[:2]:
            copy.wait()
        mine[spot, :] = (mine[spot, :].astype(F32) + other[spot, :].astype(F32)).astype(BF16)
        arriving[2].start()
    for chunk in range(chunks):
        copies(chunk)[2].wait()


def kernel_sum(extra, *refs):
    parts_in, out, parts, piece, sems = refs[extra:]
    count = parts.shape[0]
    quarter = max(count // 4, 1)
    copies = []
    for index, begin in enumerate(range(0, count, quarter)):
        spot = pl.ds(begin, quarter)
        copies.append(pltpu.make_async_copy(parts_in.at[spot], parts.at[spot], sems.at[index]))
        copies[-1].start()
    total = jnp.zeros(piece.shape, F32)
    for index, copy in enumerate(copies):
        copy.wait()
        for part in range(index * quarter, (index + 1) * quarter):
            total = total + parts[part].astype(F32)
    piece[...] = total.astype(BF16)
    for part in range(count):
        pltpu.make_async_copy(piece, out.at[part], sems.at[4]).start()
    pltpu.make_async_copy(parts, out, sems.at[4]).wait()


def kernel_unpack_half(half, packed_in, d_ex, d_out, d_in, d_sh, packed, ex, out, inward, sh, sems):
    arrays = ((ex, d_ex), (sh, d_sh), (out, d_out), (inward, d_in))
    sizes = [value.shape[0] * value.shape[1] // LANES for value, _target in arrays]
    begins = [sum(sizes[:index]) for index in range(4)]
    arriving = []
    for index in range(4):
        spot = pl.ds(begins[index], sizes[index])
        arriving.append(pltpu.make_async_copy(packed_in.at[spot], packed.at[spot], sems.at[index]))
        arriving[-1].start()
    leaving = []
    for index, (value, target) in enumerate(arrays):
        arriving[index].wait()
        at = begins[index]
        if index != 1:
            count = value.shape[0]
            for begin in range(0, value.shape[1], LANES):
                value[:, begin : begin + LANES] = packed[pl.ds(at, count), :].astype(F32)
                at += count
        else:
            count = value.shape[1]
            for begin in range(0, value.shape[0], LANES):
                value[begin : begin + LANES, :] = packed[pl.ds(at, count), :].astype(F32).T
                at += count
        rows = pl.ds(pl.multiple_of(half * value.shape[0], value.shape[0]), value.shape[0])
        leaving.append(pltpu.make_async_copy(value, target.at[rows], sems.at[4 + index]))
        leaving[-1].start()
    return leaving


def own_core():
    return lax.rem(lax.axis_index("dp"), 2)


def kernel_first_half(packed_in, *refs):
    for copy in kernel_unpack_half(own_core(), packed_in, *refs):
        copy.wait()


def kernel_second_half(
    packed_in, first_in, kept_ex, kept_out, kept_in, kept_sh,
    d_ex, d_out, d_in, d_sh, b_in, b_sh, gain2, shift2, b_out, b_ex, gain1, shift1,
    packed, ex, out, inward, sh, sems, mine, other, small_sems,
):
    del kept_ex, kept_out, kept_in, kept_sh
    rows = pl.ds(first_in.shape[0] - mine.shape[0], mine.shape[0])
    copies = [
        pltpu.make_async_copy(first_in.at[rows], mine, small_sems.at[0]),
        pltpu.make_async_copy(packed_in.at[rows], other, small_sems.at[1]),
    ]
    for copy in copies:
        copy.start()
    core = own_core()
    leaving = kernel_unpack_half(
        1 - core, packed_in, d_ex, d_out, d_in, d_sh, packed, ex, out, inward, sh, sems
    )
    for copy in copies:
        copy.wait()
    width, columns = b_sh.shape[0], b_ex.shape[0]
    swap = core == 1
    blocks = []
    for index in range(columns // LANES):
        spot = pl.ds(index // 2 * 16, 16)
        pair = mine[spot, :].astype(F32), other[spot, :].astype(F32)
        blocks.append(jnp.where(swap, pair[1 - index % 2], pair[index % 2]))
    small = jnp.concatenate(blocks, axis=1)
    for row, ref in ((0, b_sh), (1, gain2), (2, shift2), (3, b_out), (6, gain1), (7, shift1)):
        ref[...] = small[row, :width]
    b_ex[...] = small[4]
    b_in[0:1, :] = small[5:6, :width]
    b_in[1:2, :] = small[5:6, 2 * width : 3 * width]
    for copy in leaving:
        copy.wait()


def kernel_touch(*refs):
    del refs


VMEM = pl.BlockSpec(memory_space=pltpu.VMEM)
SMEM = pl.BlockSpec(memory_space=pltpu.SMEM)
ANY = pl.BlockSpec(memory_space=pl.ANY)


def params(mib):
    return pltpu.CompilerParams(vmem_limit_bytes=mib * 1024 * 1024)


def cost(flops, moved):
    return pl.CostEstimate(flops=int(flops), bytes_accessed=int(moved), transcendentals=0)


def shape(dims, dtype):
    return jax.ShapeDtypeStruct(dims, dtype)


def packed_rows(columns, small, pieces):
    half = columns // LANES * 192 + (small // LANES + 1) // 2 * 16
    return pieces * (-(-half // (8 * pieces)) * 8)


def attention_scratch(pairs):
    return [
        [pltpu.VMEM((pairs, WIN, 2 * WIN), F32)] * 2,
        [pltpu.VMEM((8, 2 * WIN), F32)] * 2,
        [pltpu.VMEM((pairs, 2 * WIN, WIN), BF16)] * 2,
        [pltpu.VMEM((8, 2 * WIN), F32)] * 2,
    ]


def own_part(segments, gain1, shift1, b_in, x, w_in):
    rows, width = x.shape
    total = rows + TILE
    pairs = width // (2 * HD)
    vmem = pltpu.VMEM
    return pl.pallas_call(
        kernel_own,
        out_shape=(
            shape((rows, 3 * width), BF16),
            shape((total, width), BF16),
            shape((rows, width), BF16),
            shape((GROUPS, pairs, 2 * WIN, WIN), BF16),
            shape((GROUPS, 8, WIN), F32),
            shape((GROUPS + 1, 8), jnp.int32),
        ),
        in_specs=[ANY] * 6,
        out_specs=(ANY, ANY, ANY, ANY, VMEM, SMEM),
        scratch_shapes=[
            vmem(segments.shape, jnp.int32),
            vmem(gain1.shape, F32),
            vmem(shift1.shape, F32),
            vmem(b_in.shape, F32),
            vmem((rows, width), BF16),
            vmem(w_in.shape, BF16),
            vmem((total, 3 * width), BF16),
            vmem((total, width), BF16),
            vmem((8, LANES), jnp.int32),
            pltpu.SMEM((8, LANES), jnp.int32),
            *attention_scratch(pairs),
            vmem((GROUPS, pairs, 2 * WIN, WIN), BF16),
            pltpu.SemaphoreType.DMA((16,)),
            pltpu.SemaphoreType.DMA((rows // OWN + 1,)),
        ],
        compiler_params=params(63),
        cost_estimate=cost(2 * 6 * rows * width * 3 * width, 1e7),
        name="own_part",
    )(segments, gain1, shift1, b_in, x, w_in)


def rest_part(table, vectors, x, cot, halo, triple, attended, scaled, raised, stats, w_in, w_out, w_ex, w_sh, pieces):
    rows, width = x.shape
    total = rows + TILE
    hidden = w_ex.shape[1]
    packed = packed_rows(2 * hidden + 4 * width, hidden, pieces)
    vmem = pltpu.VMEM
    pairs = width // (2 * HD)
    square, row = vmem((pairs, WIN, 2 * WIN), F32), vmem((8, 2 * WIN), F32)
    low = vmem((pairs, WIN, 2 * WIN), BF16)
    return pl.pallas_call(
        kernel_rest,
        out_shape=(
            shape((total, width), F32),
            shape((total, width), F32),
            shape((total, hidden), BF16),
            shape((total, 3 * width), BF16),
            shape((TILE, width), BF16),
            shape((packed, LANES), BF16),
            shape((packed, LANES), BF16),
        ),
        in_specs=[SMEM] + [ANY] * 19,
        out_specs=tuple([ANY] * 7),
        scratch_shapes=[
            vmem((total, width), BF16),
            vmem((total, width), BF16),
            vmem(w_in.shape, BF16),
            vmem(w_out.shape, BF16),
            vmem(w_ex.shape, BF16),
            vmem(w_sh.shape, BF16),
            vmem((total, 3 * width), BF16),
            vmem((total, width), BF16),
            vmem((total, width), F32),
            vmem((total, width), F32),
            vmem((total, width), BF16),
            vmem((total, hidden), BF16),
            vmem((total, 3 * width), BF16),
            vmem((GROUPS, 8, WIN), F32),
            vmem((width, hidden), F32),
            vmem((width, hidden), F32),
            vmem((width, width), F32),
            vmem((width, 3 * width), F32),
            vmem((16, 3 * width), F32),
            vmem((16, hidden), F32),
            [square],
            [row],
            [vmem((pairs, 2 * WIN, WIN), BF16)],
            [row],
            [vmem((pairs, 2 * HD, WIN), BF16)] * 2,
            [low] * 2,
            vmem((SLOTS, pairs, 2 * WIN, WIN), BF16),
            vmem((TILE, width), BF16),
            vmem((packed, LANES), BF16),
            vmem((packed, LANES), BF16),
            pltpu.SemaphoreType.DMA((40,)),
            pltpu.SemaphoreType.DMA((2,)),
            pltpu.SemaphoreType.DMA((SLOTS,)),
            *[vmem(v.shape, F32) for v in vectors],
        ],
        compiler_params=params(62),
        cost_estimate=cost(2 * 9 * rows * width * (3 * width + 8 * width), 3e7),
        name="rest_part",
    )(table, *vectors, x, cot, halo, triple, attended, scaled, raised, stats, w_in, w_out, w_ex, w_sh)


def row_outputs(after, table, gain1, b_sh, x, edge, w_in, triple_grad, middle_grad, middle, hidden, w_sh):
    rows, width = x.shape
    total = triple_grad.shape[0]
    vmem = pltpu.VMEM
    return pl.pallas_call(
        kernel_rows,
        out_shape=(shape((rows, width), F32), shape((rows, width), BF16), shape((2 * HALO, width), BF16)),
        in_specs=[ANY, SMEM, VMEM, VMEM] + [ANY] * 8,
        out_specs=(ANY, ANY, ANY),
        scratch_shapes=[
            vmem((total, width), BF16),
            vmem(w_in.shape, BF16),
            vmem((total, 3 * width), BF16),
            vmem((total, width), F32),
            vmem((total, width), F32),
            vmem(hidden.shape, BF16),
            vmem(w_sh.shape, BF16),
            vmem((total, width), BF16),
            vmem((2 * HALO, width), BF16),
            pltpu.SemaphoreType.DMA((8,)),
            pltpu.SemaphoreType.DMA((total // WIDE, 6)),
        ],
        compiler_params=params(63),
        cost_estimate=cost(2 * total * width * 16 * width, 2.7e7),
        name="row_outputs",
    )(after, table, gain1, b_sh, x, edge, w_in, triple_grad, middle_grad, middle, hidden, w_sh)


def add_halves(mine, other):
    return pl.pallas_call(
        kernel_add,
        out_shape=shape(mine.shape, BF16),
        in_specs=[ANY, ANY],
        out_specs=ANY,
        scratch_shapes=[
            pltpu.VMEM(mine.shape, BF16), pltpu.VMEM(mine.shape, BF16), pltpu.SemaphoreType.DMA((4, 3)),
        ],
        compiler_params=params(63),
        cost_estimate=cost(mine.size, mine.size * 6),
        name="add_halves",
    )(mine, other)


def sum_parts(after, parts):
    return pl.pallas_call(
        partial(kernel_sum, len(after)),
        out_shape=shape(parts.shape, BF16),
        in_specs=[ANY] * (len(after) + 1),
        out_specs=ANY,
        scratch_shapes=[
            pltpu.VMEM(parts.shape, BF16),
            pltpu.VMEM(parts.shape[1:], BF16),
            pltpu.SemaphoreType.DMA((5,)),
        ],
        compiler_params=params(63),
        cost_estimate=cost(parts.size, parts.size * 4),
        name="sum_parts",
    )(*after, parts)


def half_shapes(width, hidden):
    dims = ((width, hidden), (width, width), (width, 3 * width), (hidden, width))
    scratch = [pltpu.VMEM((rows // 2, columns), F32) for rows, columns in dims]
    return tuple(shape(dim, F32) for dim in dims), [*scratch, pltpu.SemaphoreType.DMA((8,))]


def unpack_first(packed, width, hidden):
    shapes, scratch = half_shapes(width, hidden)
    return pl.pallas_call(
        kernel_first_half,
        out_shape=shapes,
        in_specs=[ANY],
        out_specs=(ANY,) * 4,
        scratch_shapes=[pltpu.VMEM(packed.shape, BF16), *scratch],
        compiler_params=params(63),
        cost_estimate=cost(packed.size, packed.size * 6),
        name="unpack_first",
    )(packed)


def unpack_second(packed, first, kept, used, width, hidden):
    shapes, scratch = half_shapes(width, hidden)
    rows = first.shape[0] - used
    small = tuple(shape(dims, F32) for dims in ((2, width),) + ((width,),) * 4 + ((hidden,), (width,), (width,)))
    return pl.pallas_call(
        kernel_second_half,
        out_shape=shapes + small,
        in_specs=[ANY] * 6,
        out_specs=(ANY,) * 4 + (VMEM,) * 8,
        scratch_shapes=[
            pltpu.VMEM(packed.shape, BF16), *scratch, pltpu.VMEM((rows, LANES), BF16), pltpu.VMEM((rows, LANES), BF16),
            pltpu.SemaphoreType.DMA((2,)),
        ],
        input_output_aliases={2: 0, 3: 1, 4: 2, 5: 3},
        compiler_params=params(63),
        cost_estimate=cost(packed.size, packed.size * 6),
        name="unpack_second",
    )(packed, first, *kept)


def touch(value, *after):
    return pl.pallas_call(
        kernel_touch,
        out_shape=shape(value.shape, value.dtype),
        in_specs=[ANY] * (1 + len(after)),
        out_specs=ANY,
        input_output_aliases={0: 0},
        name="touch",
    )(value, *after)


def same_core_groups():
    packs, parts = lax.axis_size("dp"), lax.axis_size("mp")
    return [[d * parts + m for d in range(c, packs, 2) for m in range(parts)] for c in range(2)]


def swap_cores(block):
    packs = lax.axis_size("dp")
    return lax.ppermute(block, "dp", [(i, i ^ 1) for i in range(packs)])


def exchange(parts):
    return lax.all_to_all(parts, ("dp", "mp"), 0, 0, axis_index_groups=same_core_groups())


def passed(block, distance):
    count = lax.axis_size("mp")
    route = [(i, i + distance) for i in range(count) if 0 <= i + distance < count]
    return lax.ppermute(block, "mp", route)


def kernel_take_over(table, halo_in, input_in, result_in, input_out, result_out, halo, input_own, result_own, sems):
    rows = pl.ds(0, HALO)
    copies = [
        pltpu.make_async_copy(halo_in, halo, sems.at[0]),
        pltpu.make_async_copy(input_in.at[rows], input_own, sems.at[1]),
        pltpu.make_async_copy(result_in.at[rows], result_own, sems.at[2]),
    ]
    for copy in copies:
        copy.start()
    for copy in copies:
        copy.wait()
    other = lax.broadcasted_iota(jnp.int32, (HALO, 1), 0) < table[GROUPS, 1]
    input_own[...] = jnp.where(other, halo[:HALO, :].astype(F32), input_own[...])
    result_own[...] = jnp.where(other, halo[HALO:, :].astype(F32), result_own[...].astype(F32)).astype(BF16)
    copies = [
        pltpu.make_async_copy(input_own, input_out.at[rows], sems.at[3]),
        pltpu.make_async_copy(result_own, result_out.at[rows], sems.at[4]),
    ]
    for copy in copies:
        copy.start()
    for copy in copies:
        copy.wait()


def take_over(table, halo, input_grad, result):
    width = input_grad.shape[1]
    return pl.pallas_call(
        kernel_take_over,
        out_shape=(shape(input_grad.shape, F32), shape(result.shape, BF16)),
        in_specs=[SMEM, ANY, ANY, ANY],
        out_specs=(ANY, ANY),
        scratch_shapes=[
            pltpu.VMEM(halo.shape, BF16), pltpu.VMEM((HALO, width), F32), pltpu.VMEM((HALO, width), BF16),
            pltpu.SemaphoreType.DMA((5,)),
        ],
        input_output_aliases={2: 0, 3: 1},
        compiler_params=params(63),
        name="take_over",
    )(table, halo, input_grad, result)


def body(
    layer_input, segments, cotangent, first_gain, first_shift, inward_weight, inward_bias, outward_weight,
    outward_bias, second_gain, second_shift, expand_weight, expand_bias, shrink_weight, shrink_bias,
):
    rows, width = layer_input.shape
    hidden_width = expand_weight.shape[1]
    pieces = lax.axis_size("dp") * lax.axis_size("mp") // 2
    gain1, shift1, b_out, gain2, shift2, b_ex, b_sh = (
        first_gain, first_shift, outward_bias, second_gain, second_shift, expand_bias, shrink_bias
    )
    halo = passed(jnp.concatenate([layer_input[:HALO], cotangent[:HALO]], axis=0), -1)
    triple, attended, scaled, raised, stats, table = own_part(
        segments, gain1, shift1, inward_bias, layer_input, inward_weight
    )
    middle, middle_grad, hidden, triple_grad, edge, mine, other = rest_part(
        table, (gain1, shift1, inward_bias, b_out, gain2, shift2, b_ex), layer_input, cotangent, halo, triple,
        attended, scaled, raised, stats, inward_weight, outward_weight, expand_weight, shrink_weight, pieces,
    )
    both = add_halves(mine, swap_cores(other))
    parts = exchange(both.reshape(pieces, -1, LANES))
    input_grad, result, halo = row_outputs(
        both, table, gain1, b_sh, layer_input, edge, inward_weight, triple_grad, middle_grad, middle, hidden,
        shrink_weight,
    )
    summed = sum_parts((halo,), parts)
    mine = exchange(summed).reshape(-1, LANES)
    input_grad, result = take_over(table, touch(passed(halo, 1), summed), input_grad, result)
    mine = touch(mine, input_grad, result)
    other = swap_cores(mine)
    used = 192 * (2 * hidden_width + 4 * width) // LANES
    half = unpack_first(mine, width, hidden_width)
    d_ex, d_out, d_in, d_sh, d_b_in, d_b_sh, d_gain2, d_shift2, d_b_out, d_b_ex, d_gain1, d_shift1 = unpack_second(
        other, mine, half, used, width, hidden_width
    )
    return (
        result, input_grad, d_gain1, d_shift1, d_in, d_b_in, d_out, d_b_out, d_gain2, d_shift2, d_ex, d_b_ex, d_sh,
        d_b_sh,
    )


def solution(mesh):
    rows = P(("dp", "mp"), None)
    in_specs = (rows, P("dp", None), rows) + (P(),) * 12
    out_specs = (rows, rows) + (P(),) * 12
    return jax.shard_map(body, mesh=mesh, in_specs=in_specs, out_specs=out_specs, check_vma=False)
```

```python
from functools import partial

import jax
import jax.numpy as jnp
from jax import lax
from jax.experimental import pallas as pl
from jax.experimental.pallas import tpu as pltpu
from jax.sharding import PartitionSpec as P

HD = 64
SEQ = 198
EPSILON = 1e-06
MASKED = -1000000000.0
LOG2E = 1.4426950408889634
WIN = 256
TILE = 256
HALO = 208
WIDE = 768
OWN = 1024
BLOCK = 512
GROUPS = 24
SLOTS = 5
LANES = 128
CHUNK = 256
FEED = 768
BIG = 1 << 20
F32 = jnp.float32
BF16 = jnp.bfloat16
NT = (((1,), (1,)), ((), ()))
TN = (((0,), (0,)), ((), ()))


def row_of(ref):
    return ref[...].reshape(1, -1)


def dot(a, b):
    return jnp.dot(a, b, preferred_element_type=F32)


def dot_nt(a, b):
    return lax.dot_general(a, b, NT, preferred_element_type=F32)


def dot_tn(a, b):
    return lax.dot_general(a, b, TN, preferred_element_type=F32)


def normalize(rows):
    center = jnp.mean(rows, axis=-1, keepdims=True)
    centred = rows - center
    spread = jnp.mean(centred * centred, axis=-1, keepdims=True)
    inverse = lax.rsqrt(spread + EPSILON)
    return centred * inverse, inverse


def normalize_back(upstream, scaled, inverse, gain):
    direct = upstream * gain
    first = jnp.mean(direct, axis=-1, keepdims=True)
    second = jnp.mean(direct * scaled, axis=-1, keepdims=True)
    return inverse * (direct - first - scaled * second)


def gelu_parts(v, half_upstream):
    scaled = v * 0.7071067811865476
    double = 1.0 + lax.erf(scaled)
    bell = jnp.exp2((scaled * scaled) * -1.4426950408889634)
    return (0.5 * v) * double, half_upstream * (double + (v * 0.7978845608028654) * bell)


def image_ends(seg, base, work):
    ident = lax.broadcasted_iota(jnp.int32, (LANES, LANES), 0)
    below = jnp.zeros((LANES, LANES), F32)
    for begin in range(0, seg.shape[1], LANES):
        row = seg[0:1, begin : begin + LANES]
        row = jnp.where(row < 0, BIG, row)
        below = below + jnp.where(row <= ident, 1.0, 0.0)
    ends = jnp.broadcast_to(jnp.sum(below, axis=1, keepdims=True), (LANES, LANES))
    started = jnp.sum(jnp.where(ends < base.astype(F32), 1.0, 0.0), axis=0, keepdims=True)
    work[0:1, :] = ends.T[0:1].astype(jnp.int32)
    work[1:2, :] = started.astype(jnp.int32)


def plan_groups(ends, position, rows, table):
    base = position * rows
    limit = jnp.minimum(base + rows, ends[0, LANES - 1]) - base
    image = jnp.where(position == 0, 0, ends[1, 0] + 1)
    first = jnp.where(position == 0, 0, ends[0, jnp.maximum(image - 1, 0)]) - base

    def body(state):
        at, image, group, window, start, c1, c2 = state
        after = ends[0, jnp.minimum(image, LANES - 1)] - base
        fits = after - window <= WIN

        @pl.when(jnp.logical_not(fits))
        def _():
            write_group(table, group, window, start, c1, c2, at)

        group = jnp.where(fits, group, group + 1)
        new_c1 = jnp.where(fits, jnp.where(at == start, c1, jnp.where(c1 < 0, at, c1)), -1)
        new_c2 = jnp.where(fits, jnp.where(jnp.logical_and(at != start, c1 >= 0), jnp.where(c2 < 0, at, c2), c2), -1)
        start = jnp.where(fits, start, at)
        window = jnp.where(fits, window, (at // 16) * 16)
        return after, image + 1, group, window, start, new_c1, new_c2

    init = (first, image, jnp.int32(0), (first // 16) * 16, first, jnp.int32(-1), jnp.int32(-1))
    at, image, group, window, start, c1, c2 = lax.while_loop(lambda s: s[0] < limit, body, init)
    write_group(table, group, window, start, c1, c2, at)
    table[GROUPS, 0] = group + 1
    table[GROUPS, 1] = first
    table[GROUPS, 2] = at


def write_group(table, group, window, start, c1, c2, end):
    table[group, 0] = window
    table[group, 1] = start - window
    table[group, 2] = jnp.where(c1 < 0, end, c1) - window
    table[group, 3] = jnp.where(c2 < 0, end, c2) - window
    table[group, 4] = end - window


def group_bias(table, group):
    bounds = [table[group, i] for i in range(1, 5)]
    row = lax.broadcasted_iota(jnp.int32, (WIN, LANES), 0)
    col = lax.broadcasted_iota(jnp.int32, (1, WIN), 1)

    def ident(index):
        return sum((index >= b).astype(jnp.int32) for b in bounds)

    row, col = ident(row), ident(col)
    return jnp.concatenate(
        [jnp.where(row == col[:, at : at + LANES], 0.0, MASKED) for at in range(0, WIN, LANES)], axis=1
    )


def group_mask_factors(table, group):
    bounds = [table[group, i] for i in range(1, 5)]

    def ident(index):
        return sum((index >= b).astype(jnp.int32) for b in bounds)

    row = ident(lax.broadcasted_iota(jnp.int32, (WIN, LANES), 0))
    left = jnp.where(row == lax.broadcasted_iota(jnp.int32, (WIN, LANES), 1), 1.0, 0.0).astype(BF16)
    col = ident(lax.broadcasted_iota(jnp.int32, (1, WIN), 1))
    kind = lax.broadcasted_iota(jnp.int32, (16, WIN), 0)
    right = jnp.where(kind == col, 0.0, MASKED).astype(BF16)
    right = jnp.concatenate([right, jnp.zeros((LANES - 16, WIN), BF16)], axis=0)
    return left, jnp.concatenate([right, right], axis=1)


def head_masks():
    lane = lax.broadcasted_iota(jnp.int32, (WIN, 2 * HD), 1)
    return lane < HD, lane >= HD


def keep_first(ref, window, begin, cols, value):
    head = pl.ds(window, 16)
    old = ref[head, cols]
    row = lax.broadcasted_iota(jnp.int32, (16, 2 * HD), 0)
    ref[head, cols] = jnp.where(row >= begin, value[:16].astype(F32), old.astype(F32)).astype(BF16)
    ref[pl.ds(window + 16, WIN - 16), cols] = value[16:].astype(BF16)


def block_diagonal(pair_t):
    zero = jnp.zeros((HD, pair_t.shape[1]), pair_t.dtype)
    return jnp.concatenate(
        [jnp.concatenate([pair_t[:HD], zero], axis=1), jnp.concatenate([zero, pair_t[HD:]], axis=1)], axis=0
    )


def pipelined(groups, first, second, third, keep_copy):
    def clamped(group):
        return jnp.minimum(group, groups - 1)

    def half(group, slot):
        first(clamped(group), slot)
        second(clamped(group - 1), 1 - slot)
        third(clamped(group - 2), slot)

    first(0, 0)
    first(clamped(1), 1)
    second(0, 0)
    steps = (groups + 1) // 2

    def both(step, _):
        keep_copy(clamped(2 * step)).start()

        @pl.when(step > 0)
        def _():
            keep_copy(clamped(2 * step - 1)).start()

        half(2 * step + 2, 0)
        half(2 * step + 3, 1)
        return 0

    lax.fori_loop(0, steps, both, 0)
    keep_copy(clamped(2 * steps - 1)).start()

    def settle(_, carry):
        keep_copy(0).wait()
        return carry

    return lambda: lax.fori_loop(0, 2 * steps, settle, 0)


def group_rows(table, group):
    return pl.ds(pl.multiple_of(table[group, 0], 16), WIN)


def attend_groups(groups, table, triple, attended, stats, scores, peaks, raised, scales, alone=None, kept=None, keep_copy=None):
    width = attended.shape[1]
    pairs = range(width // (2 * HD))

    def first(group, slot):
        rows = group_rows(table, group)
        left, right = group_mask_factors(table, group)
        for pair in pairs:
            query_t = triple[rows, pl.ds(pair * 2 * HD, 2 * HD)].T
            key = triple[rows, pl.ds(width + pair * 2 * HD, 2 * HD)]
            value = dot(
                jnp.concatenate([key, left], axis=1), jnp.concatenate([block_diagonal(query_t), right], axis=0)
            )
            scores[slot][pair] = value
            peaks[slot][pair : pair + 1, :] = jnp.max(value, axis=0, keepdims=True)

    def second(group, slot):
        for pair in pairs:
            peak = peaks[slot][pair : pair + 1, :]
            value = jnp.exp2(scores[slot][pair] - peak)
            total = jnp.sum(value, axis=0, keepdims=True)
            low = value.astype(BF16)
            raised[slot][pair, :WIN] = low[:, :WIN]
            raised[slot][pair, WIN:] = low[:, WIN:]
            if kept is not None:
                kept[group, pair, :WIN] = low[:, :WIN]
                kept[group, pair, WIN:] = low[:, WIN:]
            scale = 1.0 / total
            scales[slot][pair : pair + 1, :] = scale
            stats[group, pl.ds(2 * pair, 1), :] = scale[:, :WIN]
            stats[group, pl.ds(2 * pair + 1, 1), :] = scale[:, WIN:]

    def third(group, slot):
        rows = group_rows(table, group)
        for pair in pairs:
            value_t = block_diagonal(triple[rows, pl.ds(2 * width + pair * 2 * HD, 2 * HD)].T)
            out = dot(value_t, raised[slot][pair])
            scale = scales[slot][pair : pair + 1, :]
            out = jnp.concatenate([out[:HD] * scale[:, :WIN], out[HD:] * scale[:, WIN:]], axis=0)
            keep_first(attended, rows.start, table[group, 1], pl.ds(pair * 2 * HD, 2 * HD), out.T)

    if alone is None:
        return pipelined(groups, first, second, third, keep_copy)
    for part in (first, second, third):
        part(alone, 0)
    return None


def attend_back_groups(
    groups, table, triple, attended, upstream, stats, triple_grad, scores_grads, scaled_up, kept, kept_copy
):
    width = attended.shape[1]
    pairs = range(width // (2 * HD))
    masks = head_masks()

    def columns(pair, block):
        return pl.ds(block * width + pair * 2 * HD, 2 * HD)

    def side_by_side(turn, pair):
        low = kept[lax.rem(turn, SLOTS), pair]
        return jnp.concatenate([low[:WIN], low[WIN:]], axis=1)

    def first(turn, group, slot):
        rows = group_rows(table, group)
        for pair in pairs:
            scale = [jnp.broadcast_to(stats[group, pl.ds(2 * pair + h, 1), :], (HD, WIN)) for h in range(2)]
            up_t = upstream[rows, columns(pair, 0)].T.astype(F32) * jnp.concatenate(scale, axis=0)
            product = attended[rows, columns(pair, 0)].T.astype(F32) * up_t
            agreement = jnp.concatenate(
                [jnp.sum(product[:HD], axis=0, keepdims=True), jnp.sum(product[HD:], axis=0, keepdims=True)], axis=1
            )
            up_low = up_t.astype(BF16)
            scaled_up[slot][pair] = up_low
            probs_grad = dot(triple[rows, columns(pair, 2)], block_diagonal(up_low))
            prob = side_by_side(turn, pair).astype(F32)
            scores_grads[slot][pair] = (prob * (probs_grad - agreement)).astype(BF16)

    def stacked(pair_rows):
        zero = jnp.zeros_like(pair_rows)
        return jnp.concatenate([jnp.where(mask, pair_rows, zero) for mask in masks], axis=0)

    def second(turn, group, slot):
        rows = group_rows(table, group)
        window, begin = rows.start, table[group, 1]
        for pair in pairs:
            scores_grad = scores_grads[slot][pair]
            value_grad = dot_nt(side_by_side(turn, pair), block_diagonal(scaled_up[slot][pair]))
            key_grad = dot(scores_grad, stacked(triple[rows, columns(pair, 0)]))
            key_t = block_diagonal(triple[rows, columns(pair, 1)].T)
            query_grad = dot(key_t, jnp.concatenate([scores_grad[:, :WIN], scores_grad[:, WIN:]], axis=0))
            keep_first(triple_grad, window, begin, columns(pair, 0), (query_grad * HD ** (-0.5)).T)
            keep_first(triple_grad, window, begin, columns(pair, 1), key_grad * (1.0 / LOG2E))
            keep_first(triple_grad, window, begin, columns(pair, 2), value_grad)

    def clamped(turn):
        return jnp.minimum(turn, groups - 1)

    def half(turn, slot):
        first(turn, clamped(turn), slot)
        second(turn - 1, clamped(turn - 1), 1 - slot)

    steps = (groups + 1) // 2

    def fetch(turn):
        kept_copy(clamped(turn), lax.rem(turn, SLOTS))

    def arrived(turn):
        kept_copy(None, lax.rem(turn, SLOTS))

    arrived(jnp.int32(0))
    first(jnp.int32(0), 0, 0)

    def both(step, _):
        @pl.when(step + 1 < steps)
        def _():
            fetch(2 * step + 3)
            fetch(2 * step + 4)

        arrived(2 * step + 1)
        arrived(2 * step + 2)
        half(2 * step + 1, 1)
        half(2 * step + 2, 0)
        return 0

    lax.fori_loop(0, steps, both, 0)


def interval(tile, first, end, size=TILE):
    row = lax.broadcasted_iota(jnp.int32, (size, 1), 0) + tile * size
    return jnp.logical_and(row >= first, row < end)


class Mover:
    def __init__(self, sems):
        self.sems = sems
        self.count = 0

    def start(self, source, target):
        copy = pltpu.make_async_copy(source, target, self.sems.at[self.count])
        self.count += 1
        copy.start()
        return copy


def project_rows(rows, gain1, shift1, w_in, b_in, target, spot, scaled_ref, scaled_spot):
    width = rows.shape[1]
    scaled, _inverse = normalize(rows)
    scaled_ref[scaled_spot, :] = scaled.astype(BF16)
    normed = (scaled * row_of(gain1) + row_of(shift1)).astype(BF16)
    q = dot(normed, w_in[:, :width]) + b_in[0:1, :]
    target[spot, :width] = (q.astype(BF16).astype(F32) * (HD ** (-0.5) * LOG2E)).astype(BF16)
    target[spot, width : 2 * width] = dot(normed, w_in[:, width : 2 * width]).astype(BF16)
    target[spot, 2 * width :] = (dot(normed, w_in[:, 2 * width :]) + b_in[1:2, :]).astype(BF16)


def kernel_own(
    seg_in, gain1_in, shift1_in, b_in_in, x_in, w_in_in,
    triple_out, attended_out, scaled_out, raised_out, stats, table,
    seg, gain1, shift1, b_in, x, w_in, triple, attended, work, ends, scores, peaks, raised, scales, kept, sems, tile_sems,
):
    rows, width = x_in.shape
    move = Mover(sems)
    seg_copy = move.start(seg_in, seg)
    early = [
        move.start(gain1_in, gain1), move.start(shift1_in, shift1), move.start(b_in_in, b_in),
        move.start(x_in, x), move.start(w_in_in, w_in),
    ]
    seg_copy.wait()
    image_ends(seg, lax.axis_index("mp") * rows, work)
    end_copy = move.start(work, ends)
    attended[...] = jnp.zeros_like(attended)
    spare = pl.ds(rows, triple.shape[0] - rows)
    triple[spare, :] = jnp.zeros((triple.shape[0] - rows, 3 * width), BF16)
    for copy in early:
        copy.wait()

    def step_copy(step):
        spot = pl.ds(pl.multiple_of(step * OWN, OWN), OWN)
        return pltpu.make_async_copy(triple.at[spot], triple_out.at[spot], tile_sems.at[step])

    def step_rows(step, _):
        spot = pl.ds(pl.multiple_of(step * OWN, OWN), OWN)
        project_rows(x[spot, :].astype(F32), gain1, shift1, w_in, b_in, triple, spot, x, spot)
        step_copy(step).start()
        return 0

    lax.fori_loop(0, rows // OWN, step_rows, 0)
    scaled_copy = move.start(x, scaled_out)
    end_copy.wait()
    plan_groups(ends, lax.axis_index("mp"), rows, table)

    def keep_copy(group):
        return pltpu.make_async_copy(kept.at[group], raised_out.at[group], tile_sems.at[rows // OWN])

    settle = attend_groups(
        jnp.maximum(table[GROUPS, 0] - 1, 1), table, triple, attended, stats, scores, peaks, raised, scales,
        kept=kept, keep_copy=keep_copy,
    )
    leaving = move.start(attended, attended_out)
    scaled_copy.wait()
    settle()
    for step in range(rows // OWN):
        step_copy(step).wait()
    leaving.wait()


def kernel_rest(
    table, *refs
):
    vectors_in, refs = refs[:7], refs[7:]
    vectors, refs = refs[-7:], refs[:-7]
    rest_body(table, vectors_in, vectors, *refs)


def rest_body(
    table, vectors_in, vectors,
    x_in, cot_in, halo_in, triple_in, attended_in, scaled_in, raised_in, stats_in, w_in_in, w_out_in, w_ex_in, w_sh_in,
    middle_out, middle_grad_out, hidden_out, triple_grad_out, edge_out, mine_out, other_out,
    x, back, w_in, w_out, w_ex, w_sh, triple, attended, middle, middle_grad, upstream, hidden, triple_grad, stats,
    d_ex, d_sh, d_out, product, sums, small, scores, peaks, raised, scales, scaled_up, scores_grads,
    kept, edge, mine, other, sems, tile_sems, kept_sems,
):
    rows, width = x_in.shape
    total = x.shape[0]
    tiles = total // FEED
    normed2, normed_grad = upstream, middle_grad
    move = Mover(sems)
    own, over = pl.ds(0, rows), pl.ds(rows, HALO)
    gain1, shift1, b_in, b_out, gain2, shift2, b_ex = vectors
    near, far = pl.ds(2 * WIDE, rows - 2 * WIDE), pl.ds(0, 2 * WIDE)
    first_copies = [move.start(halo_in.at[pl.ds(0, HALO)], x.at[over])]
    first_copies += [move.start(source, target) for source, target in zip(vectors_in, vectors)]
    first_copies.append(move.start(w_in_in, w_in))
    early = [
        move.start(triple_in.at[near], triple.at[near]),
        move.start(stats_in, stats),
        move.start(attended_in, attended),
    ]
    late = [
        move.start(w_out_in, w_out),
        move.start(x_in, x.at[own]),
        move.start(cot_in, back.at[own]),
        move.start(halo_in.at[pl.ds(HALO, HALO)], back.at[over]),
    ]
    weight_copies = [move.start(w_ex_in, w_ex), move.start(w_sh_in, w_sh)]
    last = move.start(triple_in.at[far], triple.at[far])
    rest = pl.ds(rows + HALO, total - rows - HALO)
    x[rest, :] = jnp.zeros((total - rows - HALO, width), BF16)
    back[rest, :] = jnp.zeros((total - rows - HALO, width), BF16)
    for ref in (d_ex, d_sh, d_out, product, sums, small, triple_grad):
        ref[...] = jnp.zeros_like(ref)
    groups, first, end = table[GROUPS, 0], table[GROUPS, 1], table[GROUPS, 2]
    for copy in first_copies:
        copy.wait()
    tail = pl.ds(rows, TILE)
    edge_copy = move.start(x.at[tail], edge_out)
    project_rows(x[tail, :].astype(F32), gain1, shift1, w_in, b_in, triple, tail, edge, slice(None))
    for copy in early:
        copy.wait()
    attend_groups(groups, table, triple, attended, stats, scores, peaks, raised, scales, alone=groups - 1)
    def kept_copy(group, slot):
        if group is None:
            pltpu.make_async_copy(raised[0], kept.at[slot], kept_sems.at[slot]).wait()
            return

        @pl.when(group == groups - 1)
        def _():
            pltpu.make_async_copy(raised[0], kept.at[slot], kept_sems.at[slot]).start()

        @pl.when(group != groups - 1)
        def _():
            pltpu.make_async_copy(raised_in.at[group], kept.at[slot], kept_sems.at[slot]).start()

    for turn in range(3):
        kept_copy(jnp.int32(turn), turn)
    for copy in late:
        copy.wait()
    leaving = []

    hidden_width = w_ex.shape[1]
    begins = list(range(0, hidden_width, CHUNK))

    def wide_rows(step):
        return pl.ds(step * WIDE, WIDE)

    def before_feed(step, _):
        spot = wide_rows(step)
        value = x[spot, :].astype(F32) + dot(attended[spot, :], w_out[...]) + row_of(b_out)
        scaled, _inverse = normalize(value)
        middle[spot, :] = value
        normed2[spot, :] = (scaled * row_of(gain2) + row_of(shift2)).astype(BF16)
        keep = interval(step, first, end, WIDE)
        back[spot, :] = jnp.where(keep, back[spot, :].astype(F32), 0.0).astype(BF16)
        return 0

    def feed(tile, _):
        spot = pl.ds(pl.multiple_of(tile * FEED, FEED), FEED)
        normed = normed2[spot, :]
        back_low = back[spot, :]
        back_half = (0.5 * back_low.astype(F32)).astype(BF16)

        def first_part(begin):
            cols = slice(begin, begin + CHUNK)
            before = dot(normed, w_ex[:, cols]) + b_ex[cols].reshape(1, -1)
            return before, dot_nt(back_half, w_sh[cols, :])

        held = [first_part(begins[0])]
        total_grad = jnp.zeros((width, FEED), F32)
        for index, begin in enumerate(begins):
            cols = slice(begin, begin + CHUNK)
            if index + 1 < len(begins):
                held.append(first_part(begins[index + 1]))
            value, grad = gelu_parts(*held[index])
            value, grad = value.astype(BF16), grad.astype(BF16)
            hidden[spot, cols] = value
            total_grad = total_grad + dot_nt(w_ex[:, cols], grad)
            d_sh[:, cols] += dot_tn(back_low, value)
            d_ex[:, cols] += dot_tn(normed, grad)
            small[4:5, cols] += jnp.sum(grad.astype(F32), axis=0, keepdims=True)
        normed_grad[spot, :] = total_grad.T
        pltpu.make_async_copy(hidden.at[spot], hidden_out.at[spot], tile_sems.at[0]).start()
        return 0

    def after_feed(step, _):
        spot = wide_rows(step)
        back32 = back[spot, :].astype(F32)
        scaled, inverse = normalize(middle[spot, :])
        upstream2 = normed_grad[spot, :]
        small[0:1, :width] += jnp.sum(back32, axis=0, keepdims=True)
        small[1:2, :width] += jnp.sum(upstream2 * scaled, axis=0, keepdims=True)
        small[2:3, :width] += jnp.sum(upstream2, axis=0, keepdims=True)
        grad = back32 + normalize_back(upstream2, scaled, inverse, row_of(gain2))
        small[3:4, :width] += jnp.sum(grad, axis=0, keepdims=True)
        middle_grad[spot, :] = grad
        grad_low = grad.astype(BF16)
        d_out[...] += dot_tn(attended[spot, :], grad_low)
        upstream[spot, :] = dot_nt(grad_low, w_out[...]).astype(BF16)
        pltpu.make_async_copy(middle_grad.at[spot], middle_grad_out.at[spot], tile_sems.at[1]).start()
        return 0

    for step in range(total // WIDE):
        before_feed(step, 0)
    for copy in weight_copies:
        copy.wait()
    edge_copy.wait()
    scaled_copy = move.start(scaled_in, x.at[own])
    x[tail, :] = edge[...]
    leaving.append(move.start(middle, middle_out))
    lax.fori_loop(0, tiles, feed, 0)
    for step in range(total // WIDE):
        after_feed(step, 0)
    core = lax.rem(lax.axis_index("dp"), 2)
    for half, target in ((core, mine), (1 - core, other)):
        at = pack((d_out,), half, target, pack_turned(d_sh, half, target, pack((d_ex,), half, target, 0)))
    ready = pl.ds(0, at)
    leaving += [move.start(mine.at[ready], mine_out.at[ready]), move.start(other.at[ready], other_out.at[ready])]
    last.wait()
    attend_back_groups(
        groups, table, triple, attended, upstream, stats, triple_grad, scores_grads, scaled_up, kept, kept_copy
    )
    leaving.append(move.start(triple_grad, triple_grad_out))
    scaled_copy.wait()
    ones = jnp.ones((16, WIDE), BF16)

    def multiply(step, _):
        spot = pl.ds(pl.multiple_of(step * WIDE, WIDE), WIDE)
        grad = triple_grad[spot, :]
        product[...] += dot_tn(x[spot, :], grad)
        sums[...] += dot(ones, grad)
        return 0

    lax.fori_loop(0, total // WIDE, multiply, 0)
    gain = jnp.broadcast_to(row_of(gain1), (LANES, width)).T
    shift = jnp.broadcast_to(row_of(shift1), (LANES, width)).T
    by_gain = jnp.zeros((width, LANES), F32)
    by_shift = jnp.zeros((width, LANES), F32)
    for begin in range(0, 3 * width, LANES):
        cols = slice(begin, begin + LANES)
        block, sum_row = product[:, cols], sums[0:1, cols]
        weight = w_in[:, cols].astype(F32)
        by_gain = by_gain + weight * block
        by_shift = by_shift + weight * sum_row
        product[:, cols] = gain * block + shift * sum_row
    small[5:6, : 3 * width] = sums[0:1, :]
    by_gain = jnp.broadcast_to(jnp.sum(by_gain, axis=1, keepdims=True), (width, LANES)).T
    by_shift = jnp.broadcast_to(jnp.sum(by_shift, axis=1, keepdims=True), (width, LANES)).T
    small[6:7, :width] = by_gain[0:1]
    small[7:8, :width] = by_shift[0:1]
    begin = at
    for half, target in ((core, mine), (1 - core, other)):
        at = pack((product,), half, target, begin)
    pack_small(small, core, mine, other, at)
    ready = pl.ds(begin, mine.shape[0] - begin)
    leaving += [move.start(mine.at[ready], mine_out.at[ready]), move.start(other.at[ready], other_out.at[ready])]
    for copy in leaving:
        copy.wait()
    pltpu.make_async_copy(hidden, hidden_out, tile_sems.at[0]).wait()
    pltpu.make_async_copy(middle_grad, middle_grad_out, tile_sems.at[1]).wait()


def pack(grads, half, target, at):
    for grad in grads:
        count = grad.shape[0] // 2
        rows = pl.ds(pl.multiple_of(half * count, count), count)
        for begin in range(0, grad.shape[1], LANES):
            target[pl.ds(at, count), :] = grad[rows, begin : begin + LANES].astype(BF16)
            at += count
    return at


def pack_turned(grad, half, target, at):
    count, columns = grad.shape[0], grad.shape[1] // 2
    for begin in range(0, columns, LANES):
        cols = pl.ds(pl.multiple_of(half * columns + begin, LANES), LANES)
        target[pl.ds(at, count), :] = grad[:, cols].astype(BF16)
        at += count
    return at


def pack_small(small, core, mine, other, at):
    rest = mine.shape[0] - at
    mine[pl.ds(at, rest), :] = jnp.zeros((rest, LANES), BF16)
    other[pl.ds(at, rest), :] = jnp.zeros((rest, LANES), BF16)
    for index in range(small.shape[1] // LANES):
        value = small[:, index * LANES : (index + 1) * LANES].astype(BF16)
        spot = pl.ds(at + (index // 2) * 16, 16)

        @pl.when(core == index % 2)
        def _():
            mine[spot, :] = value

        @pl.when(core != index % 2)
        def _():
            other[spot, :] = value


def step_copies(arrays, step, sems, skip=0):
    spot = pl.ds(step * WIDE, WIDE)
    return [
        pltpu.make_async_copy(source.at[spot], target.at[spot], sems.at[step, skip + at])
        for at, (source, target) in enumerate(arrays)
    ]


def kernel_rows(
    begin, end, after, table, gain1, b_sh, x_in, w_in_in, triple_grad_in, middle_grad_in, middle_in, hidden_in, w_sh_in,
    *refs,
):
    del after
    outs = 2 if end - begin > TILE else 1
    x, w_in, triple_grad, middle_grad, middle, hidden, w_sh, result, halo, sems, step_sems = refs[outs:]
    move = Mover(sems)
    early = [move.start(w_in_in, w_in), move.start(x_in, x)]
    size = min(BLOCK, end - begin)
    steps = range((end - begin) // size)

    def copies(step, arrays, skip):
        source_rows, rows = pl.ds(begin + step * size, size), pl.ds(step * size, size)
        some = [
            pltpu.make_async_copy(source.at[source_rows], target.at[rows], step_sems.at[step, skip + at])
            for at, (source, target) in enumerate(arrays)
        ]
        for copy in some:
            copy.start()
        return some

    parts = [
        copies(step, ((triple_grad_in, triple_grad), (middle_grad_in, middle_grad)), 0) for step in steps
    ]
    weight_copy = move.start(w_sh_in, w_sh)
    more = [copies(step, ((middle_in, middle), (hidden_in, hidden)), 2) for step in steps]
    for copy in early:
        copy.wait()
    leaving = []
    for step in steps:
        for copy in parts[step]:
            copy.wait()
        spot = pl.ds(step * size, size)
        scaled, inverse = normalize(x[spot, :].astype(F32))
        normed_grad = dot_nt(triple_grad[spot, :], w_in[...])
        middle_grad[spot, :] = middle_grad[spot, :] + normalize_back(normed_grad, scaled, inverse, row_of(gain1))
        if outs == 2:
            leaving.append(pltpu.make_async_copy(middle_grad.at[spot], refs[0].at[spot], step_sems.at[step, 4]))
            leaving[-1].start()
    weight_copy.wait()
    for step in steps:
        for copy in more[step]:
            copy.wait()
        spot = pl.ds(step * size, size)
        row = lax.broadcasted_iota(jnp.int32, (size, 1), 0) + begin + step * size
        keep = jnp.logical_and(row >= table[GROUPS, 1], row < table[GROUPS, 2])
        value = middle[spot, :] + row_of(b_sh) + dot(hidden[spot, :], w_sh[...])
        result[spot, :] = jnp.where(keep, value, 0.0).astype(BF16)
        if outs == 2:
            leaving.append(pltpu.make_async_copy(result.at[spot], refs[1].at[spot], step_sems.at[step, 5]))
            leaving[-1].start()
    if outs == 1:
        halo[:HALO, :] = middle_grad[:HALO, :].astype(BF16)
        halo[HALO:, :] = result[:HALO, :]
        leaving.append(move.start(halo, refs[0]))
    for copy in leaving:
        copy.wait()


def kernel_add(mine_in, other_in, out, mine, other, sems):
    chunks = sems.shape[0]
    size = mine.shape[0] // chunks

    def copies(chunk):
        spot = pl.ds(chunk * size, size)
        return [
            pltpu.make_async_copy(mine_in.at[spot], mine.at[spot], sems.at[chunk, 0]),
            pltpu.make_async_copy(other_in.at[spot], other.at[spot], sems.at[chunk, 1]),
            pltpu.make_async_copy(mine.at[spot], out.at[spot], sems.at[chunk, 2]),
        ]

    for chunk in range(chunks):
        for copy in copies(chunk)[:2]:
            copy.start()
    for chunk in range(chunks):
        spot = pl.ds(chunk * size, size)
        arriving = copies(chunk)
        for copy in arriving[:2]:
            copy.wait()
        mine[spot, :] = (mine[spot, :].astype(F32) + other[spot, :].astype(F32)).astype(BF16)
        arriving[2].start()
    for chunk in range(chunks):
        copies(chunk)[2].wait()


def kernel_sum(extra, *refs):
    parts_in, out, parts, piece, sems = refs[extra:]
    count = parts.shape[0]
    quarter = max(count // 4, 1)
    copies = []
    for index, begin in enumerate(range(0, count, quarter)):
        spot = pl.ds(begin, quarter)
        copies.append(pltpu.make_async_copy(parts_in.at[spot], parts.at[spot], sems.at[index]))
        copies[-1].start()
    total = jnp.zeros(piece.shape, F32)
    for index, copy in enumerate(copies):
        copy.wait()
        for part in range(index * quarter, (index + 1) * quarter):
            total = total + parts[part].astype(F32)
    piece[...] = total.astype(BF16)
    for part in range(count):
        pltpu.make_async_copy(piece, out.at[part], sems.at[4]).start()
    pltpu.make_async_copy(parts, out, sems.at[4]).wait()


def kernel_unpack_half(half, packed_in, d_ex, d_out, d_in, d_sh, packed, ex, out, inward, sh, sems):
    arrays = ((ex, d_ex), (sh, d_sh), (out, d_out), (inward, d_in))
    sizes = [value.shape[0] * value.shape[1] // LANES for value, _target in arrays]
    begins = [sum(sizes[:index]) for index in range(4)]
    arriving = []
    for index in range(4):
        spot = pl.ds(begins[index], sizes[index])
        arriving.append(pltpu.make_async_copy(packed_in.at[spot], packed.at[spot], sems.at[index]))
        arriving[-1].start()
    leaving = []
    for index, (value, target) in enumerate(arrays):
        arriving[index].wait()
        at = begins[index]
        if index != 1:
            count = value.shape[0]
            for begin in range(0, value.shape[1], LANES):
                value[:, begin : begin + LANES] = packed[pl.ds(at, count), :].astype(F32)
                at += count
        else:
            count = value.shape[1]
            for begin in range(0, value.shape[0], LANES):
                value[begin : begin + LANES, :] = packed[pl.ds(at, count), :].astype(F32).T
                at += count
        rows = pl.ds(pl.multiple_of(half * value.shape[0], value.shape[0]), value.shape[0])
        leaving.append(pltpu.make_async_copy(value, target.at[rows], sems.at[4 + index]))
        leaving[-1].start()
    return leaving


def own_core():
    return lax.rem(lax.axis_index("dp"), 2)


def kernel_first_half(packed_in, *refs):
    for copy in kernel_unpack_half(own_core(), packed_in, *refs):
        copy.wait()


def kernel_second_half(
    packed_in, first_in, kept_ex, kept_out, kept_in, kept_sh,
    d_ex, d_out, d_in, d_sh, b_in, b_sh, gain2, shift2, b_out, b_ex, gain1, shift1,
    packed, ex, out, inward, sh, sems, mine, other, small_sems,
):
    del kept_ex, kept_out, kept_in, kept_sh
    rows = pl.ds(first_in.shape[0] - mine.shape[0], mine.shape[0])
    copies = [
        pltpu.make_async_copy(first_in.at[rows], mine, small_sems.at[0]),
        pltpu.make_async_copy(packed_in.at[rows], other, small_sems.at[1]),
    ]
    for copy in copies:
        copy.start()
    core = own_core()
    leaving = kernel_unpack_half(
        1 - core, packed_in, d_ex, d_out, d_in, d_sh, packed, ex, out, inward, sh, sems
    )
    for copy in copies:
        copy.wait()
    width, columns = b_sh.shape[0], b_ex.shape[0]
    swap = core == 1
    blocks = []
    for index in range(columns // LANES):
        spot = pl.ds(index // 2 * 16, 16)
        pair = mine[spot, :].astype(F32), other[spot, :].astype(F32)
        blocks.append(jnp.where(swap, pair[1 - index % 2], pair[index % 2]))
    small = jnp.concatenate(blocks, axis=1)
    for row, ref in ((0, b_sh), (1, gain2), (2, shift2), (3, b_out), (6, gain1), (7, shift1)):
        ref[...] = small[row, :width]
    b_ex[...] = small[4]
    b_in[0:1, :] = small[5:6, :width]
    b_in[1:2, :] = small[5:6, 2 * width : 3 * width]
    for copy in leaving:
        copy.wait()


def kernel_touch(*refs):
    del refs


VMEM = pl.BlockSpec(memory_space=pltpu.VMEM)
SMEM = pl.BlockSpec(memory_space=pltpu.SMEM)
ANY = pl.BlockSpec(memory_space=pl.ANY)


def params(mib):
    return pltpu.CompilerParams(vmem_limit_bytes=mib * 1024 * 1024)


def cost(flops, moved):
    return pl.CostEstimate(flops=int(flops), bytes_accessed=int(moved), transcendentals=0)


def shape(dims, dtype):
    return jax.ShapeDtypeStruct(dims, dtype)


def packed_rows(columns, small, pieces):
    half = columns // LANES * 192 + (small // LANES + 1) // 2 * 16
    return pieces * (-(-half // (8 * pieces)) * 8)


def attention_scratch(pairs):
    return [
        [pltpu.VMEM((pairs, WIN, 2 * WIN), F32)] * 2,
        [pltpu.VMEM((8, 2 * WIN), F32)] * 2,
        [pltpu.VMEM((pairs, 2 * WIN, WIN), BF16)] * 2,
        [pltpu.VMEM((8, 2 * WIN), F32)] * 2,
    ]


def own_part(segments, gain1, shift1, b_in, x, w_in):
    rows, width = x.shape
    total = rows + TILE
    pairs = width // (2 * HD)
    vmem = pltpu.VMEM
    return pl.pallas_call(
        kernel_own,
        out_shape=(
            shape((rows, 3 * width), BF16),
            shape((total, width), BF16),
            shape((rows, width), BF16),
            shape((GROUPS, pairs, 2 * WIN, WIN), BF16),
            shape((GROUPS, 8, WIN), F32),
            shape((GROUPS + 1, 8), jnp.int32),
        ),
        in_specs=[ANY] * 6,
        out_specs=(ANY, ANY, ANY, ANY, VMEM, SMEM),
        scratch_shapes=[
            vmem(segments.shape, jnp.int32),
            vmem(gain1.shape, F32),
            vmem(shift1.shape, F32),
            vmem(b_in.shape, F32),
            vmem((rows, width), BF16),
            vmem(w_in.shape, BF16),
            vmem((total, 3 * width), BF16),
            vmem((total, width), BF16),
            vmem((8, LANES), jnp.int32),
            pltpu.SMEM((8, LANES), jnp.int32),
            *attention_scratch(pairs),
            vmem((GROUPS, pairs, 2 * WIN, WIN), BF16),
            pltpu.SemaphoreType.DMA((16,)),
            pltpu.SemaphoreType.DMA((rows // OWN + 1,)),
        ],
        compiler_params=params(63),
        cost_estimate=cost(2 * 6 * rows * width * 3 * width, 1e7),
        name="own_part",
    )(segments, gain1, shift1, b_in, x, w_in)


def rest_part(table, vectors, x, cot, halo, triple, attended, scaled, raised, stats, w_in, w_out, w_ex, w_sh, pieces):
    rows, width = x.shape
    total = rows + TILE
    hidden = w_ex.shape[1]
    packed = packed_rows(2 * hidden + 4 * width, hidden, pieces)
    vmem = pltpu.VMEM
    pairs = width // (2 * HD)
    square, row = vmem((pairs, WIN, 2 * WIN), F32), vmem((8, 2 * WIN), F32)
    low = vmem((pairs, WIN, 2 * WIN), BF16)
    return pl.pallas_call(
        kernel_rest,
        out_shape=(
            shape((total, width), F32),
            shape((total, width), F32),
            shape((total, hidden), BF16),
            shape((total, 3 * width), BF16),
            shape((TILE, width), BF16),
            shape((packed, LANES), BF16),
            shape((packed, LANES), BF16),
        ),
        in_specs=[SMEM] + [ANY] * 19,
        out_specs=tuple([ANY] * 7),
        scratch_shapes=[
            vmem((total, width), BF16),
            vmem((total, width), BF16),
            vmem(w_in.shape, BF16),
            vmem(w_out.shape, BF16),
            vmem(w_ex.shape, BF16),
            vmem(w_sh.shape, BF16),
            vmem((total, 3 * width), BF16),
            vmem((total, width), BF16),
            vmem((total, width), F32),
            vmem((total, width), F32),
            vmem((total, width), BF16),
            vmem((total, hidden), BF16),
            vmem((total, 3 * width), BF16),
            vmem((GROUPS, 8, WIN), F32),
            vmem((width, hidden), F32),
            vmem((width, hidden), F32),
            vmem((width, width), F32),
            vmem((width, 3 * width), F32),
            vmem((16, 3 * width), F32),
            vmem((16, hidden), F32),
            [square],
            [row],
            [vmem((pairs, 2 * WIN, WIN), BF16)],
            [row],
            [vmem((pairs, 2 * HD, WIN), BF16)] * 2,
            [low] * 2,
            vmem((SLOTS, pairs, 2 * WIN, WIN), BF16),
            vmem((TILE, width), BF16),
            vmem((packed, LANES), BF16),
            vmem((packed, LANES), BF16),
            pltpu.SemaphoreType.DMA((40,)),
            pltpu.SemaphoreType.DMA((2,)),
            pltpu.SemaphoreType.DMA((SLOTS,)),
            *[vmem(v.shape, F32) for v in vectors],
        ],
        compiler_params=params(62),
        cost_estimate=cost(2 * 9 * rows * width * (3 * width + 8 * width), 3e7),
        name="rest_part",
    )(table, *vectors, x, cot, halo, triple, attended, scaled, raised, stats, w_in, w_out, w_ex, w_sh)


def row_outputs(begin, after, table, gain1, b_sh, x, w_in, triple_grad, middle_grad, middle, hidden, w_sh):
    rows, width = x.shape
    vmem = pltpu.VMEM
    if rows > TILE:
        out_shape = (shape((rows, width), F32), shape((rows, width), BF16))
    else:
        out_shape = (shape((2 * HALO, width), BF16),)
    return pl.pallas_call(
        partial(kernel_rows, begin, begin + rows),
        out_shape=out_shape,
        in_specs=[ANY, SMEM, VMEM, VMEM] + [ANY] * 7,
        out_specs=(ANY,) * len(out_shape),
        scratch_shapes=[
            vmem((rows, width), BF16),
            vmem(w_in.shape, BF16),
            vmem((rows, 3 * width), BF16),
            vmem((rows, width), F32),
            vmem((rows, width), F32),
            vmem((rows, hidden.shape[1]), BF16),
            vmem(w_sh.shape, BF16),
            vmem((rows, width), BF16),
            vmem((2 * HALO, width), BF16),
            pltpu.SemaphoreType.DMA((8,)),
            pltpu.SemaphoreType.DMA((max(rows // BLOCK, 1), 6)),
        ],
        compiler_params=params(63),
        cost_estimate=cost(2 * rows * width * 16 * width, rows * 13e3),
        name="row_outputs",
    )(after, table, gain1, b_sh, x, w_in, triple_grad, middle_grad, middle, hidden, w_sh)


def add_halves(mine, other):
    return pl.pallas_call(
        kernel_add,
        out_shape=shape(mine.shape, BF16),
        in_specs=[ANY, ANY],
        out_specs=ANY,
        scratch_shapes=[
            pltpu.VMEM(mine.shape, BF16), pltpu.VMEM(mine.shape, BF16), pltpu.SemaphoreType.DMA((4, 3)),
        ],
        compiler_params=params(63),
        cost_estimate=cost(mine.size, mine.size * 6),
        name="add_halves",
    )(mine, other)


def sum_parts(after, parts):
    return pl.pallas_call(
        partial(kernel_sum, len(after)),
        out_shape=shape(parts.shape, BF16),
        in_specs=[ANY] * (len(after) + 1),
        out_specs=ANY,
        scratch_shapes=[
            pltpu.VMEM(parts.shape, BF16),
            pltpu.VMEM(parts.shape[1:], BF16),
            pltpu.SemaphoreType.DMA((5,)),
        ],
        compiler_params=params(63),
        cost_estimate=cost(parts.size, parts.size * 4),
        name="sum_parts",
    )(*after, parts)


def half_shapes(width, hidden):
    dims = ((width, hidden), (width, width), (width, 3 * width), (hidden, width))
    scratch = [pltpu.VMEM((rows // 2, columns), F32) for rows, columns in dims]
    return tuple(shape(dim, F32) for dim in dims), [*scratch, pltpu.SemaphoreType.DMA((8,))]


def unpack_first(packed, width, hidden):
    shapes, scratch = half_shapes(width, hidden)
    return pl.pallas_call(
        kernel_first_half,
        out_shape=shapes,
        in_specs=[ANY],
        out_specs=(ANY,) * 4,
        scratch_shapes=[pltpu.VMEM(packed.shape, BF16), *scratch],
        compiler_params=params(63),
        cost_estimate=cost(packed.size, packed.size * 6),
        name="unpack_first",
    )(packed)


def unpack_second(packed, first, kept, used, width, hidden):
    shapes, scratch = half_shapes(width, hidden)
    rows = first.shape[0] - used
    small = tuple(shape(dims, F32) for dims in ((2, width),) + ((width,),) * 4 + ((hidden,), (width,), (width,)))
    return pl.pallas_call(
        kernel_second_half,
        out_shape=shapes + small,
        in_specs=[ANY] * 6,
        out_specs=(ANY,) * 4 + (VMEM,) * 8,
        scratch_shapes=[
            pltpu.VMEM(packed.shape, BF16), *scratch, pltpu.VMEM((rows, LANES), BF16), pltpu.VMEM((rows, LANES), BF16),
            pltpu.SemaphoreType.DMA((2,)),
        ],
        input_output_aliases={2: 0, 3: 1, 4: 2, 5: 3},
        compiler_params=params(63),
        cost_estimate=cost(packed.size, packed.size * 6),
        name="unpack_second",
    )(packed, first, *kept)


def touch(value, *after):
    return pl.pallas_call(
        kernel_touch,
        out_shape=shape(value.shape, value.dtype),
        in_specs=[ANY] * (1 + len(after)),
        out_specs=ANY,
        input_output_aliases={0: 0},
        name="touch",
    )(value, *after)


def same_core_groups():
    packs, parts = lax.axis_size("dp"), lax.axis_size("mp")
    return [[d * parts + m for d in range(c, packs, 2) for m in range(parts)] for c in range(2)]


def swap_cores(block):
    packs = lax.axis_size("dp")
    return lax.ppermute(block, "dp", [(i, i ^ 1) for i in range(packs)])


def exchange(parts):
    return lax.all_to_all(parts, ("dp", "mp"), 0, 0, axis_index_groups=same_core_groups())


def passed(block, distance):
    count = lax.axis_size("mp")
    route = [(i, i + distance) for i in range(count) if 0 <= i + distance < count]
    return lax.ppermute(block, "mp", route)


def kernel_take_over(table, halo_in, input_in, result_in, input_out, result_out, halo, input_own, result_own, sems):
    rows = pl.ds(0, HALO)
    copies = [
        pltpu.make_async_copy(halo_in, halo, sems.at[0]),
        pltpu.make_async_copy(input_in.at[rows], input_own, sems.at[1]),
        pltpu.make_async_copy(result_in.at[rows], result_own, sems.at[2]),
    ]
    for copy in copies:
        copy.start()
    for copy in copies:
        copy.wait()
    other = lax.broadcasted_iota(jnp.int32, (HALO, 1), 0) < table[GROUPS, 1]
    input_own[...] = jnp.where(other, halo[:HALO, :].astype(F32), input_own[...])
    result_own[...] = jnp.where(other, halo[HALO:, :].astype(F32), result_own[...].astype(F32)).astype(BF16)
    copies = [
        pltpu.make_async_copy(input_own, input_out.at[rows], sems.at[3]),
        pltpu.make_async_copy(result_own, result_out.at[rows], sems.at[4]),
    ]
    for copy in copies:
        copy.start()
    for copy in copies:
        copy.wait()


def take_over(table, halo, input_grad, result):
    width = input_grad.shape[1]
    return pl.pallas_call(
        kernel_take_over,
        out_shape=(shape(input_grad.shape, F32), shape(result.shape, BF16)),
        in_specs=[SMEM, ANY, ANY, ANY],
        out_specs=(ANY, ANY),
        scratch_shapes=[
            pltpu.VMEM(halo.shape, BF16), pltpu.VMEM((HALO, width), F32), pltpu.VMEM((HALO, width), BF16),
            pltpu.SemaphoreType.DMA((5,)),
        ],
        input_output_aliases={2: 0, 3: 1},
        compiler_params=params(63),
        name="take_over",
    )(table, halo, input_grad, result)


def body(
    layer_input, segments, cotangent, first_gain, first_shift, inward_weight, inward_bias, outward_weight,
    outward_bias, second_gain, second_shift, expand_weight, expand_bias, shrink_weight, shrink_bias,
):
    rows, width = layer_input.shape
    hidden_width = expand_weight.shape[1]
    pieces = lax.axis_size("dp") * lax.axis_size("mp") // 2
    gain1, shift1, b_out, gain2, shift2, b_ex, b_sh = (
        first_gain, first_shift, outward_bias, second_gain, second_shift, expand_bias, shrink_bias
    )
    halo = passed(jnp.concatenate([layer_input[:HALO], cotangent[:HALO]], axis=0), -1)
    triple, attended, scaled, raised, stats, table = own_part(
        segments, gain1, shift1, inward_bias, layer_input, inward_weight
    )
    middle, middle_grad, hidden, triple_grad, edge, mine, other = rest_part(
        table, (gain1, shift1, inward_bias, b_out, gain2, shift2, b_ex), layer_input, cotangent, halo, triple,
        attended, scaled, raised, stats, inward_weight, outward_weight, expand_weight, shrink_weight, pieces,
    )
    both = add_halves(mine, swap_cores(other))
    parts = exchange(both.reshape(pieces, -1, LANES))
    kept = (inward_weight, triple_grad, middle_grad, middle, hidden, shrink_weight)
    (halo,) = row_outputs(rows, both, table, gain1, b_sh, edge, *kept)
    other_halo = passed(halo, 1)
    input_grad, result = row_outputs(0, halo, table, gain1, b_sh, layer_input, *kept)
    summed = sum_parts((other_halo, result), parts)
    mine = exchange(summed).reshape(-1, LANES)
    input_grad, result = take_over(table, touch(other_halo, summed), input_grad, result)
    mine = touch(mine, input_grad, result)
    other = swap_cores(mine)
    used = 192 * (2 * hidden_width + 4 * width) // LANES
    half = unpack_first(mine, width, hidden_width)
    d_ex, d_out, d_in, d_sh, d_b_in, d_b_sh, d_gain2, d_shift2, d_b_out, d_b_ex, d_gain1, d_shift1 = unpack_second(
        other, mine, half, used, width, hidden_width
    )
    return (
        result, input_grad, d_gain1, d_shift1, d_in, d_b_in, d_out, d_b_out, d_gain2, d_shift2, d_ex, d_b_ex, d_sh,
        d_b_sh,
    )


def solution(mesh):
    rows = P(("dp", "mp"), None)
    in_specs = (rows, P("dp", None), rows) + (P(),) * 12
    out_specs = (rows, rows) + (P(),) * 12
    return jax.shard_map(body, mesh=mesh, in_specs=in_specs, out_specs=out_specs, check_vma=False)
```

```python
from functools import partial

import jax
import jax.numpy as jnp
from jax import lax
from jax.experimental import pallas as pl
from jax.experimental.pallas import tpu as pltpu
from jax.sharding import PartitionSpec as P

HD = 64
SEQ = 198
EPSILON = 1e-06
MASKED = -1000000000.0
LOG2E = 1.4426950408889634
WIN = 256
TILE = 256
HALO = 208
WIDE = 768
OWN = 1024
BLOCK = 512
GROUPS = 24
SLOTS = 5
LANES = 128
CHUNK = 256
FEED = 768
BIG = 1 << 20
F32 = jnp.float32
BF16 = jnp.bfloat16
NT = (((1,), (1,)), ((), ()))
TN = (((0,), (0,)), ((), ()))


def row_of(ref):
    return ref[...].reshape(1, -1)


def dot(a, b):
    return jnp.dot(a, b, preferred_element_type=F32)


def dot_nt(a, b):
    return lax.dot_general(a, b, NT, preferred_element_type=F32)


def dot_tn(a, b):
    return lax.dot_general(a, b, TN, preferred_element_type=F32)


def normalize(rows):
    center = jnp.mean(rows, axis=-1, keepdims=True)
    centred = rows - center
    spread = jnp.mean(centred * centred, axis=-1, keepdims=True)
    inverse = lax.rsqrt(spread + EPSILON)
    return centred * inverse, inverse


def normalize_back(upstream, scaled, inverse, gain):
    direct = upstream * gain
    first = jnp.mean(direct, axis=-1, keepdims=True)
    second = jnp.mean(direct * scaled, axis=-1, keepdims=True)
    return inverse * (direct - first - scaled * second)


def gelu_parts(v, half_upstream):
    scaled = v * 0.7071067811865476
    double = 1.0 + lax.erf(scaled)
    bell = jnp.exp2((scaled * scaled) * -1.4426950408889634)
    return (0.5 * v) * double, half_upstream * (double + (v * 0.7978845608028654) * bell)


def image_ends(seg, base, work):
    ident = lax.broadcasted_iota(jnp.int32, (LANES, LANES), 0)
    below = jnp.zeros((LANES, LANES), F32)
    for begin in range(0, seg.shape[1], LANES):
        row = seg[0:1, begin : begin + LANES]
        row = jnp.where(row < 0, BIG, row)
        below = below + jnp.where(row <= ident, 1.0, 0.0)
    ends = jnp.broadcast_to(jnp.sum(below, axis=1, keepdims=True), (LANES, LANES))
    started = jnp.sum(jnp.where(ends < base.astype(F32), 1.0, 0.0), axis=0, keepdims=True)
    work[0:1, :] = ends.T[0:1].astype(jnp.int32)
    work[1:2, :] = started.astype(jnp.int32)


def plan_groups(ends, position, rows, table):
    base = position * rows
    limit = jnp.minimum(base + rows, ends[0, LANES - 1]) - base
    image = jnp.where(position == 0, 0, ends[1, 0] + 1)
    first = jnp.where(position == 0, 0, ends[0, jnp.maximum(image - 1, 0)]) - base

    def body(state):
        at, image, group, window, start, c1, c2 = state
        after = ends[0, jnp.minimum(image, LANES - 1)] - base
        fits = after - window <= WIN

        @pl.when(jnp.logical_not(fits))
        def _():
            write_group(table, group, window, start, c1, c2, at)

        group = jnp.where(fits, group, group + 1)
        new_c1 = jnp.where(fits, jnp.where(at == start, c1, jnp.where(c1 < 0, at, c1)), -1)
        new_c2 = jnp.where(fits, jnp.where(jnp.logical_and(at != start, c1 >= 0), jnp.where(c2 < 0, at, c2), c2), -1)
        start = jnp.where(fits, start, at)
        window = jnp.where(fits, window, (at // 16) * 16)
        return after, image + 1, group, window, start, new_c1, new_c2

    init = (first, image, jnp.int32(0), (first // 16) * 16, first, jnp.int32(-1), jnp.int32(-1))
    at, image, group, window, start, c1, c2 = lax.while_loop(lambda s: s[0] < limit, body, init)
    write_group(table, group, window, start, c1, c2, at)
    table[GROUPS, 0] = group + 1
    table[GROUPS, 1] = first
    table[GROUPS, 2] = at


def write_group(table, group, window, start, c1, c2, end):
    table[group, 0] = window
    table[group, 1] = start - window
    table[group, 2] = jnp.where(c1 < 0, end, c1) - window
    table[group, 3] = jnp.where(c2 < 0, end, c2) - window
    table[group, 4] = end - window


def group_bias(table, group):
    bounds = [table[group, i] for i in range(1, 5)]
    row = lax.broadcasted_iota(jnp.int32, (WIN, LANES), 0)
    col = lax.broadcasted_iota(jnp.int32, (1, WIN), 1)

    def ident(index):
        return sum((index >= b).astype(jnp.int32) for b in bounds)

    row, col = ident(row), ident(col)
    return jnp.concatenate(
        [jnp.where(row == col[:, at : at + LANES], 0.0, MASKED) for at in range(0, WIN, LANES)], axis=1
    )


def group_mask_factors(table, group):
    bounds = [table[group, i] for i in range(1, 5)]

    def ident(index):
        return sum((index >= b).astype(jnp.int32) for b in bounds)

    row = ident(lax.broadcasted_iota(jnp.int32, (WIN, LANES), 0))
    left = jnp.where(row == lax.broadcasted_iota(jnp.int32, (WIN, LANES), 1), 1.0, 0.0).astype(BF16)
    col = ident(lax.broadcasted_iota(jnp.int32, (1, WIN), 1))
    kind = lax.broadcasted_iota(jnp.int32, (16, WIN), 0)
    right = jnp.where(kind == col, 0.0, MASKED).astype(BF16)
    right = jnp.concatenate([right, jnp.zeros((LANES - 16, WIN), BF16)], axis=0)
    return left, jnp.concatenate([right, right], axis=1)


def head_masks():
    lane = lax.broadcasted_iota(jnp.int32, (WIN, 2 * HD), 1)
    return lane < HD, lane >= HD


def keep_first(ref, window, begin, cols, value):
    head = pl.ds(window, 16)
    old = ref[head, cols]
    row = lax.broadcasted_iota(jnp.int32, (16, 2 * HD), 0)
    ref[head, cols] = jnp.where(row >= begin, value[:16].astype(F32), old.astype(F32)).astype(BF16)
    ref[pl.ds(window + 16, WIN - 16), cols] = value[16:].astype(BF16)


def block_diagonal(pair_t):
    zero = jnp.zeros((HD, pair_t.shape[1]), pair_t.dtype)
    return jnp.concatenate(
        [jnp.concatenate([pair_t[:HD], zero], axis=1), jnp.concatenate([zero, pair_t[HD:]], axis=1)], axis=0
    )


def pipelined(groups, first, second, third, keep_copy):
    def clamped(group):
        return jnp.minimum(group, groups - 1)

    def half(group, slot):
        first(clamped(group), slot)
        second(clamped(group - 1), 1 - slot)
        third(clamped(group - 2), slot)

    first(0, 0)
    first(clamped(1), 1)
    second(0, 0)
    steps = (groups + 1) // 2

    def both(step, _):
        keep_copy(clamped(2 * step)).start()

        @pl.when(step > 0)
        def _():
            keep_copy(clamped(2 * step - 1)).start()

        half(2 * step + 2, 0)
        half(2 * step + 3, 1)
        return 0

    lax.fori_loop(0, steps, both, 0)
    keep_copy(clamped(2 * steps - 1)).start()

    def settle(_, carry):
        keep_copy(0).wait()
        return carry

    return lambda: lax.fori_loop(0, 2 * steps, settle, 0)


def group_rows(table, group):
    return pl.ds(pl.multiple_of(table[group, 0], 16), WIN)


def attend_groups(groups, table, triple, attended, stats, scores, peaks, raised, scales, alone=None, kept=None, keep_copy=None):
    width = attended.shape[1]
    pairs = range(width // (2 * HD))

    def first(group, slot):
        rows = group_rows(table, group)
        left, right = group_mask_factors(table, group)
        for pair in pairs:
            query_t = triple[rows, pl.ds(pair * 2 * HD, 2 * HD)].T
            key = triple[rows, pl.ds(width + pair * 2 * HD, 2 * HD)]
            value = dot(
                jnp.concatenate([key, left], axis=1), jnp.concatenate([block_diagonal(query_t), right], axis=0)
            )
            scores[slot][pair] = value
            peaks[slot][pair : pair + 1, :] = jnp.max(value, axis=0, keepdims=True)

    def second(group, slot):
        for pair in pairs:
            peak = peaks[slot][pair : pair + 1, :]
            value = jnp.exp2(scores[slot][pair] - peak)
            total = jnp.sum(value, axis=0, keepdims=True)
            low = value.astype(BF16)
            raised[slot][pair, :WIN] = low[:, :WIN]
            raised[slot][pair, WIN:] = low[:, WIN:]
            if kept is not None:
                kept[group, pair, :WIN] = low[:, :WIN]
                kept[group, pair, WIN:] = low[:, WIN:]
            scale = 1.0 / total
            scales[slot][pair : pair + 1, :] = scale
            stats[group, pl.ds(2 * pair, 1), :] = scale[:, :WIN]
            stats[group, pl.ds(2 * pair + 1, 1), :] = scale[:, WIN:]

    def third(group, slot):
        rows = group_rows(table, group)
        for pair in pairs:
            value_t = block_diagonal(triple[rows, pl.ds(2 * width + pair * 2 * HD, 2 * HD)].T)
            out = dot(value_t, raised[slot][pair])
            scale = scales[slot][pair : pair + 1, :]
            out = jnp.concatenate([out[:HD] * scale[:, :WIN], out[HD:] * scale[:, WIN:]], axis=0)
            keep_first(attended, rows.start, table[group, 1], pl.ds(pair * 2 * HD, 2 * HD), out.T)

    if alone is None:
        return pipelined(groups, first, second, third, keep_copy)
    for part in (first, second, third):
        part(alone, 0)
    return None


def attend_back_groups(
    groups, table, triple, attended, upstream, stats, triple_grad, scores_grads, scaled_up, kept, kept_copy
):
    width = attended.shape[1]
    pairs = range(width // (2 * HD))
    masks = head_masks()

    def columns(pair, block):
        return pl.ds(block * width + pair * 2 * HD, 2 * HD)

    def side_by_side(turn, pair):
        low = kept[lax.rem(turn, SLOTS), pair]
        return jnp.concatenate([low[:WIN], low[WIN:]], axis=1)

    def first(turn, group, slot):
        rows = group_rows(table, group)
        for pair in pairs:
            scale = [jnp.broadcast_to(stats[group, pl.ds(2 * pair + h, 1), :], (HD, WIN)) for h in range(2)]
            up_t = upstream[rows, columns(pair, 0)].T.astype(F32) * jnp.concatenate(scale, axis=0)
            product = attended[rows, columns(pair, 0)].T.astype(F32) * up_t
            agreement = jnp.concatenate(
                [jnp.sum(product[:HD], axis=0, keepdims=True), jnp.sum(product[HD:], axis=0, keepdims=True)], axis=1
            )
            up_low = up_t.astype(BF16)
            scaled_up[slot][pair] = up_low
            probs_grad = dot(triple[rows, columns(pair, 2)], block_diagonal(up_low))
            prob = side_by_side(turn, pair).astype(F32)
            scores_grads[slot][pair] = (prob * (probs_grad - agreement)).astype(BF16)

    def stacked(pair_rows):
        zero = jnp.zeros_like(pair_rows)
        return jnp.concatenate([jnp.where(mask, pair_rows, zero) for mask in masks], axis=0)

    def second(turn, group, slot):
        rows = group_rows(table, group)
        window, begin = rows.start, table[group, 1]
        for pair in pairs:
            scores_grad = scores_grads[slot][pair]
            value_grad = dot_nt(side_by_side(turn, pair), block_diagonal(scaled_up[slot][pair]))
            key_grad = dot(scores_grad, stacked(triple[rows, columns(pair, 0)]))
            key_t = block_diagonal(triple[rows, columns(pair, 1)].T)
            query_grad = dot(key_t, jnp.concatenate([scores_grad[:, :WIN], scores_grad[:, WIN:]], axis=0))
            keep_first(triple_grad, window, begin, columns(pair, 0), (query_grad * HD ** (-0.5)).T)
            keep_first(triple_grad, window, begin, columns(pair, 1), key_grad * (1.0 / LOG2E))
            keep_first(triple_grad, window, begin, columns(pair, 2), value_grad)

    def clamped(turn):
        return jnp.minimum(turn, groups - 1)

    def half(turn, slot):
        first(turn, clamped(turn), slot)
        second(turn - 1, clamped(turn - 1), 1 - slot)

    steps = (groups + 1) // 2

    def fetch(turn):
        kept_copy(clamped(turn), lax.rem(turn, SLOTS))

    def arrived(turn):
        kept_copy(None, lax.rem(turn, SLOTS))

    arrived(jnp.int32(0))
    first(jnp.int32(0), 0, 0)

    def both(step, _):
        @pl.when(step + 1 < steps)
        def _():
            fetch(2 * step + 3)
            fetch(2 * step + 4)

        arrived(2 * step + 1)
        arrived(2 * step + 2)
        half(2 * step + 1, 1)
        half(2 * step + 2, 0)
        return 0

    lax.fori_loop(0, steps, both, 0)


def interval(tile, first, end, size=TILE):
    row = lax.broadcasted_iota(jnp.int32, (size, 1), 0) + tile * size
    return jnp.logical_and(row >= first, row < end)


class Mover:
    def __init__(self, sems):
        self.sems = sems
        self.count = 0

    def start(self, source, target):
        copy = pltpu.make_async_copy(source, target, self.sems.at[self.count])
        self.count += 1
        copy.start()
        return copy


def project_rows(rows, gain1, shift1, w_in, b_in, target, spot, scaled_ref, scaled_spot):
    width = rows.shape[1]
    scaled, _inverse = normalize(rows)
    scaled_ref[scaled_spot, :] = scaled.astype(BF16)
    normed = (scaled * row_of(gain1) + row_of(shift1)).astype(BF16)
    q = dot(normed, w_in[:, :width]) + b_in[0:1, :]
    target[spot, :width] = (q.astype(BF16).astype(F32) * (HD ** (-0.5) * LOG2E)).astype(BF16)
    target[spot, width : 2 * width] = dot(normed, w_in[:, width : 2 * width]).astype(BF16)
    target[spot, 2 * width :] = (dot(normed, w_in[:, 2 * width :]) + b_in[1:2, :]).astype(BF16)


def kernel_own(
    seg_in, gain1_in, shift1_in, b_in_in, x_in, w_in_in,
    triple_out, attended_out, scaled_out, raised_out, stats, table,
    seg, gain1, shift1, b_in, x, w_in, triple, attended, work, ends, scores, peaks, raised, scales, kept, sems, tile_sems,
):
    rows, width = x_in.shape
    move = Mover(sems)
    seg_copy = move.start(seg_in, seg)
    early = [
        move.start(gain1_in, gain1), move.start(shift1_in, shift1), move.start(b_in_in, b_in),
        move.start(x_in, x), move.start(w_in_in, w_in),
    ]
    seg_copy.wait()
    image_ends(seg, lax.axis_index("mp") * rows, work)
    end_copy = move.start(work, ends)
    attended[...] = jnp.zeros_like(attended)
    spare = pl.ds(rows, triple.shape[0] - rows)
    triple[spare, :] = jnp.zeros((triple.shape[0] - rows, 3 * width), BF16)
    for copy in early:
        copy.wait()

    def step_copy(step):
        spot = pl.ds(pl.multiple_of(step * OWN, OWN), OWN)
        return pltpu.make_async_copy(triple.at[spot], triple_out.at[spot], tile_sems.at[step])

    def step_rows(step, _):
        spot = pl.ds(pl.multiple_of(step * OWN, OWN), OWN)
        project_rows(x[spot, :].astype(F32), gain1, shift1, w_in, b_in, triple, spot, x, spot)
        step_copy(step).start()
        return 0

    lax.fori_loop(0, rows // OWN, step_rows, 0)
    scaled_copy = move.start(x, scaled_out)
    end_copy.wait()
    plan_groups(ends, lax.axis_index("mp"), rows, table)

    def keep_copy(group):
        return pltpu.make_async_copy(kept.at[group], raised_out.at[group], tile_sems.at[rows // OWN])

    settle = attend_groups(
        jnp.maximum(table[GROUPS, 0] - 1, 1), table, triple, attended, stats, scores, peaks, raised, scales,
        kept=kept, keep_copy=keep_copy,
    )
    leaving = move.start(attended, attended_out)
    scaled_copy.wait()
    settle()
    for step in range(rows // OWN):
        step_copy(step).wait()
    leaving.wait()


def kernel_rest(
    table, *refs
):
    vectors_in, refs = refs[:7], refs[7:]
    vectors, refs = refs[-7:], refs[:-7]
    rest_body(table, vectors_in, vectors, *refs)


def rest_body(
    table, vectors_in, vectors,
    x_in, cot_in, halo_in, triple_in, attended_in, scaled_in, raised_in, stats_in, w_in_in, w_out_in, w_ex_in, w_sh_in,
    middle_out, middle_grad_out, hidden_out, triple_grad_out, edge_out, mine_out, other_out,
    x, back, w_in, w_out, w_ex, w_sh, triple, attended, middle, middle_grad, upstream, hidden, triple_grad, stats,
    d_ex, d_sh, d_out, product, sums, small, scores, peaks, raised, scales, scaled_up, scores_grads,
    kept, edge, mine, other, sems, tile_sems, kept_sems,
):
    rows, width = x_in.shape
    total = x.shape[0]
    tiles = total // FEED
    normed2, normed_grad = upstream, middle_grad
    move = Mover(sems)
    own, over = pl.ds(0, rows), pl.ds(rows, HALO)
    gain1, shift1, b_in, b_out, gain2, shift2, b_ex = vectors
    near, far = pl.ds(2 * WIDE, rows - 2 * WIDE), pl.ds(0, 2 * WIDE)
    first_copies = [move.start(halo_in.at[pl.ds(0, HALO)], x.at[over])]
    first_copies += [move.start(source, target) for source, target in zip(vectors_in, vectors)]
    first_copies.append(move.start(w_in_in, w_in))
    early = [
        move.start(triple_in.at[near], triple.at[near]),
        move.start(stats_in, stats),
        move.start(attended_in, attended),
    ]
    late = [
        move.start(w_out_in, w_out),
        move.start(x_in, x.at[own]),
        move.start(cot_in, back.at[own]),
        move.start(halo_in.at[pl.ds(HALO, HALO)], back.at[over]),
    ]
    weight_copies = [move.start(w_ex_in, w_ex), move.start(w_sh_in, w_sh)]
    last = move.start(triple_in.at[far], triple.at[far])
    rest = pl.ds(rows + HALO, total - rows - HALO)
    x[rest, :] = jnp.zeros((total - rows - HALO, width), BF16)
    back[rest, :] = jnp.zeros((total - rows - HALO, width), BF16)
    for ref in (d_ex, d_sh, d_out, product, sums, small, triple_grad):
        ref[...] = jnp.zeros_like(ref)
    groups, first, end = table[GROUPS, 0], table[GROUPS, 1], table[GROUPS, 2]
    for copy in first_copies:
        copy.wait()
    tail = pl.ds(rows, TILE)
    edge_copy = move.start(x.at[tail], edge_out)
    project_rows(x[tail, :].astype(F32), gain1, shift1, w_in, b_in, triple, tail, edge, slice(None))
    for copy in early:
        copy.wait()
    attend_groups(groups, table, triple, attended, stats, scores, peaks, raised, scales, alone=groups - 1)
    def kept_copy(group, slot):
        if group is None:
            pltpu.make_async_copy(raised[0], kept.at[slot], kept_sems.at[slot]).wait()
            return

        @pl.when(group == groups - 1)
        def _():
            pltpu.make_async_copy(raised[0], kept.at[slot], kept_sems.at[slot]).start()

        @pl.when(group != groups - 1)
        def _():
            pltpu.make_async_copy(raised_in.at[group], kept.at[slot], kept_sems.at[slot]).start()

    for turn in range(3):
        kept_copy(jnp.int32(turn), turn)
    for copy in late:
        copy.wait()
    leaving = []

    hidden_width = w_ex.shape[1]
    begins = list(range(0, hidden_width, CHUNK))

    def wide_rows(step):
        return pl.ds(step * WIDE, WIDE)

    def before_feed(step, _):
        spot = wide_rows(step)
        value = x[spot, :].astype(F32) + dot(attended[spot, :], w_out[...]) + row_of(b_out)
        scaled, _inverse = normalize(value)
        middle[spot, :] = value
        normed2[spot, :] = (scaled * row_of(gain2) + row_of(shift2)).astype(BF16)
        keep = interval(step, first, end, WIDE)
        back[spot, :] = jnp.where(keep, back[spot, :].astype(F32), 0.0).astype(BF16)
        return 0

    def feed(tile, _):
        spot = pl.ds(pl.multiple_of(tile * FEED, FEED), FEED)
        normed = normed2[spot, :]
        back_low = back[spot, :]
        back_half = (0.5 * back_low.astype(F32)).astype(BF16)

        def first_part(begin):
            cols = slice(begin, begin + CHUNK)
            before = dot(normed, w_ex[:, cols]) + b_ex[cols].reshape(1, -1)
            return before, dot_nt(back_half, w_sh[cols, :])

        held = [first_part(begins[0])]
        total_grad = jnp.zeros((width, FEED), F32)
        for index, begin in enumerate(begins):
            cols = slice(begin, begin + CHUNK)
            if index + 1 < len(begins):
                held.append(first_part(begins[index + 1]))
            value, grad = gelu_parts(*held[index])
            value, grad = value.astype(BF16), grad.astype(BF16)
            hidden[spot, cols] = value
            total_grad = total_grad + dot_nt(w_ex[:, cols], grad)
            d_sh[:, cols] += dot_tn(back_low, value)
            d_ex[:, cols] += dot_tn(normed, grad)
            small[4:5, cols] += jnp.sum(grad.astype(F32), axis=0, keepdims=True)
        normed_grad[spot, :] = total_grad.T
        pltpu.make_async_copy(hidden.at[spot], hidden_out.at[spot], tile_sems.at[0]).start()
        return 0

    def after_feed(step, _):
        spot = wide_rows(step)
        back32 = back[spot, :].astype(F32)
        scaled, inverse = normalize(middle[spot, :])
        upstream2 = normed_grad[spot, :]
        small[0:1, :width] += jnp.sum(back32, axis=0, keepdims=True)
        small[1:2, :width] += jnp.sum(upstream2 * scaled, axis=0, keepdims=True)
        small[2:3, :width] += jnp.sum(upstream2, axis=0, keepdims=True)
        grad = back32 + normalize_back(upstream2, scaled, inverse, row_of(gain2))
        small[3:4, :width] += jnp.sum(grad, axis=0, keepdims=True)
        middle_grad[spot, :] = grad
        grad_low = grad.astype(BF16)
        d_out[...] += dot_tn(attended[spot, :], grad_low)
        upstream[spot, :] = dot_nt(grad_low, w_out[...]).astype(BF16)
        pltpu.make_async_copy(middle_grad.at[spot], middle_grad_out.at[spot], tile_sems.at[1]).start()
        return 0

    for step in range(total // WIDE):
        before_feed(step, 0)
    for copy in weight_copies:
        copy.wait()
    edge_copy.wait()
    scaled_copy = move.start(scaled_in, x.at[own])
    x[tail, :] = edge[...]
    leaving.append(move.start(middle, middle_out))
    lax.fori_loop(0, tiles, feed, 0)
    for step in range(total // WIDE):
        after_feed(step, 0)
    core = lax.rem(lax.axis_index("dp"), 2)
    for half, target in ((core, mine), (1 - core, other)):
        at = pack((d_out,), half, target, pack_turned(d_sh, half, target, pack((d_ex,), half, target, 0)))
    ready = pl.ds(0, at)
    leaving += [move.start(mine.at[ready], mine_out.at[ready]), move.start(other.at[ready], other_out.at[ready])]
    last.wait()
    attend_back_groups(
        groups, table, triple, attended, upstream, stats, triple_grad, scores_grads, scaled_up, kept, kept_copy
    )
    leaving.append(move.start(triple_grad, triple_grad_out))
    scaled_copy.wait()
    ones = jnp.ones((16, WIDE), BF16)

    def multiply(step, _):
        spot = pl.ds(pl.multiple_of(step * WIDE, WIDE), WIDE)
        grad = triple_grad[spot, :]
        product[...] += dot_tn(x[spot, :], grad)
        sums[...] += dot(ones, grad)
        return 0

    lax.fori_loop(0, total // WIDE, multiply, 0)
    gain = jnp.broadcast_to(row_of(gain1), (LANES, width)).T
    shift = jnp.broadcast_to(row_of(shift1), (LANES, width)).T
    by_gain = jnp.zeros((width, LANES), F32)
    by_shift = jnp.zeros((width, LANES), F32)
    for begin in range(0, 3 * width, LANES):
        cols = slice(begin, begin + LANES)
        block, sum_row = product[:, cols], sums[0:1, cols]
        weight = w_in[:, cols].astype(F32)
        by_gain = by_gain + weight * block
        by_shift = by_shift + weight * sum_row
        product[:, cols] = gain * block + shift * sum_row
    small[5:6, : 3 * width] = sums[0:1, :]
    by_gain = jnp.broadcast_to(jnp.sum(by_gain, axis=1, keepdims=True), (width, LANES)).T
    by_shift = jnp.broadcast_to(jnp.sum(by_shift, axis=1, keepdims=True), (width, LANES)).T
    small[6:7, :width] = by_gain[0:1]
    small[7:8, :width] = by_shift[0:1]
    begin = at
    for half, target in ((core, mine), (1 - core, other)):
        at = pack((product,), half, target, begin)
    pack_small(small, core, mine, other, at)
    ready = pl.ds(begin, mine.shape[0] - begin)
    leaving += [move.start(mine.at[ready], mine_out.at[ready]), move.start(other.at[ready], other_out.at[ready])]
    for copy in leaving:
        copy.wait()
    pltpu.make_async_copy(hidden, hidden_out, tile_sems.at[0]).wait()
    pltpu.make_async_copy(middle_grad, middle_grad_out, tile_sems.at[1]).wait()


def pack(grads, half, target, at):
    for grad in grads:
        count = grad.shape[0] // 2
        rows = pl.ds(pl.multiple_of(half * count, count), count)
        for begin in range(0, grad.shape[1], LANES):
            target[pl.ds(at, count), :] = grad[rows, begin : begin + LANES].astype(BF16)
            at += count
    return at


def pack_turned(grad, half, target, at):
    count, columns = grad.shape[0], grad.shape[1] // 2
    for begin in range(0, columns, LANES):
        cols = pl.ds(pl.multiple_of(half * columns + begin, LANES), LANES)
        target[pl.ds(at, count), :] = grad[:, cols].astype(BF16)
        at += count
    return at


def pack_small(small, core, mine, other, at):
    rest = mine.shape[0] - at
    mine[pl.ds(at, rest), :] = jnp.zeros((rest, LANES), BF16)
    other[pl.ds(at, rest), :] = jnp.zeros((rest, LANES), BF16)
    for index in range(small.shape[1] // LANES):
        value = small[:, index * LANES : (index + 1) * LANES].astype(BF16)
        spot = pl.ds(at + (index // 2) * 16, 16)

        @pl.when(core == index % 2)
        def _():
            mine[spot, :] = value

        @pl.when(core != index % 2)
        def _():
            other[spot, :] = value


def step_copies(arrays, step, sems, skip=0):
    spot = pl.ds(step * WIDE, WIDE)
    return [
        pltpu.make_async_copy(source.at[spot], target.at[spot], sems.at[step, skip + at])
        for at, (source, target) in enumerate(arrays)
    ]


def kernel_rows(
    begin, end, after, table, gain1, b_sh, x_in, w_in_in, triple_grad_in, middle_grad_in, middle_in, hidden_in, w_sh_in,
    *refs,
):
    del after
    outs = 2 if end - begin > TILE else 1
    x, w_in, triple_grad, middle_grad, middle, hidden, w_sh, result, halo, sems, step_sems = refs[outs:]
    move = Mover(sems)
    early = [move.start(w_in_in, w_in), move.start(x_in, x)]
    size = min(BLOCK, end - begin)
    steps = range((end - begin) // size)

    def copies(step, arrays, skip):
        source_rows, rows = pl.ds(begin + step * size, size), pl.ds(step * size, size)
        return [
            pltpu.make_async_copy(source.at[source_rows], target.at[rows], step_sems.at[step, skip + at])
            for at, (source, target) in enumerate(arrays)
        ]

    inward = ((triple_grad_in, triple_grad), (middle_grad_in, middle_grad))
    onward = ((middle_in, middle), (hidden_in, hidden))
    for step in steps:
        for copy in copies(step, inward, 0):
            copy.start()
    weight_copy = move.start(w_sh_in, w_sh)
    for step in steps:
        for copy in copies(step, onward, 2):
            copy.start()
    for copy in early:
        copy.wait()

    def spot_of(step):
        return pl.ds(pl.multiple_of(step * size, size), size)

    def leave(step, value, at):
        spot = spot_of(step)
        return pltpu.make_async_copy(value.at[spot], refs[at].at[spot], step_sems.at[step, 4 + at])

    def input_step(step, _):
        for copy in copies(step, inward, 0):
            copy.wait()
        spot = spot_of(step)
        scaled, inverse = normalize(x[spot, :].astype(F32))
        normed_grad = dot_nt(triple_grad[spot, :], w_in[...])
        middle_grad[spot, :] = middle_grad[spot, :] + normalize_back(normed_grad, scaled, inverse, row_of(gain1))
        if outs == 2:
            leave(step, middle_grad, 0).start()
        return 0

    lax.fori_loop(0, len(steps), input_step, 0)
    weight_copy.wait()

    def result_step(step, _):
        for copy in copies(step, onward, 2):
            copy.wait()
        spot = spot_of(step)
        row = lax.broadcasted_iota(jnp.int32, (size, 1), 0) + begin + step * size
        keep = jnp.logical_and(row >= table[GROUPS, 1], row < table[GROUPS, 2])
        value = middle[spot, :] + row_of(b_sh) + dot(hidden[spot, :], w_sh[...])
        result[spot, :] = jnp.where(keep, value, 0.0).astype(BF16)
        if outs == 2:
            leave(step, result, 1).start()
        return 0

    lax.fori_loop(0, len(steps), result_step, 0)
    if outs == 1:
        halo[:HALO, :] = middle_grad[:HALO, :].astype(BF16)
        halo[HALO:, :] = result[:HALO, :]
        move.start(halo, refs[0]).wait()
        return
    for step in steps:
        leave(step, middle_grad, 0).wait()
        leave(step, result, 1).wait()


def kernel_add(mine_in, other_in, out, mine, other, sems):
    chunks = sems.shape[0]
    size = mine.shape[0] // chunks

    def copies(chunk):
        spot = pl.ds(chunk * size, size)
        return [
            pltpu.make_async_copy(mine_in.at[spot], mine.at[spot], sems.at[chunk, 0]),
            pltpu.make_async_copy(other_in.at[spot], other.at[spot], sems.at[chunk, 1]),
            pltpu.make_async_copy(mine.at[spot], out.at[spot], sems.at[chunk, 2]),
        ]

    for chunk in range(chunks):
        for copy in copies(chunk)[:2]:
            copy.start()
    for chunk in range(chunks):
        spot = pl.ds(chunk * size, size)
        arriving = copies(chunk)
        for copy in arriving[:2]:
            copy.wait()
        mine[spot, :] = (mine[spot, :].astype(F32) + other[spot, :].astype(F32)).astype(BF16)
        arriving[2].start()
    for chunk in range(chunks):
        copies(chunk)[2].wait()


def kernel_sum(extra, *refs):
    parts_in, out, parts, piece, sems = refs[extra:]
    count = parts.shape[0]
    quarter = max(count // 4, 1)
    copies = []
    for index, begin in enumerate(range(0, count, quarter)):
        spot = pl.ds(begin, quarter)
        copies.append(pltpu.make_async_copy(parts_in.at[spot], parts.at[spot], sems.at[index]))
        copies[-1].start()
    total = jnp.zeros(piece.shape, F32)
    for index, copy in enumerate(copies):
        copy.wait()
        for part in range(index * quarter, (index + 1) * quarter):
            total = total + parts[part].astype(F32)
    piece[...] = total.astype(BF16)
    for part in range(count):
        pltpu.make_async_copy(piece, out.at[part], sems.at[4]).start()
    pltpu.make_async_copy(parts, out, sems.at[4]).wait()


def kernel_unpack_half(half, packed_in, d_ex, d_out, d_in, d_sh, packed, ex, out, inward, sh, sems):
    arrays = ((ex, d_ex), (sh, d_sh), (out, d_out), (inward, d_in))
    sizes = [value.shape[0] * value.shape[1] // LANES for value, _target in arrays]
    begins = [sum(sizes[:index]) for index in range(4)]
    arriving = []
    for index in range(4):
        spot = pl.ds(begins[index], sizes[index])
        arriving.append(pltpu.make_async_copy(packed_in.at[spot], packed.at[spot], sems.at[index]))
        arriving[-1].start()
    leaving = []
    for index, (value, target) in enumerate(arrays):
        arriving[index].wait()
        at = begins[index]
        if index != 1:
            count = value.shape[0]
            for begin in range(0, value.shape[1], LANES):
                value[:, begin : begin + LANES] = packed[pl.ds(at, count), :].astype(F32)
                at += count
        else:
            count = value.shape[1]
            for begin in range(0, value.shape[0], LANES):
                value[begin : begin + LANES, :] = packed[pl.ds(at, count), :].astype(F32).T
                at += count
        rows = pl.ds(pl.multiple_of(half * value.shape[0], value.shape[0]), value.shape[0])
        leaving.append(pltpu.make_async_copy(value, target.at[rows], sems.at[4 + index]))
        leaving[-1].start()
    return leaving


def own_core():
    return lax.rem(lax.axis_index("dp"), 2)


def kernel_first_half(packed_in, *refs):
    for copy in kernel_unpack_half(own_core(), packed_in, *refs):
        copy.wait()


def kernel_second_half(
    packed_in, first_in, kept_ex, kept_out, kept_in, kept_sh,
    d_ex, d_out, d_in, d_sh, b_in, b_sh, gain2, shift2, b_out, b_ex, gain1, shift1,
    packed, ex, out, inward, sh, sems, mine, other, small_sems,
):
    del kept_ex, kept_out, kept_in, kept_sh
    rows = pl.ds(first_in.shape[0] - mine.shape[0], mine.shape[0])
    copies = [
        pltpu.make_async_copy(first_in.at[rows], mine, small_sems.at[0]),
        pltpu.make_async_copy(packed_in.at[rows], other, small_sems.at[1]),
    ]
    for copy in copies:
        copy.start()
    core = own_core()
    leaving = kernel_unpack_half(
        1 - core, packed_in, d_ex, d_out, d_in, d_sh, packed, ex, out, inward, sh, sems
    )
    for copy in copies:
        copy.wait()
    width, columns = b_sh.shape[0], b_ex.shape[0]
    swap = core == 1
    blocks = []
    for index in range(columns // LANES):
        spot = pl.ds(index // 2 * 16, 16)
        pair = mine[spot, :].astype(F32), other[spot, :].astype(F32)
        blocks.append(jnp.where(swap, pair[1 - index % 2], pair[index % 2]))
    small = jnp.concatenate(blocks, axis=1)
    for row, ref in ((0, b_sh), (1, gain2), (2, shift2), (3, b_out), (6, gain1), (7, shift1)):
        ref[...] = small[row, :width]
    b_ex[...] = small[4]
    b_in[0:1, :] = small[5:6, :width]
    b_in[1:2, :] = small[5:6, 2 * width : 3 * width]
    for copy in leaving:
        copy.wait()


def kernel_touch(*refs):
    del refs


VMEM = pl.BlockSpec(memory_space=pltpu.VMEM)
SMEM = pl.BlockSpec(memory_space=pltpu.SMEM)
ANY = pl.BlockSpec(memory_space=pl.ANY)


def params(mib):
    return pltpu.CompilerParams(vmem_limit_bytes=mib * 1024 * 1024)


def cost(flops, moved):
    return pl.CostEstimate(flops=int(flops), bytes_accessed=int(moved), transcendentals=0)


def shape(dims, dtype):
    return jax.ShapeDtypeStruct(dims, dtype)


def packed_rows(columns, small, pieces):
    half = columns // LANES * 192 + (small // LANES + 1) // 2 * 16
    return pieces * (-(-half // (8 * pieces)) * 8)


def attention_scratch(pairs):
    return [
        [pltpu.VMEM((pairs, WIN, 2 * WIN), F32)] * 2,
        [pltpu.VMEM((8, 2 * WIN), F32)] * 2,
        [pltpu.VMEM((pairs, 2 * WIN, WIN), BF16)] * 2,
        [pltpu.VMEM((8, 2 * WIN), F32)] * 2,
    ]


def own_part(segments, gain1, shift1, b_in, x, w_in):
    rows, width = x.shape
    total = rows + TILE
    pairs = width // (2 * HD)
    vmem = pltpu.VMEM
    return pl.pallas_call(
        kernel_own,
        out_shape=(
            shape((rows, 3 * width), BF16),
            shape((total, width), BF16),
            shape((rows, width), BF16),
            shape((GROUPS, pairs, 2 * WIN, WIN), BF16),
            shape((GROUPS, 8, WIN), F32),
            shape((GROUPS + 1, 8), jnp.int32),
        ),
        in_specs=[ANY] * 6,
        out_specs=(ANY, ANY, ANY, ANY, VMEM, SMEM),
        scratch_shapes=[
            vmem(segments.shape, jnp.int32),
            vmem(gain1.shape, F32),
            vmem(shift1.shape, F32),
            vmem(b_in.shape, F32),
            vmem((rows, width), BF16),
            vmem(w_in.shape, BF16),
            vmem((total, 3 * width), BF16),
            vmem((total, width), BF16),
            vmem((8, LANES), jnp.int32),
            pltpu.SMEM((8, LANES), jnp.int32),
            *attention_scratch(pairs),
            vmem((GROUPS, pairs, 2 * WIN, WIN), BF16),
            pltpu.SemaphoreType.DMA((16,)),
            pltpu.SemaphoreType.DMA((rows // OWN + 1,)),
        ],
        compiler_params=params(63),
        cost_estimate=cost(2 * 6 * rows * width * 3 * width, 1e7),
        name="own_part",
    )(segments, gain1, shift1, b_in, x, w_in)


def rest_part(table, vectors, x, cot, halo, triple, attended, scaled, raised, stats, w_in, w_out, w_ex, w_sh, pieces):
    rows, width = x.shape
    total = rows + TILE
    hidden = w_ex.shape[1]
    packed = packed_rows(2 * hidden + 4 * width, hidden, pieces)
    vmem = pltpu.VMEM
    pairs = width // (2 * HD)
    square, row = vmem((pairs, WIN, 2 * WIN), F32), vmem((8, 2 * WIN), F32)
    low = vmem((pairs, WIN, 2 * WIN), BF16)
    return pl.pallas_call(
        kernel_rest,
        out_shape=(
            shape((total, width), F32),
            shape((total, width), F32),
            shape((total, hidden), BF16),
            shape((total, 3 * width), BF16),
            shape((TILE, width), BF16),
            shape((packed, LANES), BF16),
            shape((packed, LANES), BF16),
        ),
        in_specs=[SMEM] + [ANY] * 19,
        out_specs=tuple([ANY] * 7),
        scratch_shapes=[
            vmem((total, width), BF16),
            vmem((total, width), BF16),
            vmem(w_in.shape, BF16),
            vmem(w_out.shape, BF16),
            vmem(w_ex.shape, BF16),
            vmem(w_sh.shape, BF16),
            vmem((total, 3 * width), BF16),
            vmem((total, width), BF16),
            vmem((total, width), F32),
            vmem((total, width), F32),
            vmem((total, width), BF16),
            vmem((total, hidden), BF16),
            vmem((total, 3 * width), BF16),
            vmem((GROUPS, 8, WIN), F32),
            vmem((width, hidden), F32),
            vmem((width, hidden), F32),
            vmem((width, width), F32),
            vmem((width, 3 * width), F32),
            vmem((16, 3 * width), F32),
            vmem((16, hidden), F32),
            [square],
            [row],
            [vmem((pairs, 2 * WIN, WIN), BF16)],
            [row],
            [vmem((pairs, 2 * HD, WIN), BF16)] * 2,
            [low] * 2,
            vmem((SLOTS, pairs, 2 * WIN, WIN), BF16),
            vmem((TILE, width), BF16),
            vmem((packed, LANES), BF16),
            vmem((packed, LANES), BF16),
            pltpu.SemaphoreType.DMA((40,)),
            pltpu.SemaphoreType.DMA((2,)),
            pltpu.SemaphoreType.DMA((SLOTS,)),
            *[vmem(v.shape, F32) for v in vectors],
        ],
        compiler_params=params(62),
        cost_estimate=cost(2 * 9 * rows * width * (3 * width + 8 * width), 3e7),
        name="rest_part",
    )(table, *vectors, x, cot, halo, triple, attended, scaled, raised, stats, w_in, w_out, w_ex, w_sh)


def row_outputs(begin, after, table, gain1, b_sh, x, w_in, triple_grad, middle_grad, middle, hidden, w_sh):
    rows, width = x.shape
    vmem = pltpu.VMEM
    if rows > TILE:
        out_shape = (shape((rows, width), F32), shape((rows, width), BF16))
    else:
        out_shape = (shape((2 * HALO, width), BF16),)
    return pl.pallas_call(
        partial(kernel_rows, begin, begin + rows),
        out_shape=out_shape,
        in_specs=[ANY, SMEM, VMEM, VMEM] + [ANY] * 7,
        out_specs=(ANY,) * len(out_shape),
        scratch_shapes=[
            vmem((rows, width), BF16),
            vmem(w_in.shape, BF16),
            vmem((rows, 3 * width), BF16),
            vmem((rows, width), F32),
            vmem((rows, width), F32),
            vmem((rows, hidden.shape[1]), BF16),
            vmem(w_sh.shape, BF16),
            vmem((rows, width), BF16),
            vmem((2 * HALO, width), BF16),
            pltpu.SemaphoreType.DMA((8,)),
            pltpu.SemaphoreType.DMA((max(rows // BLOCK, 1), 6)),
        ],
        compiler_params=params(63),
        cost_estimate=cost(2 * rows * width * 16 * width, rows * 13e3),
        name="row_outputs",
    )(after, table, gain1, b_sh, x, w_in, triple_grad, middle_grad, middle, hidden, w_sh)


def add_halves(mine, other):
    return pl.pallas_call(
        kernel_add,
        out_shape=shape(mine.shape, BF16),
        in_specs=[ANY, ANY],
        out_specs=ANY,
        scratch_shapes=[
            pltpu.VMEM(mine.shape, BF16), pltpu.VMEM(mine.shape, BF16), pltpu.SemaphoreType.DMA((4, 3)),
        ],
        compiler_params=params(63),
        cost_estimate=cost(mine.size, mine.size * 6),
        name="add_halves",
    )(mine, other)


def sum_parts(after, parts):
    return pl.pallas_call(
        partial(kernel_sum, len(after)),
        out_shape=shape(parts.shape, BF16),
        in_specs=[ANY] * (len(after) + 1),
        out_specs=ANY,
        scratch_shapes=[
            pltpu.VMEM(parts.shape, BF16),
            pltpu.VMEM(parts.shape[1:], BF16),
            pltpu.SemaphoreType.DMA((5,)),
        ],
        compiler_params=params(63),
        cost_estimate=cost(parts.size, parts.size * 4),
        name="sum_parts",
    )(*after, parts)


def half_shapes(width, hidden):
    dims = ((width, hidden), (width, width), (width, 3 * width), (hidden, width))
    scratch = [pltpu.VMEM((rows // 2, columns), F32) for rows, columns in dims]
    return tuple(shape(dim, F32) for dim in dims), [*scratch, pltpu.SemaphoreType.DMA((8,))]


def unpack_first(packed, width, hidden):
    shapes, scratch = half_shapes(width, hidden)
    return pl.pallas_call(
        kernel_first_half,
        out_shape=shapes,
        in_specs=[ANY],
        out_specs=(ANY,) * 4,
        scratch_shapes=[pltpu.VMEM(packed.shape, BF16), *scratch],
        compiler_params=params(63),
        cost_estimate=cost(packed.size, packed.size * 6),
        name="unpack_first",
    )(packed)


def unpack_second(packed, first, kept, used, width, hidden):
    shapes, scratch = half_shapes(width, hidden)
    rows = first.shape[0] - used
    small = tuple(shape(dims, F32) for dims in ((2, width),) + ((width,),) * 4 + ((hidden,), (width,), (width,)))
    return pl.pallas_call(
        kernel_second_half,
        out_shape=shapes + small,
        in_specs=[ANY] * 6,
        out_specs=(ANY,) * 4 + (VMEM,) * 8,
        scratch_shapes=[
            pltpu.VMEM(packed.shape, BF16), *scratch, pltpu.VMEM((rows, LANES), BF16), pltpu.VMEM((rows, LANES), BF16),
            pltpu.SemaphoreType.DMA((2,)),
        ],
        input_output_aliases={2: 0, 3: 1, 4: 2, 5: 3},
        compiler_params=params(63),
        cost_estimate=cost(packed.size, packed.size * 6),
        name="unpack_second",
    )(packed, first, *kept)


def touch(value, *after):
    return pl.pallas_call(
        kernel_touch,
        out_shape=shape(value.shape, value.dtype),
        in_specs=[ANY] * (1 + len(after)),
        out_specs=ANY,
        input_output_aliases={0: 0},
        name="touch",
    )(value, *after)


def same_core_groups():
    packs, parts = lax.axis_size("dp"), lax.axis_size("mp")
    return [[d * parts + m for d in range(c, packs, 2) for m in range(parts)] for c in range(2)]


def swap_cores(block):
    packs = lax.axis_size("dp")
    return lax.ppermute(block, "dp", [(i, i ^ 1) for i in range(packs)])


def exchange(parts):
    return lax.all_to_all(parts, ("dp", "mp"), 0, 0, axis_index_groups=same_core_groups())


def passed(block, distance):
    count = lax.axis_size("mp")
    route = [(i, i + distance) for i in range(count) if 0 <= i + distance < count]
    return lax.ppermute(block, "mp", route)


def kernel_take_over(table, halo_in, input_in, result_in, input_out, result_out, halo, input_own, result_own, sems):
    rows = pl.ds(0, HALO)
    copies = [
        pltpu.make_async_copy(halo_in, halo, sems.at[0]),
        pltpu.make_async_copy(input_in.at[rows], input_own, sems.at[1]),
        pltpu.make_async_copy(result_in.at[rows], result_own, sems.at[2]),
    ]
    for copy in copies:
        copy.start()
    for copy in copies:
        copy.wait()
    other = lax.broadcasted_iota(jnp.int32, (HALO, 1), 0) < table[GROUPS, 1]
    input_own[...] = jnp.where(other, halo[:HALO, :].astype(F32), input_own[...])
    result_own[...] = jnp.where(other, halo[HALO:, :].astype(F32), result_own[...].astype(F32)).astype(BF16)
    copies = [
        pltpu.make_async_copy(input_own, input_out.at[rows], sems.at[3]),
        pltpu.make_async_copy(result_own, result_out.at[rows], sems.at[4]),
    ]
    for copy in copies:
        copy.start()
    for copy in copies:
        copy.wait()


def take_over(table, halo, input_grad, result):
    width = input_grad.shape[1]
    return pl.pallas_call(
        kernel_take_over,
        out_shape=(shape(input_grad.shape, F32), shape(result.shape, BF16)),
        in_specs=[SMEM, ANY, ANY, ANY],
        out_specs=(ANY, ANY),
        scratch_shapes=[
            pltpu.VMEM(halo.shape, BF16), pltpu.VMEM((HALO, width), F32), pltpu.VMEM((HALO, width), BF16),
            pltpu.SemaphoreType.DMA((5,)),
        ],
        input_output_aliases={2: 0, 3: 1},
        compiler_params=params(63),
        name="take_over",
    )(table, halo, input_grad, result)


def body(
    layer_input, segments, cotangent, first_gain, first_shift, inward_weight, inward_bias, outward_weight,
    outward_bias, second_gain, second_shift, expand_weight, expand_bias, shrink_weight, shrink_bias,
):
    rows, width = layer_input.shape
    hidden_width = expand_weight.shape[1]
    pieces = lax.axis_size("dp") * lax.axis_size("mp") // 2
    gain1, shift1, b_out, gain2, shift2, b_ex, b_sh = (
        first_gain, first_shift, outward_bias, second_gain, second_shift, expand_bias, shrink_bias
    )
    halo = passed(jnp.concatenate([layer_input[:HALO], cotangent[:HALO]], axis=0), -1)
    triple, attended, scaled, raised, stats, table = own_part(
        segments, gain1, shift1, inward_bias, layer_input, inward_weight
    )
    middle, middle_grad, hidden, triple_grad, edge, mine, other = rest_part(
        table, (gain1, shift1, inward_bias, b_out, gain2, shift2, b_ex), layer_input, cotangent, halo, triple,
        attended, scaled, raised, stats, inward_weight, outward_weight, expand_weight, shrink_weight, pieces,
    )
    both = add_halves(mine, swap_cores(other))
    parts = exchange(both.reshape(pieces, -1, LANES))
    kept = (inward_weight, triple_grad, middle_grad, middle, hidden, shrink_weight)
    (halo,) = row_outputs(rows, both, table, gain1, b_sh, edge, *kept)
    other_halo = passed(halo, 1)
    input_grad, result = row_outputs(0, halo, table, gain1, b_sh, layer_input, *kept)
    summed = sum_parts((other_halo, result), parts)
    mine = exchange(summed).reshape(-1, LANES)
    input_grad, result = take_over(table, touch(other_halo, summed), input_grad, result)
    mine = touch(mine, input_grad, result)
    other = swap_cores(mine)
    used = 192 * (2 * hidden_width + 4 * width) // LANES
    half = unpack_first(mine, width, hidden_width)
    d_ex, d_out, d_in, d_sh, d_b_in, d_b_sh, d_gain2, d_shift2, d_b_out, d_b_ex, d_gain1, d_shift1 = unpack_second(
        other, mine, half, used, width, hidden_width
    )
    return (
        result, input_grad, d_gain1, d_shift1, d_in, d_b_in, d_out, d_b_out, d_gain2, d_shift2, d_ex, d_b_ex, d_sh,
        d_b_sh,
    )


def solution(mesh):
    rows = P(("dp", "mp"), None)
    in_specs = (rows, P("dp", None), rows) + (P(),) * 12
    out_specs = (rows, rows) + (P(),) * 12
    return jax.shard_map(body, mesh=mesh, in_specs=in_specs, out_specs=out_specs, check_vma=False)
```
